32 devices in a mesh: fsdp: 32 (over z, y, x, core).
Axes of the slice: x: 2, y: 2, z: 4, core: 2. Of those that a mesh axis runs over, the one named last changes fastest.
Arguments:
- images: bfloat16 [256, 196, 768], P('fsdp'), may hold values from -6 to 6
- cotangent: bfloat16 [256, 196, 768], P('fsdp'), may hold values from -6 to 6
- counts: int32 [32], P('fsdp'), may hold values from 1 to 8, as said below
- w_token_in: float32 [75264], P('fsdp'), may hold values from -0.4375 to 0.4375
- w_token_out: float32 [75264], P('fsdp'), may hold values from -0.3125 to 0.3125
- w_chan_in: float32 [2359296], P('fsdp'), may hold values from -0.21875 to 0.21875
- w_chan_out: float32 [2359296], P('fsdp'), may hold values from -0.109375 to 0.109375
- gains: float32 [2, 768], replicated, may hold values from 0.4 to 1.8
- row_states: float32 [4420], replicated
- col_states: float32 [4420], replicated
- gain_states: float32 [2, 768], replicated, may hold values from 7056 to 28224
Outputs:
- block_out: float32 [256, 196, 768], P('fsdp')
- grad_input: float32 [256, 196, 768], P('fsdp')
- grad_token_in: float32 [75264], P('fsdp')
- grad_token_out: float32 [75264], P('fsdp')
- grad_chan_in: float32 [2359296], P('fsdp')
- grad_chan_out: float32 [2359296], P('fsdp')
- new_token_in: float32 [75264], P('fsdp')
- new_token_out: float32 [75264], P('fsdp')
- new_chan_in: float32 [2359296], P('fsdp')
- new_chan_out: float32 [2359296], P('fsdp')
- gain_grads: float32 [2, 768], replicated
- gain_stats: float32 [2, 768], replicated
- new_gains: float32 [2, 768], replicated
- row_stats: float32 [4420], replicated
- col_stats: float32 [4420], replicated
- update_rms: float32 [6], replicated
The draws below stay inside these ranges and needn't reach their ends.
Inputs may be any that keep to these rules, and one draw needn't show every extreme that they name: `counts`: slots of a device at or past its count are padding; the first device holds one image and the last is full.
All inputs are finite; a program needn't handle non-finite values.
Results may differ from the reference program's by a relative error of at most 0.0081.
Values may be sent and summed in bfloat16 or wider, within the bound.
No kernel may reach another device: no remote copies, remote signals or barrier semaphores. Data moves between devices by JAX's collectives and lax.ppermute only.
A program may use at most 256 MiB of HBM per device.

```python
import math
import jax
import jax.numpy as jnp
from jax import lax

D = 768
PATCH_COUNT = 196
TOKEN_HIDDEN = 384
DC = 3072
IMG_DEV = 8
IMAGES = 256
N_FSDP = 32


def draw_counts(key, part):
    key = jax.random.fold_in(key, 3)
    jitter = jax.random.randint(key, (N_FSDP,), -1, 2)
    position = jnp.arange(N_FSDP, dtype=jnp.int32)
    rising = 1 + (IMG_DEV - 1) * position // (N_FSDP - 1)
    varied = jnp.clip(rising + jitter, 1, IMG_DEV)
    varied = jnp.where(position == 0, 1, varied)
    return jnp.where(position == N_FSDP - 1, IMG_DEV, varied).astype(jnp.int32)


def draw_gains(key, part):
    key = jax.random.fold_in(key, 5)
    ramp = 0.5 + jnp.arange(D, dtype=jnp.float32) / D
    factor = jax.random.uniform(key, (2, D), jnp.float32, 0.8, 1.2)
    return ramp[None, :] * factor


def segment_scales(lengths, factors):
    valid = (IMG_DEV + 1) * N_FSDP * 0.5
    pieces = [jnp.full((length,), factor * valid, jnp.float32) for length, factor in zip(lengths, factors)]
    return jnp.concatenate(pieces)


def draw_row_states(key, part):
    key = jax.random.fold_in(key, 7)
    scales = segment_scales((PATCH_COUNT, TOKEN_HIDDEN, D, DC), (0.13 * D, 0.36 * D, 0.06 * PATCH_COUNT, 0.36 * PATCH_COUNT))
    spread = jax.random.uniform(key, scales.shape, jnp.float32, 0.0, math.log(4.0))
    return scales * jnp.exp(spread)


def draw_col_states(key, part):
    key = jax.random.fold_in(key, 9)
    scales = segment_scales((TOKEN_HIDDEN, PATCH_COUNT, DC, D), (0.13 * D, 0.36 * D, 0.06 * PATCH_COUNT, 0.36 * PATCH_COUNT))
    spread = jax.random.uniform(key, scales.shape, jnp.float32, 0.0, math.log(4.0))
    return scales * jnp.exp(spread)


def level_of(stream_key, extent, shards, low, top_value):
    def one(axis_at, blocks):
        steps = jax.random.uniform(jax.random.fold_in(jax.random.fold_in(stream_key, 6), axis_at), (blocks,), jnp.float32, low / len(shards), top_value / len(shards))
        return jnp.repeat(jnp.exp(steps), extent[axis_at] // blocks).reshape((-1,) + (1,) * (len(extent) - axis_at - 1))

    factor_of = one(*shards[0])
    for cut in shards[1:]:
        factor_of = factor_of * one(*cut)
    return factor_of


def bell_draw(rng, shape, scale, bound, shards=(), kind=jnp.bfloat16):
    level = level_of(rng, shape, shards, -0.22, 0.18) if shards else 1.0
    drawn = jax.random.normal(rng, shape, jnp.float32) * scale * level
    return jnp.minimum(jnp.maximum(drawn, -bound), bound).astype(kind)


def setup_inputs(seed: int = 0) -> dict:
    splits = jax.random.split(jax.random.key(seed), 12)
    return {
        "images": bell_draw(splits[0], (IMAGES, PATCH_COUNT, D), 1.0, 6.0, ((0, 32),)),
        "cotangent": bell_draw(splits[1], (IMAGES, PATCH_COUNT, D), 1.0, 6.0, ((0, 32),)),
        "counts": draw_counts(jax.random.fold_in(splits[11], 71), 0),
        "w_token_in": bell_draw(splits[3], (PATCH_COUNT * TOKEN_HIDDEN,), PATCH_COUNT ** -0.5, 0.4375, ((0, 32),), jnp.float32),
        "w_token_out": bell_draw(splits[4], (TOKEN_HIDDEN * PATCH_COUNT,), TOKEN_HIDDEN ** -0.5, 0.3125, ((0, 32),), jnp.float32),
        "w_chan_in": bell_draw(splits[5], (D * DC,), D ** -0.5, 0.21875, ((0, 32),), jnp.float32),
        "w_chan_out": bell_draw(splits[6], (DC * D,), DC ** -0.5, 0.109375, ((0, 32),), jnp.float32),
        "gains": draw_gains(jax.random.fold_in(splits[11], 71), 0),
        "row_states": draw_row_states(jax.random.fold_in(splits[11], 71), 0),
        "col_states": draw_col_states(jax.random.fold_in(splits[11], 71), 0),
        "gain_states": jnp.clip(jnp.exp(jax.random.uniform(splits[10], (2, D), jnp.float32, math.log(7056.0), math.log(28224.0))), 7056.0, 28224.0),
    }


decay_rate = 0.5
clip_level = 0.5
step_rate = 1.0
highest_precision = lax.Precision.HIGHEST

@jax.custom_vjp
def reduced_precision(v):
    return lax.optimization_barrier(v.astype(jnp.bfloat16)).astype(jnp.float32)

@jax.custom_vjp
def reduced_backward(v):
    return v

def low_keep(v):
    return (reduced_precision(v), None)

def low_pass(kept, grad):
    return (grad,)

def back_keep(v):
    return (v, None)

def back_low(kept, grad):
    return (reduced_precision(grad),)
reduced_precision.defvjp(low_keep, low_pass)
reduced_backward.defvjp(back_keep, back_low)

def layer_norm(values, gain):
    centred = values - lax.optimization_barrier(jnp.mean(values, axis=-1, keepdims=True))
    spread = lax.optimization_barrier(jnp.mean(centred * centred, axis=-1, keepdims=True))
    return centred * lax.rsqrt(spread + 1e-06) * gain

def mixer_block(values, first_weight, second_weight, w_three, w_four, gain_pair):
    token_input = reduced_precision(layer_norm(values, gain_pair[0]))
    token_preactivation = reduced_backward(jnp.einsum('mpw,px->mxw', token_input, reduced_precision(first_weight.reshape(PATCH_COUNT, TOKEN_HIDDEN)), precision=highest_precision))
    token_activation = reduced_precision(jax.nn.gelu(token_preactivation))
    token_branch = reduced_backward(jnp.einsum('gjo,jp->gpo', token_activation, reduced_precision(second_weight.reshape(TOKEN_HIDDEN, PATCH_COUNT)), precision=highest_precision))
    mixed = values + token_branch
    in_chan = reduced_precision(layer_norm(mixed, gain_pair[1]))
    pre_chan = reduced_backward(jnp.einsum('bsd,df->bsf', in_chan, reduced_precision(w_three.reshape(D, DC)), precision=highest_precision))
    act_chan = reduced_precision(jax.nn.gelu(pre_chan))
    branch_chan = reduced_backward(jnp.einsum('bsf,fd->bsd', act_chan, reduced_precision(w_four.reshape(DC, D)), precision=highest_precision))
    return mixed + branch_chan

def factored(grad, weight, row_old, col_old):
    squares = grad * grad + 1e-30
    row_new = decay_rate * row_old + (1.0 - decay_rate) * lax.optimization_barrier(jnp.mean(squares, axis=1))
    col_new = decay_rate * col_old + (1.0 - decay_rate) * lax.optimization_barrier(jnp.mean(squares, axis=0))
    second = row_new[:, None] * col_new[None, :] / jnp.mean(row_new)
    update = grad * lax.rsqrt(second)
    update_size = jnp.sqrt(jnp.mean(update * update))
    update = update / jnp.maximum(1.0, update_size / clip_level)
    weight_scale = jnp.sqrt(jnp.mean(weight * weight) + 1e-06)
    return (row_new, col_new, update_size, weight - step_rate * weight_scale * update)

def reference(images, cotangent, counts, w_token_in, w_token_out, w_chan_in, w_chan_out, gains, row_states, col_states, gain_states):
    weights = (w_token_in, w_token_out, w_chan_in, w_chan_out, gains)
    slot_ids = jnp.arange(IMG_DEV, dtype=jnp.int32)
    mask = (slot_ids[None, :] < counts[:, None]).astype(jnp.float32)
    blocks = (images.reshape(N_FSDP, IMG_DEV, PATCH_COUNT, D), cotangent.reshape(N_FSDP, IMG_DEV, PATCH_COUNT, D), mask)

    def one_block(totals, item):
        block_in, block_cot, block_mask = item
        block_keep = block_mask[:, None, None]

        def forward(values, first_weight, second_weight, w_three, w_four, gain_pair):
            return mixer_block(values, first_weight, second_weight, w_three, w_four, gain_pair) * block_keep
        result, pull = jax.vjp(forward, block_in.astype(jnp.float32), *weights)
        grads = pull(block_cot.astype(jnp.float32))
        totals = tuple((total_part + grad_part for total_part, grad_part in zip(totals, grads[1:])))
        return (totals, (result, grads[0]))
    initial = tuple((jnp.zeros_like(weight) for weight in weights))
    totals, (results, backs) = lax.scan(one_block, initial, blocks)
    block_out = results.reshape(IMAGES, PATCH_COUNT, D)
    grad_input = backs.reshape(IMAGES, PATCH_COUNT, D)
    shapes = ((PATCH_COUNT, TOKEN_HIDDEN), (TOKEN_HIDDEN, PATCH_COUNT), (D, DC), (DC, D))
    row_edges = (0, PATCH_COUNT, PATCH_COUNT + TOKEN_HIDDEN, PATCH_COUNT + TOKEN_HIDDEN + D, PATCH_COUNT + TOKEN_HIDDEN + D + DC)
    col_edges = (0, TOKEN_HIDDEN, TOKEN_HIDDEN + PATCH_COUNT, TOKEN_HIDDEN + PATCH_COUNT + DC, TOKEN_HIDDEN + PATCH_COUNT + DC + D)
    rows_out, cols_out, sizes, new_weights = ([], [], [], [])
    for which in range(4):
        row_count, col_count = shapes[which]
        row_new, col_new, update_size, new_weight = factored(totals[which].reshape(row_count, col_count), weights[which].reshape(row_count, col_count), row_states[row_edges[which]:row_edges[which + 1]], col_states[col_edges[which]:col_edges[which + 1]])
        rows_out.append(row_new)
        cols_out.append(col_new)
        sizes.append(update_size)
        new_weights.append(new_weight.reshape(-1))
    gain_grads = totals[4]
    gain_stats = decay_rate * gain_states + (1.0 - decay_rate) * (gain_grads * gain_grads + 1e-30)
    gain_update = gain_grads * lax.rsqrt(gain_stats)
    gain_sizes = jnp.sqrt(lax.optimization_barrier(jnp.mean(gain_update * gain_update, axis=1)))
    gain_update = gain_update / jnp.maximum(1.0, gain_sizes / clip_level)[:, None]
    gain_scale = jnp.sqrt(lax.optimization_barrier(jnp.mean(gains * gains, axis=1)) + 1e-06)
    new_gains = gains - step_rate * gain_scale[:, None] * gain_update
    update_rms = jnp.concatenate([jnp.stack(sizes), gain_sizes])
    return (block_out, grad_input, totals[0], totals[1], totals[2], totals[3], new_weights[0], new_weights[1], new_weights[2], new_weights[3], gain_grads, gain_stats, new_gains, jnp.concatenate(rows_out), jnp.concatenate(cols_out), update_rms)
```

```python
import functools

import jax
import jax.numpy as jnp
from jax import lax
from jax.experimental import pallas as pl
from jax.experimental.pallas import tpu as pltpu
from jax.sharding import PartitionSpec as P

D = 768
PATCHES = 196
HIDDEN = 384
DC = 3072
PAD = 208
UNITS = 2
F = DC // (2 * UNITS)
BLOCKS = 16
TILE = D // BLOCKS
GROUP = 2

DECAY = 0.5
CLIP = 0.5
STEP = 1.0

NN = ((1,), (0,))
NT = ((1,), (1,))
TN = ((0,), (0,))

GELU_A = 0.7978845608028654
GELU_B = 0.7978845608028654 * 0.044715

BF = jnp.bfloat16
F32 = jnp.float32


def dot(a, b, dims):
    return lax.dot_general(a, b, (dims, ((), ())), preferred_element_type=F32)


def gelu_pair(v):
    square = v * v
    t = jnp.tanh(v * (GELU_A + GELU_B * square))
    half = 0.5 + 0.5 * t
    slope = half + (0.5 * v) * (1.0 - t * t) * (GELU_A + (3.0 * GELU_B) * square)
    return v * half, slope


def normalize(values):
    centred = values - jnp.mean(values, axis=-1, keepdims=True)
    spread = jnp.mean(centred * centred, axis=-1, keepdims=True)
    inverse = lax.rsqrt(spread + 1e-06)
    return centred * inverse, inverse


def norm_back(grad, normed, inverse):
    first = jnp.mean(grad, axis=-1, keepdims=True)
    second = jnp.mean(grad * normed, axis=-1, keepdims=True)
    return inverse * (grad - first - normed * second)


def params(mib=56):
    return pltpu.CompilerParams(vmem_limit_bytes=mib * 2**20)


ANY = pl.BlockSpec(memory_space=pl.ANY)
SMEM = pl.BlockSpec(memory_space=pltpu.SMEM)


def whole(shape):
    return pl.BlockSpec(shape, lambda *_: (0,) * len(shape))


def image(rows):
    return pl.BlockSpec((1, rows, D), lambda i: (i, 0, 0))


def struct(shape, dtype):
    return jax.ShapeDtypeStruct(shape, dtype)


def first_kernel(counts, x, cot, gains, y1, dout):
    normed, _ = normalize(x[0].astype(F32))
    y1[0] = (normed * gains[0:1, :]).astype(BF)
    keep = (pl.program_id(0) < counts[0]).astype(F32)
    dout[0, :PATCHES, :] = (cot[0].astype(F32) * keep).astype(BF)
    dout[0, PATCHES:, :] = jnp.zeros((PAD - PATCHES, D), BF)


def first_norm(counts, images, cotangent, gains):
    count = images.shape[0]
    return pl.pallas_call(
        first_kernel,
        grid=(count,),
        in_specs=[SMEM, image(PATCHES), image(PATCHES), whole((2, D))],
        out_specs=[image(PATCHES), image(PAD)],
        out_shape=[struct((count, PATCHES, D), BF), struct((count, PAD, D), BF)],
        compiler_params=params(),
        name="first_norm",
    )(counts, images, cotangent, gains)


def token_kernel(x, y1, w1, w2, gains, h, slope, x1, y2):
    act, der = gelu_pair(dot(w1[...], y1[0], TN))
    act = act.astype(BF)
    h[0] = act
    slope[0] = der.astype(BF)
    mixed = x[0].astype(F32) + dot(w2[...], act, TN)
    x1[0] = mixed
    normed, _ = normalize(mixed)
    y2[0, :PATCHES, :] = (normed * gains[1:2, :]).astype(BF)
    y2[0, PATCHES:, :] = jnp.zeros((PAD - PATCHES, D), BF)


def token_forward(images, y1, w1, w2, gains):
    count = images.shape[0]
    return pl.pallas_call(
        token_kernel,
        grid=(count,),
        in_specs=[
            image(PATCHES),
            image(PATCHES),
            whole((PATCHES, HIDDEN)),
            whole((HIDDEN, PATCHES)),
            whole((2, D)),
        ],
        out_specs=[image(HIDDEN), image(HIDDEN), image(PATCHES), image(PAD)],
        out_shape=[
            struct((count, HIDDEN, D), BF),
            struct((count, HIDDEN, D), BF),
            struct((count, PATCHES, D), F32),
            struct((count, PAD, D), BF),
        ],
        compiler_params=params(),
        name="token_forward",
    )(images, y1, w1, w2, gains)


def load_unit(table, pieces, unit, dest, sems):
    copies = []
    for at in range(BLOCKS):
        source = pieces[at * 2 // BLOCKS].at[at % (BLOCKS // 2), unit]
        row = pl.multiple_of(table[at] * TILE, 16)
        copies.append(pltpu.make_async_copy(source, dest.at[pl.ds(row, TILE), :], sems.at[at]))
    return copies


def channel_kernel(unit, forward, table, lo, hi, left, right, *refs):
    if forward:
        out, slope, grad, weight, kept, other, sems, other_sem = refs
    else:
        slope, out, grad, weight, kept, other, sems, other_sem = refs
    step = pl.program_id(0)
    rows = left.shape[0]
    other_copy = pltpu.make_async_copy(right, other, other_sem)

    @pl.when(step == 0)
    def _():
        copies = load_unit(table, (lo, hi), unit, weight, sems)
        for copy in copies:
            copy.start()
        other_copy.start()
        for copy in copies:
            copy.wait()

    here = pl.ds(pl.multiple_of(step * rows, 16), rows)
    if forward:
        act, der = gelu_pair(dot(left[...], weight[...], NN))
        act = act.astype(BF)
        slope[...] = der.astype(BF)
    else:
        act = (slope[...].astype(F32) * dot(left[...], weight[...], NT)).astype(BF)
    out[...] = act
    kept[here, :] = act

    @pl.when(step == pl.num_programs(0) - 1)
    def _():
        other_copy.wait()
        if forward:
            total = dot(kept[...], other[...], TN)
        else:
            total = dot(other[...], kept[...], TN)
        total = total.astype(BF)
        for at in range(BLOCKS):
            grad[table[BLOCKS + at]] = total[at * TILE : (at + 1) * TILE, :]


def channel_unit(forward, unit, table, pieces, left, right, slope=None):
    rows = left.shape[0]
    tile = GROUP * PAD
    tiles = pl.BlockSpec((tile, D), lambda i: (i, 0))
    acts = pl.BlockSpec((tile, F), lambda i: (i, 0))
    grad = whole((BLOCKS, TILE, D))
    operands = [table, pieces[0], pieces[1], left, right]
    in_specs = [SMEM, ANY, ANY, tiles, ANY]
    if forward:
        out_specs = [acts, acts, grad]
        out_shape = [struct((rows, F), BF)] * 2 + [struct((BLOCKS, TILE, D), BF)]
    else:
        operands.append(slope)
        in_specs.append(acts)
        out_specs = [acts, grad]
        out_shape = [struct((rows, F), BF), struct((BLOCKS, TILE, D), BF)]
    return pl.pallas_call(
        functools.partial(channel_kernel, unit, forward),
        grid=(rows // tile,),
        in_specs=in_specs,
        out_specs=out_specs,
        out_shape=out_shape,
        scratch_shapes=[
            pltpu.VMEM((D, F), BF),
            pltpu.VMEM((rows, F), BF),
            pltpu.VMEM((rows, D), BF),
            pltpu.SemaphoreType.DMA((BLOCKS,)),
            pltpu.SemaphoreType.DMA,
        ],
        compiler_params=params(),
        cost_estimate=pl.CostEstimate(
            flops=4 * rows * D * F, bytes_accessed=12 * 2**20, transcendentals=rows * F
        ),
        name="channel_forward" if forward else "channel_backward",
    )(*operands)


def back_kernel(own_table, other_table, *refs):
    pieces = refs[0:4]
    d0, d1, d2, d3, dout, x1, h, slope, y1, w2, gains = refs[4:15]
    dx1, da, g1, g2, dg2, weights, sems = refs[15:]
    step = pl.program_id(0)

    @pl.when(step == 0)
    def _():
        copies = []
        for at in range(2 * UNITS):
            table = own_table if at < UNITS else other_table
            pair = pieces[0:2] if at < UNITS else pieces[2:4]
            copies += load_unit(table, pair, at % UNITS, weights.at[at], sems.at[at])
        for copy in copies:
            copy.start()
        for copy in copies:
            copy.wait()
        g1[...] = jnp.zeros_like(g1)
        g2[...] = jnp.zeros_like(g2)
        dg2[...] = jnp.zeros_like(dg2)

    dy2 = dot(d0[...], weights[0], NT)
    dy2 += dot(d1[...], weights[1], NT)
    dy2 += dot(d2[...], weights[2], NT)
    dy2 += dot(d3[...], weights[3], NT)
    for at in range(GROUP):
        grad = dy2[at * PAD : at * PAD + PATCHES, :]
        normed, inverse = normalize(x1[at])
        dg2[...] += jnp.sum(grad * normed, axis=0, keepdims=True)
        total = dout[at, :PATCHES, :].astype(F32) + norm_back(
            grad * gains[1:2, :], normed, inverse
        )
        dx1[at] = total
        low = total.astype(BF)
        g2[...] += dot(h[at], low, NT)
        back = (slope[at].astype(F32) * dot(w2[...], low, NN)).astype(BF)
        da[at] = back
        g1[...] += dot(y1[at], back, NT)


def backward(tables, pieces, dcs, dout, x1, h, slope, y1, w2, gains):
    count = x1.shape[0]
    tile = GROUP * PAD

    def images(rows):
        return pl.BlockSpec((GROUP, rows, D), lambda i: (i, 0, 0))

    acts = pl.BlockSpec((tile, F), lambda i: (i, 0))
    return pl.pallas_call(
        back_kernel,
        grid=(count // GROUP,),
        in_specs=[SMEM, SMEM]
        + [ANY] * 4
        + [acts] * 4
        + [
            images(PAD),
            images(PATCHES),
            images(HIDDEN),
            images(HIDDEN),
            images(PATCHES),
            whole((HIDDEN, PATCHES)),
            whole((2, D)),
        ],
        out_specs=[
            images(PATCHES),
            images(HIDDEN),
            whole((PATCHES, HIDDEN)),
            whole((HIDDEN, PATCHES)),
            whole((1, D)),
        ],
        out_shape=[
            struct((count, PATCHES, D), F32),
            struct((count, HIDDEN, D), BF),
            struct((PATCHES, HIDDEN), F32),
            struct((HIDDEN, PATCHES), F32),
            struct((1, D), F32),
        ],
        scratch_shapes=[
            pltpu.VMEM((2 * UNITS, D, F), BF),
            pltpu.SemaphoreType.DMA((2 * UNITS, BLOCKS)),
        ],
        compiler_params=params(),
        cost_estimate=pl.CostEstimate(
            flops=2 * count * PAD * D * DC, bytes_accessed=40 * 2**20, transcendentals=0
        ),
        name="backward",
    )(*tables, *pieces, *dcs, dout, x1, h, slope, y1, w2, gains)


def input_kernel(x, da, dx1, w1, gains, out, dg1):
    @pl.when(pl.program_id(0) == 0)
    def _():
        dg1[...] = jnp.zeros_like(dg1)

    grad = dot(w1[...], da[0], NN)
    normed, inverse = normalize(x[0].astype(F32))
    dg1[...] += jnp.sum(grad * normed, axis=0, keepdims=True)
    out[0] = dx1[0] + norm_back(grad * gains[0:1, :], normed, inverse)


def input_gradient(images, da, dx1, w1, gains):
    count = images.shape[0]
    return pl.pallas_call(
        input_kernel,
        grid=(count,),
        in_specs=[
            image(PATCHES),
            image(HIDDEN),
            image(PATCHES),
            whole((PATCHES, HIDDEN)),
            whole((2, D)),
        ],
        out_specs=[image(PATCHES), whole((1, D))],
        out_shape=[struct((count, PATCHES, D), F32), struct((1, D), F32)],
        compiler_params=params(),
        cost_estimate=pl.CostEstimate(
            flops=2 * count * PATCHES * D * HIDDEN, bytes_accessed=16 * 2**20, transcendentals=0
        ),
        name="input_gradient",
    )(images, da, dx1, w1, gains)


def out_kernel(counts, own_table, other_table, *refs):
    pieces = refs[0:4]
    a0, a1, a2, a3, x1 = refs[4:9]
    out, weights, sems = refs[9:]
    step = pl.program_id(0)

    @pl.when(step == 0)
    def _():
        copies = []
        for at in range(2 * UNITS):
            table = own_table if at < UNITS else other_table
            pair = pieces[0:2] if at < UNITS else pieces[2:4]
            copies += load_unit(table, pair, at % UNITS, weights.at[at], sems.at[at])
        for copy in copies:
            copy.start()
        for copy in copies:
            copy.wait()

    total = dot(a0[...], weights[0], NN)
    total += dot(a1[...], weights[1], NN)
    total += dot(a2[...], weights[2], NN)
    total += dot(a3[...], weights[3], NN)
    for at in range(GROUP):
        keep = (step * GROUP + at < counts[0]).astype(F32)
        out[at] = keep * (x1[at] + total[at * PAD : at * PAD + PATCHES, :])


def block_output(counts, tables, pieces, acts, x1):
    count = x1.shape[0]
    tile = GROUP * PAD
    images = pl.BlockSpec((GROUP, PATCHES, D), lambda i: (i, 0, 0))
    return pl.pallas_call(
        out_kernel,
        grid=(count // GROUP,),
        in_specs=[SMEM, SMEM, SMEM]
        + [ANY] * 4
        + [pl.BlockSpec((tile, F), lambda i: (i, 0))] * 4
        + [images],
        out_specs=images,
        out_shape=struct((count, PATCHES, D), F32),
        scratch_shapes=[
            pltpu.VMEM((2 * UNITS, F, D), BF),
            pltpu.SemaphoreType.DMA((2 * UNITS, BLOCKS)),
        ],
        compiler_params=params(),
        cost_estimate=pl.CostEstimate(
            flops=2 * count * PAD * D * DC, bytes_accessed=24 * 2**20, transcendentals=0
        ),
        name="block_output",
    )(counts, *tables, *pieces, *acts, x1)


class Links:
    def __init__(self, size):
        self.size = size
        self.chips = size // 2
        bits = self.chips.bit_length() - 1
        high = [1 << b for b in range(2, bits)]
        self.orders = (high + [1, 2], high + [2, 1])
        self.index = lax.axis_index("fsdp")
        self.core = self.index & 1
        self.chip = self.index >> 1

    def swap(self, x, mask):
        return lax.ppermute(x, "fsdp", [(i, i ^ mask) for i in range(self.size)])

    def stage(self, x, level):
        pairs = [(i, i ^ (self.orders[i & 1][level] << 1)) for i in range(self.size)]
        return lax.ppermute(x, "fsdp", pairs)

    def owners(self, core):
        place = jnp.arange(self.chips, dtype=jnp.int32)
        owner = jnp.full((self.chips,), self.chip, jnp.int32)
        for level in range(len(self.orders[0])):
            bit = (place >> level) & 1
            mask = jnp.where(core == 0, self.orders[0][level], self.orders[1][level])
            owner = owner ^ (bit * mask)
        return owner

    def places(self, core):
        relative = jnp.arange(self.chips, dtype=jnp.int32) ^ self.chip
        place = jnp.zeros_like(relative)
        for level in range(len(self.orders[0])):
            mask = jnp.where(core == 0, self.orders[0][level], self.orders[1][level])
            place = place | (((relative & mask) != 0).astype(jnp.int32) << level)
        return place

    def table(self, core):
        if self.chips == BLOCKS:
            return jnp.concatenate([self.owners(core), self.places(core)])
        order = jnp.arange(BLOCKS, dtype=jnp.int32)
        return jnp.concatenate([order, order])

    def gather(self, x):
        x = x[None]
        for level in range(len(self.orders[0]) - 1):
            x = jnp.concatenate([x, self.stage(x, level)], axis=0)
        return x, self.stage(x, len(self.orders[0]) - 1)

    def as_blocks(self, halves, core):
        if self.chips == BLOCKS:
            return halves
        x = jnp.take(jnp.concatenate(halves, axis=0), self.places(core), axis=0)
        units = x.shape[1]
        x = x.transpose(1, 0, 2, 3).reshape(units, BLOCKS, TILE, D).transpose(1, 0, 2, 3)
        return x[: BLOCKS // 2], x[BLOCKS // 2 :]

    def from_blocks(self, x, core):
        if self.chips == BLOCKS:
            return x
        return jnp.take(x.reshape(self.chips, -1, D), self.owners(core), axis=0)

    def scatter(self, mine, received):
        x = [(a.astype(F32), b.astype(F32)) for a, b in zip(mine, received)]
        x = jnp.stack([a + b for a, b in x], axis=1)
        for level in reversed(range(len(self.orders[0]))):
            half = x.shape[0] // 2
            x = x[:half] + self.stage(x[half:].astype(BF), level).astype(F32)
        return x[0]

    def gather_flat(self, x):
        mask = 1
        while mask < self.size:
            got = self.swap(x, mask)
            upper = (self.index & mask) != 0
            x = jnp.where(
                upper, jnp.concatenate([got, x], axis=1), jnp.concatenate([x, got], axis=1)
            )
            mask *= 2
        return x

    def scatter_flat(self, x):
        mask = self.size // 2
        while mask:
            half = x.shape[1] // 2
            upper = (self.index & mask) != 0
            keep = jnp.where(upper, x[:, half:], x[:, :half])
            send = jnp.where(upper, x[:, :half], x[:, half:])
            x = keep + self.swap(send.astype(BF), mask).astype(F32)
            mask //= 2
        return x

    def total(self, x):
        mask = 1
        while mask < self.size:
            x = x + self.swap(x, mask)
            mask *= 2
        return x


def shards(
    images,
    cotangent,
    counts,
    w_token_in,
    w_token_out,
    w_chan_in,
    w_chan_out,
    gains,
    row_states,
    col_states,
    gain_states,
):
    links = Links(D * DC // w_chan_in.shape[0])
    size, chips, core = links.size, links.chips, links.core
    count = images.shape[0]
    own_table, other_table = links.table(core), links.table(1 - core)
    tables = (own_table, other_table)

    token = links.gather_flat(jnp.stack([w_token_in, w_token_out]).astype(BF))
    w1 = token[0].reshape(PATCHES, HIDDEN)
    w2 = token[1].reshape(HIDDEN, PATCHES)

    rows3 = D // size
    rows4 = DC // size
    sub = rows4 // UNITS
    local3 = w_chan_in.astype(BF).reshape(rows3, chips, 2, UNITS, sub)
    local3 = local3.transpose(2, 3, 0, 1, 4).reshape(2, UNITS, rows3, F)
    mine = lax.dynamic_index_in_dim(local3, core, 0, keepdims=False)
    theirs = lax.dynamic_index_in_dim(local3, 1 - core, 0, keepdims=False)
    got = links.swap(theirs, 1)
    local3 = jnp.where(
        core == 0, jnp.concatenate([mine, got], axis=1), jnp.concatenate([got, mine], axis=1)
    )
    local4 = w_chan_out.astype(BF).reshape(UNITS, sub, D)
    gathered3 = links.gather(local3)
    gathered4 = links.gather(local4)
    other3 = tuple(links.swap(x, 1) for x in gathered3)
    other4 = tuple(links.swap(x, 1) for x in gathered4)
    own3 = links.as_blocks(gathered3, core)
    own4 = links.as_blocks(gathered4, core)
    other3 = links.as_blocks(other3, 1 - core)
    other4 = links.as_blocks(other4, 1 - core)

    y1, dout = first_norm(counts, images, cotangent, gains)
    h, slope1, x1, y2 = token_forward(images, y1, w1, w2, gains)
    y2_rows = y2.reshape(count * PAD, D)
    dout_rows = dout.reshape(count * PAD, D)
    order = [(own_table, own3, own4, u) for u in range(UNITS)]
    order += [(other_table, other3, other4, u) for u in range(UNITS)]
    acts, slopes, grads4 = [], [], []
    for table, pieces, _, unit in order:
        act, slope, grad = channel_unit(True, unit, table, pieces, y2_rows, dout_rows)
        acts.append(act)
        slopes.append(slope)
        grads4.append(grad)

    def finish(grads):
        grads = [links.from_blocks(g, core if k < UNITS else 1 - core) for k, g in enumerate(grads)]
        received = [links.swap(g, 1) for g in grads[UNITS:]]
        return links.scatter(grads[:UNITS], received)

    dcs, grads3 = [], []
    for (table, _, pieces, unit), slope in zip(order, slopes):
        dc, grad = channel_unit(False, unit, table, pieces, dout_rows, y2_rows, slope)
        dcs.append(dc)
        grads3.append(grad)
    grad4 = finish(grads4).reshape(rows4, D)
    grad3 = finish(grads3)
    mine = lax.dynamic_slice_in_dim(grad3, core * rows3, rows3, 1)
    theirs = lax.dynamic_slice_in_dim(grad3, (1 - core) * rows3, rows3, 1)
    got = links.swap(theirs, 1)
    grad3 = jnp.where(core == 0, jnp.stack([mine, got]), jnp.stack([got, mine]))
    grad3 = grad3.reshape(2, UNITS, rows3, chips, sub).transpose(2, 3, 0, 1, 4).reshape(rows3, DC)

    dx1, da, g1, g2, dg2 = backward(
        tables, own3 + other3, dcs, dout, x1, h, slope1, y1, w2, gains
    )
    token_grads = links.scatter_flat(jnp.stack([g1.reshape(-1), g2.reshape(-1)]))
    token_all = links.gather_flat(token_grads.astype(BF)).astype(F32)
    full = (token_all[0].reshape(PATCHES, HIDDEN), token_all[1].reshape(HIDDEN, PATCHES))
    grad_input, dg1 = input_gradient(images, da, dx1, w1, gains)
    block_out = block_output(counts, tables, own4 + other4, acts, x1)

    edges_r = (0, PATCHES, PATCHES + HIDDEN, PATCHES + HIDDEN + D, PATCHES + HIDDEN + D + DC)
    edges_c = (0, HIDDEN, HIDDEN + PATCHES, HIDDEN + PATCHES + DC, HIDDEN + PATCHES + DC + D)
    old_rows = [row_states[edges_r[k] : edges_r[k + 1]] for k in range(4)]
    old_cols = [col_states[edges_c[k] : edges_c[k + 1]] for k in range(4)]
    masters = (w_token_in, w_token_out, w_chan_in, w_chan_out)
    shapes = ((PATCHES, HIDDEN), (HIDDEN, PATCHES), (D, DC), (DC, D))
    own_rows, parts = [], []
    for which, grad, rows in ((2, grad3, rows3), (3, grad4, rows4)):
        squares = grad * grad + 1e-30
        old = lax.dynamic_slice_in_dim(old_rows[which], links.index * rows, rows)
        row = DECAY * old + (1.0 - DECAY) * jnp.mean(squares, axis=1)
        own_rows.append(row)
        parts.append(
            lax.dynamic_update_slice_in_dim(
                jnp.zeros((shapes[which][0],), F32), row, links.index * rows, 0
            )
        )
        parts.append(jnp.sum(squares, axis=0))
        parts.append(jnp.sum(grad * grad / row[:, None], axis=0))
    parts.append(jnp.stack([jnp.sum(m * m) for m in masters]))
    parts.append(dg1[0])
    parts.append(dg2[0])
    sizes_of = [p.shape[0] for p in parts]
    summed = links.total(jnp.concatenate(parts))
    pieces, at = [], 0
    for length in sizes_of:
        pieces.append(summed[at : at + length])
        at += length
    row3, col3, weighted3, row4, col4, weighted4, weight_squares, dg1, dg2 = pieces

    rows_out, cols_out, update_sizes, new_weights = [None] * 4, [None] * 4, [None] * 4, [None] * 4
    factors = [None] * 4
    for which in range(2):
        row_count, col_count = shapes[which]
        squares = full[which] * full[which]
        row = DECAY * old_rows[which] + (1.0 - DECAY) * jnp.mean(squares + 1e-30, axis=1)
        col = DECAY * old_cols[which] + (1.0 - DECAY) * jnp.mean(squares + 1e-30, axis=0)
        mean_row = jnp.mean(row)
        scaled = squares / (row[:, None] * col[None, :])
        update_sizes[which] = jnp.sqrt(jnp.mean(scaled) * mean_row)
        rows_out[which], cols_out[which] = row, col
        flat = lax.rsqrt(row[:, None] * col[None, :] / mean_row).reshape(-1)
        length = masters[which].shape[0]
        factors[which] = lax.dynamic_slice_in_dim(flat, links.index * length, length)
    for which, row, col_sum, weighted, mine in (
        (2, row3, col3, weighted3, own_rows[0]),
        (3, row4, col4, weighted4, own_rows[1]),
    ):
        row_count, col_count = shapes[which]
        col = DECAY * old_cols[which] + (1.0 - DECAY) * (col_sum / row_count)
        mean_row = jnp.mean(row)
        update_sizes[which] = jnp.sqrt(
            jnp.sum(weighted / col) * mean_row / (row_count * col_count)
        )
        rows_out[which], cols_out[which] = row, col
        factors[which] = lax.rsqrt(mine[:, None] * col[None, :] / mean_row)
    token_grads = [token_grads[0], token_grads[1]]
    own_grads = token_grads + [grad3, grad4]
    for which in range(4):
        row_count, col_count = shapes[which]
        scale = jnp.sqrt(weight_squares[which] / (row_count * col_count) + 1e-06)
        scale = STEP * scale / jnp.maximum(1.0, update_sizes[which] / CLIP)
        update = (own_grads[which] * factors[which] * scale).reshape(-1)
        new_weights[which] = masters[which] - update

    gain_grads = jnp.stack([dg1, dg2])
    gain_stats = DECAY * gain_states + (1.0 - DECAY) * (gain_grads * gain_grads + 1e-30)
    gain_update = gain_grads * lax.rsqrt(gain_stats)
    gain_sizes = jnp.sqrt(jnp.mean(gain_update * gain_update, axis=1))
    gain_update = gain_update / jnp.maximum(1.0, gain_sizes / CLIP)[:, None]
    gain_scale = jnp.sqrt(jnp.mean(gains * gains, axis=1) + 1e-06)
    new_gains = gains - STEP * gain_scale[:, None] * gain_update
    update_rms = jnp.concatenate([jnp.stack(update_sizes), gain_sizes])
    return (
        block_out,
        grad_input,
        token_grads[0],
        token_grads[1],
        grad3.reshape(-1),
        grad4.reshape(-1),
        new_weights[0],
        new_weights[1],
        new_weights[2],
        new_weights[3],
        gain_grads,
        gain_stats,
        new_gains,
        jnp.concatenate(rows_out),
        jnp.concatenate(cols_out),
        update_rms,
    )


def solution(mesh):
    split = P("fsdp")
    images = P("fsdp", None, None)
    in_specs = (images, images) + (split,) * 5 + (P(),) * 4
    out_specs = (images, images) + (split,) * 8 + (P(),) * 6
    return jax.shard_map(
        shards, mesh=mesh, in_specs=in_specs, out_specs=out_specs, check_vma=False
    )
```

```python
import functools

import jax
import jax.numpy as jnp
from jax import lax
from jax.experimental import pallas as pl
from jax.experimental.pallas import tpu as pltpu
from jax.sharding import PartitionSpec as P

D = 768
PATCHES = 196
HIDDEN = 384
DC = 3072
UNITS = 2
F = DC // (2 * UNITS)
BLOCKS = 16
TILE = D // BLOCKS

DECAY = 0.5
CLIP = 0.5
STEP = 1.0

NN = ((1,), (0,))
NT = ((1,), (1,))
TN = ((0,), (0,))

GELU_A = 0.7978845608028654
GELU_B = 0.7978845608028654 * 0.044715

BF = jnp.bfloat16
F32 = jnp.float32


def dot(a, b, dims):
    return lax.dot_general(a, b, (dims, ((), ())), preferred_element_type=F32)


def gelu_pair(v):
    square = v * v
    t = jnp.tanh(v * (GELU_A + GELU_B * square))
    half = 0.5 + 0.5 * t
    slope = half + (0.5 * v) * (1.0 - t * t) * (GELU_A + (3.0 * GELU_B) * square)
    return v * half, slope


def normalize(values):
    centred = values - jnp.mean(values, axis=-1, keepdims=True)
    spread = jnp.mean(centred * centred, axis=-1, keepdims=True)
    inverse = lax.rsqrt(spread + 1e-06)
    return centred * inverse, inverse


def norm_back(grad, normed, inverse):
    first = jnp.mean(grad, axis=-1, keepdims=True)
    second = jnp.mean(grad * normed, axis=-1, keepdims=True)
    return inverse * (grad - first - normed * second)


ANY = pl.BlockSpec(memory_space=pl.ANY)
SMEM = pl.BlockSpec(memory_space=pltpu.SMEM)
VMEM = pl.BlockSpec(memory_space=pltpu.VMEM)


def struct(shape, dtype):
    return jax.ShapeDtypeStruct(shape, dtype)


def held(shape, dtype):
    return pltpu.VMEM(shape, dtype)


def hbm(shape, dtype):
    return pltpu.HBM(shape, dtype)


def call(kernel, name, inputs, in_specs, outs, scratch=(), mib=16, grid=(), out_specs=None):
    return pl.pallas_call(
        kernel,
        grid=grid,
        in_specs=in_specs,
        out_specs=out_specs or [VMEM] * len(outs),
        out_shape=outs,
        scratch_shapes=scratch,
        compiler_params=pltpu.CompilerParams(vmem_limit_bytes=mib * 2**20),
        cost_estimate=pl.CostEstimate(flops=1024, bytes_accessed=1024, transcendentals=0),
        name=name,
    )(*inputs)


def tiled(rows, size, body, carry=0):
    def step(at, carry):
        return body(pl.ds(pl.multiple_of(at * size, 16), size), at * size, carry)

    return lax.fori_loop(0, rows // size, step, carry)


LANES = 128
GROUP = D // LANES


def split(rows, dtype=F32):
    return held((GROUP, rows, LANES), dtype)


def put_rows(ref, here, value):
    for at in range(GROUP):
        ref[at, here, :] = value[:, at * LANES : (at + 1) * LANES]


def get_rows(ref, here):
    return jnp.concatenate([ref[at, here, :] for at in range(GROUP)], axis=1)


def of_image(at, count):
    return pl.ds(at, PATCHES, stride=count)


def lane_block(rows):
    return pl.BlockSpec((rows, D), lambda i: (0, i))


def row_block(rows, columns=D):
    return pl.BlockSpec((rows, columns), lambda i: (i, 0))


def used(counts, first, size, count):
    row = lax.broadcasted_iota(jnp.int32, (size, 1), 0) + first
    return lax.rem(row, count) < counts[0]


def column_sums(value):
    return jnp.sum(value.reshape(-1, 8, D), axis=0)


def from_hbm(x):
    return pltpu.with_memory_space_constraint(x, pltpu.HBM)


def prepare_kernel(place, w12, w3, w4, mine, theirs, local4, wide3, wide4, squares):
    rows3, rows4 = wide3.shape[1], wide4.shape[0]
    sub = rows4 // UNITS
    first = place[0] == 0
    per3, per4 = DC // LANES, D // LANES
    full = jnp.concatenate([w3[pl.ds(j, rows3, stride=per3), :] for j in range(per3)], axis=1)
    parts = []
    for at in range(2 * UNITS):
        step = 2 * UNITS * sub
        part = jnp.concatenate(
            [full[:, m * step + at * sub : m * step + (at + 1) * sub] for m in range(DC // step)],
            axis=1,
        )
        wide3[at] = part
        parts.append(part.astype(BF))
    for u in range(UNITS):
        mine[u] = jnp.where(first, parts[u], parts[UNITS + u])
        theirs[u] = jnp.where(first, parts[UNITS + u], parts[u])
    four = jnp.concatenate([w4[pl.ds(j, rows4, stride=per4), :] for j in range(per4)], axis=1)
    wide4[...] = four
    for u in range(UNITS):
        local4[u] = four[u * sub : (u + 1) * sub, :].astype(BF)
    squares[...] = jnp.zeros_like(squares)
    for at, value in enumerate((w12[0:1, :], w12[1:2, :], full, four)):
        total = jnp.sum(jnp.sum(value * value, axis=1, keepdims=True), axis=0, keepdims=True)
        squares[at : at + 1, :] = jnp.broadcast_to(total, (1, LANES))


def prepare(place, w12, w3, w4):
    rows3, rows4 = w3.size // DC, w4.size // D
    return call(
        prepare_kernel,
        "prepare",
        [place, w12, w3.reshape(-1, LANES), w4.reshape(-1, LANES)],
        [SMEM, VMEM, VMEM, VMEM],
        [
            struct((UNITS, rows3, F), BF),
            struct((UNITS, rows3, F), BF),
            struct((UNITS, rows4 // UNITS, D), BF),
            struct((2 * UNITS, rows3, F), F32),
            struct((rows4, D), F32),
            struct((8, LANES), F32),
        ],
        mib=8,
    )


def first_kernel(count, counts, x, cot, gains, y1, dout, scratch):
    size = x.shape[0]
    step = pl.program_id(0)
    normed, _ = normalize(x[...].astype(F32))
    put_rows(scratch, pl.ds(pl.multiple_of(step * size, 16), size), normed * gains[0:1, :])
    keep = used(counts, step * size, size, count)
    dout[...] = jnp.where(keep, cot[...].astype(F32), 0.0).astype(BF)

    @pl.when(step == pl.num_programs(0) - 1)
    def _():
        for at in range(count):
            y1[:, at * D : (at + 1) * D] = get_rows(scratch, of_image(at, count)).astype(BF)


def first_norm(counts, x, cot, gains):
    rows = x.shape[0]
    count = rows // PATCHES
    size = rows // 7
    return call(
        functools.partial(first_kernel, count),
        "first_norm",
        [counts, from_hbm(x), from_hbm(cot), gains],
        [SMEM, row_block(size), row_block(size), VMEM],
        [held((PATCHES, count * D), BF), held((rows, D), BF)],
        [split(rows)],
        mib=16,
        grid=(7,),
        out_specs=[VMEM, row_block(size)],
    )


def token_kernel(count, x, y1, w1, w2, gains, h, slope, x1, y2, scratch):
    size = x.shape[0]
    step = pl.program_id(0)

    @pl.when(step < count)
    def _():
        act, der = gelu_pair(dot(w1[...], y1[...], TN))
        act = act.astype(BF)
        h[...] = act
        slope[...] = der.astype(BF)
        put_rows(scratch, of_image(step, count), dot(w2[...], act, TN))

    @pl.when(step >= count)
    def _():
        here = pl.ds(pl.multiple_of((step - count) * size, 16), size)
        mixed = x[...].astype(F32) + get_rows(scratch, here)
        x1[...] = mixed
        normed, _ = normalize(mixed)
        y2[...] = (normed * gains[1:2, :]).astype(BF)


def token_forward(x, y1, w1, w2, gains):
    rows = x.shape[0]
    count = rows // PATCHES
    size = rows // 7
    later = pl.BlockSpec((size, D), lambda i: (jnp.maximum(i - count, 0), 0))

    def early(rows):
        return pl.BlockSpec((rows, D), lambda i: (0, jnp.minimum(i, count - 1)))

    return call(
        functools.partial(token_kernel, count),
        "token_forward",
        [from_hbm(x), y1, w1, w2, gains],
        [later, early(PATCHES), VMEM, VMEM, VMEM],
        [
            hbm((HIDDEN, count * D), BF),
            hbm((HIDDEN, count * D), BF),
            hbm((rows, D), F32),
            held((rows, D), BF),
        ],
        [split(rows)],
        mib=16,
        grid=(count + 7,),
        out_specs=[early(HIDDEN), early(HIDDEN), later, later],
    )


def load_unit(table, lo, hi, dest, sems):
    copies = []
    for at in range(BLOCKS):
        source = (lo, hi)[at * 2 // BLOCKS].at[at % (BLOCKS // 2)]
        row = pl.multiple_of(table[at] * TILE, 16)
        copies.append(pltpu.make_async_copy(source, dest.at[pl.ds(row, TILE), :], sems.at[at]))
    for copy in copies:
        copy.start()
    return copies


def store_blocks(table, send, keep, total):
    half = BLOCKS // 2
    for at in range(BLOCKS):
        block = total[at * TILE : (at + 1) * TILE, :]
        place = table[BLOCKS + at]

        @pl.when(place < half)
        def _():
            keep[place] = block

        @pl.when(place >= half)
        def _():
            send[place - half] = block


def rows_forward(y2, weight, act, slope):
    def body(here, first, carry):
        value, der = gelu_pair(dot(y2[here, :], weight[...], NN))
        act[here, :] = value.astype(BF)
        slope[here, :] = der.astype(BF)
        return carry

    tiled(y2.shape[0], y2.shape[0] // 4, body)


def forward_kernel(table, lo, hi, y2, act, slope, weight, sems):
    for copy in load_unit(table, lo, hi, weight, sems):
        copy.wait()
    rows_forward(y2, weight, act, slope)


def channel_forward(table, lo, hi, y2):
    acts = held((y2.shape[0], F), BF)
    return call(
        forward_kernel,
        "channel_forward",
        [table, lo, hi, y2],
        [SMEM, ANY, ANY, VMEM],
        [acts, acts, held((D, F), BF)],
        [pltpu.SemaphoreType.DMA((BLOCKS,))],
        mib=10,
    )


def forward_grad_kernel(table, weight, y2, act0, dout0, dout1, act, slope, send, keep):
    rows_forward(y2, weight, act, slope)
    total = dot(act0[...], dout0[...], TN) + dot(act[...], dout1[...], TN)
    store_blocks(table, send, keep, total.astype(BF))


def channel_forward_grad(table, weight, y2, act0, dout0, dout1):
    acts = held((y2.shape[0], F), BF)
    half = held((BLOCKS // 2, TILE, D), BF)
    return call(
        forward_grad_kernel,
        "channel_forward_grad",
        [table, weight, y2, act0, dout0, dout1],
        [SMEM] + [VMEM] * 5,
        [acts, acts, half, half],
        mib=14,
    )


def backward_kernel(table, lo, hi, dout0, dout1, y0, y1, slope0, slope1, dc0, dc1, send, keep, weight, sems):
    for copy in load_unit(table, lo, hi, weight, sems):
        copy.wait()
    for dout, slope, dc in ((dout0, slope0, dc0), (dout1, slope1, dc1)):

        def body(here, first, carry, dout=dout, slope=slope, dc=dc):
            value = slope[here, :].astype(F32) * dot(dout[here, :], weight[...], NT)
            dc[here, :] = value.astype(BF)
            return carry

        tiled(dout.shape[0], dout.shape[0] // 4, body)
    total = dot(y0[...], dc0[...], TN) + dot(y1[...], dc1[...], TN)
    store_blocks(table, send, keep, total.astype(BF))


def channel_backward(table, lo, hi, dout0, dout1, y0, y1, slope0, slope1):
    acts = held((y0.shape[0], F), BF)
    half = held((BLOCKS // 2, TILE, D), BF)
    return call(
        backward_kernel,
        "channel_backward",
        [table, lo, hi, dout0, dout1, y0, y1, slope0, slope1],
        [SMEM, ANY, ANY] + [VMEM] * 6,
        [acts, acts, half, half, held((F, D), BF)],
        [pltpu.SemaphoreType.DMA((BLOCKS,))],
        mib=16,
    )


def partial_kernel(dims, a0, a1, w0, w1, out):
    def body(here, first, carry):
        total = dot(a0[here, :], w0[...], dims) + dot(a1[here, :], w1[...], dims)
        out[here, :] = total.astype(BF)
        return carry

    tiled(a0.shape[0], a0.shape[0] // 4, body)


def partial_product(name, dims, acts, weights):
    return call(
        functools.partial(partial_kernel, dims),
        name,
        [*acts, *weights],
        [VMEM] * 4,
        [held((acts[0].shape[0], D), BF)],
        mib=8,
    )[0]


def second_kernel(d0, d1, w0, w1, got, dout, x1, gains, dx1, dg2):
    step = pl.program_id(0)
    size = x1.shape[0]
    here = pl.ds(pl.multiple_of(step * size, 16), size)
    grad = dot(d0[here, :], w0[...], NT) + dot(d1[here, :], w1[...], NT)
    grad += got[here, :].astype(F32)
    normed, inverse = normalize(x1[...])
    total = dout[here, :].astype(F32) + norm_back(grad * gains[1:2, :], normed, inverse)
    put_rows(dx1, here, total)
    sums = jnp.sum(column_sums(grad * normed), axis=0, keepdims=True)

    @pl.when(step == 0)
    def _():
        dg2[...] = sums

    @pl.when(step > 0)
    def _():
        dg2[...] += sums


def second_back(dcs, weights, got, dout, x1, gains):
    rows = x1.shape[0]
    return call(
        second_kernel,
        "second_back",
        [*dcs, *weights, got, dout, from_hbm(x1), gains],
        [VMEM] * 6 + [row_block(rows // 7), VMEM],
        [split(rows), held((1, D), F32)],
        mib=10,
        grid=(7,),
    )


def token_back_kernel(dx1, h, slope, y1, w2, da, g1, g2):
    step = pl.program_id(0)
    count = dx1.shape[1] // PATCHES
    low = get_rows(dx1, pl.ds(step, PATCHES, stride=count)).astype(BF)
    back = (slope[...].astype(F32) * dot(w2[...], low, NN)).astype(BF)
    da[...] = back
    one = dot(y1[...], back, NT)
    two = dot(h[...], low, NT)

    @pl.when(step == 0)
    def _():
        g1[...] = one
        g2[...] = two

    @pl.when(step > 0)
    def _():
        g1[...] += one
        g2[...] += two


def token_back(dx1, h, slope, y1, w2):
    count = dx1.shape[1] // PATCHES
    return call(
        token_back_kernel,
        "token_back",
        [dx1, from_hbm(h), from_hbm(slope), y1, w2],
        [VMEM, lane_block(HIDDEN), lane_block(HIDDEN), lane_block(PATCHES), VMEM],
        [
            held((HIDDEN, count * D), BF),
            held((PATCHES, HIDDEN), F32),
            held((HIDDEN, PATCHES), F32),
        ],
        mib=12,
        grid=(count,),
        out_specs=[lane_block(HIDDEN), VMEM, VMEM],
    )


def input_kernel(count, x, da, dx1, w1, gains, out, dg1, scratch):
    step = pl.program_id(0)
    size = out.shape[0]

    @pl.when(step == 0)
    def _():
        for at in range(count):
            lanes = slice(at * D, (at + 1) * D)
            put_rows(scratch, of_image(at, count), dot(w1[...], da[:, lanes], NN))
        dg1[...] = jnp.zeros_like(dg1)

    here = pl.ds(pl.multiple_of(step * size, 8), size)
    grad = get_rows(scratch, here)
    normed, inverse = normalize(x[...].astype(F32))
    dg1[...] += jnp.sum(column_sums(grad * normed), axis=0, keepdims=True)
    out[...] = get_rows(dx1, here) + norm_back(grad * gains[0:1, :], normed, inverse)


def input_gradient(x, da, dx1, w1, gains):
    rows = x.shape[0]
    count = rows // PATCHES
    size = rows // 7
    return call(
        functools.partial(input_kernel, count),
        "input_gradient",
        [from_hbm(x), da, dx1, w1, gains],
        [row_block(size), VMEM, VMEM, VMEM, VMEM],
        [hbm((rows, D), F32), held((1, D), F32)],
        [split(rows)],
        mib=16,
        grid=(7,),
        out_specs=[row_block(size), VMEM],
    )


def out_kernel(count, counts, a0, a1, w0, w1, got, x1, out):
    size = out.shape[0]
    first = pl.program_id(0) * size
    here = pl.ds(pl.multiple_of(first, 16), size)
    total = dot(a0[here, :], w0[...], NN) + dot(a1[here, :], w1[...], NN)
    total += got[here, :].astype(F32) + x1[...]
    out[...] = jnp.where(used(counts, first, size, count), total, 0.0)


def block_output(counts, acts, weights, got, x1):
    rows = x1.shape[0]
    size = rows // 7
    return call(
        functools.partial(out_kernel, rows // PATCHES),
        "block_output",
        [counts, *acts, *weights, got, from_hbm(x1)],
        [SMEM] + [VMEM] * 5 + [row_block(size)],
        [hbm((rows, D), F32)],
        mib=12,
        grid=(7,),
        out_specs=[row_block(size)],
    )[0]


def join_kernel(*refs):
    rows = refs[0].shape[0]
    for at, ref in enumerate(refs[:-1]):
        refs[-1][at * rows : (at + 1) * rows, :] = ref[...]


def join(parts):
    shape = parts[0].shape
    flat = [x.reshape(-1, D) for x in parts]
    out = held((len(parts) * flat[0].shape[0], D), BF)
    x = call(join_kernel, "join", flat, [VMEM] * len(parts), [out], mib=8)[0]
    return x.reshape((len(parts) * shape[0],) + shape[1:])


def fold_kernel(parts, splits, *refs):
    rows = refs[0].shape[0] // splits
    for at in range(splits):
        here = slice(at * rows, (at + 1) * rows)
        total = refs[0][here, :].astype(F32)
        for part in refs[1:parts]:
            total = total + part[here, :].astype(F32)
        refs[parts + at][...] = total.astype(refs[parts + at].dtype)


def fold(parts, splits):
    shape = parts[0].shape
    lead = shape[0] // splits
    flat = [x.reshape(-1, D) for x in parts]
    rows = flat[0].shape[0] // splits
    dtypes = [F32 if lead == 1 else BF] + [BF] * (splits - 1)
    outs = call(
        functools.partial(fold_kernel, len(parts), splits),
        "fold",
        flat,
        [VMEM] * len(parts),
        [held((rows, D), dtype) for dtype in dtypes],
        mib=10,
    )
    return [x.reshape((lead,) + shape[1:]) for x in outs]


def end_kernel(counts, *refs):
    place, refs = refs[0], refs[1:]
    mine, theirs = refs[-2:]
    rows = mine.shape[1]
    first = place[0] == 0
    at = 0
    for unit, count in enumerate(counts):
        total = refs[at][...].astype(F32)
        for ref in refs[at + 1 : at + count]:
            total = total + ref[...].astype(F32)
        at += count
        mine[unit] = jnp.where(first, total[:rows], total[rows:])
        theirs[unit] = jnp.where(first, total[rows:], total[:rows])


def end_sums(place, units):
    flat = [x.reshape(-1, D) for unit in units for x in unit]
    rows = flat[0].shape[0] // 2
    out = held((UNITS, rows, F), F32)
    return call(
        functools.partial(end_kernel, [len(unit) for unit in units]),
        "end_sums",
        [place, *flat],
        [SMEM] + [VMEM] * len(flat),
        [out, out],
        mib=8,
    )


def in_order(place, mine, got):
    first = place[0] == 0
    own = [mine[u] for u in range(UNITS)]
    other = [got[u] for u in range(UNITS)]
    return [jnp.where(first, x, y) for x, y in zip(own + other, other + own)]


def natural(parts, sub):
    return jnp.concatenate(
        [part[:, m * sub : (m + 1) * sub] for m in range(F // sub) for part in parts], axis=1
    )


def put_flat(ref, value):
    per = value.shape[1] // LANES
    for j in range(per):
        ref[pl.ds(j, value.shape[0], stride=per), :] = value[:, j * LANES : (j + 1) * LANES]


STATS = 24
COL3, WEIGHTED3, COL4, WEIGHTED4, ROW3, ROW4, GAINS, SQUARES = 0, 4, 8, 9, 10, 11, 15, 17


def row_statistics(index, grad, squares, old, vec, start):
    rows = grad.shape[0]
    spots = old.shape[0]
    column = lax.broadcasted_iota(jnp.int32, (rows, D), 1)
    target = lax.broadcasted_iota(jnp.int32, (rows, D), 0) + index * rows
    here = [column + spot * D == target for spot in range(spots)]
    before = sum(
        jnp.sum(jnp.where(mask, old[spot : spot + 1, :], 0.0), axis=1, keepdims=True)
        for spot, mask in enumerate(here)
    )
    mean = squares / (grad.shape[1]) + 1e-30
    row = DECAY * before + (1.0 - DECAY) * mean
    for spot, mask in enumerate(here):
        vec[start + spot : start + spot + 1, :] = jnp.sum(
            jnp.where(mask, row, 0.0), axis=0, keepdims=True
        )
    return row


def stats_kernel(sub, place, mine, got, g4, old3, old4, dg1, dg2, sums, vec, flat3, flat4, row3, row4):
    parts = in_order(place, mine, got)
    index = place[1]
    rows3 = parts[0].shape[0]
    squared = [x * x for x in parts]
    vec[...] = jnp.zeros_like(vec)
    total = sum(jnp.sum(x, axis=1, keepdims=True) for x in squared)
    wide = jnp.concatenate(squared, axis=1)
    row = row_statistics(index, wide, total, old3, vec, ROW3)
    row3[...] = jnp.broadcast_to(row, (rows3, LANES))
    scale = 1.0 / row
    for at, x in enumerate(squared):
        vec[COL3 + at : COL3 + at + 1, :] = jnp.sum(x, axis=0, keepdims=True)
        vec[WEIGHTED3 + at : WEIGHTED3 + at + 1, :] = jnp.sum(x * scale, axis=0, keepdims=True)
    four = g4[...]
    square4 = four * four
    row = row_statistics(
        index, square4, jnp.sum(square4, axis=1, keepdims=True), old4, vec, ROW4
    )
    row4[...] = jnp.broadcast_to(row, (four.shape[0], LANES))
    vec[COL4 : COL4 + 1, :] = jnp.sum(square4, axis=0, keepdims=True)
    vec[WEIGHTED4 : WEIGHTED4 + 1, :] = jnp.sum(square4 * (1.0 / row), axis=0, keepdims=True)
    vec[GAINS : GAINS + 1, :] = dg1[...]
    vec[GAINS + 1 : GAINS + 2, :] = dg2[...]
    vec[SQUARES : SQUARES + 4, 0:LANES] = sums[0:4, :]
    put_flat(flat3, natural(parts, sub))
    put_flat(flat4, four)


def statistics(place, mine, got, g4, old3, old4, dg1, dg2, sums, sub):
    rows3, rows4 = mine.shape[1], g4.shape[0]
    inputs = [place, mine, got, g4, old3, old4, dg1, dg2, sums]
    return call(
        functools.partial(stats_kernel, sub),
        "statistics",
        inputs,
        [SMEM] + [VMEM] * 8,
        [
            struct((STATS, D), F32),
            struct((rows3 * DC // LANES, LANES), F32),
            struct((rows4 * D // LANES, LANES), F32),
            held((rows3, LANES), F32),
            held((rows4, LANES), F32),
        ],
        mib=12,
    )


def lane_total(x):
    return jnp.sum(jnp.sum(x, axis=1, keepdims=True), axis=0, keepdims=True)


def update_kernel(sub, place, vec, mine, got, g4, wide3, wide4, row3, row4, old3, old4, new3, new4, col3, col4, sizes):
    parts = in_order(place, mine, got)
    count = float(D * DC)
    sizes[...] = jnp.zeros_like(sizes)
    for which in range(2):
        rows = vec[ROW3 : ROW3 + 1, :] if which == 0 else vec[ROW4 : ROW4 + 4, :]
        mean = lane_total(rows) / (D if which == 0 else DC)
        if which == 0:
            cols = DECAY * old3[...] + (1.0 - DECAY) * (vec[COL3 : COL3 + 4, :] / D + 1e-30)
            weighted = vec[WEIGHTED3 : WEIGHTED3 + 4, :]
        else:
            cols = DECAY * old4[...] + (1.0 - DECAY) * (vec[COL4 : COL4 + 1, :] / DC + 1e-30)
            weighted = vec[WEIGHTED4 : WEIGHTED4 + 1, :]
        size = jnp.sqrt(lane_total(weighted / cols) * mean / count)
        sizes[which : which + 1, :] = jnp.broadcast_to(size, (1, LANES))
        square = vec[SQUARES + 2 + which : SQUARES + 3 + which, 0:1]
        scale = STEP * jnp.sqrt(square / count + 1e-06) / jnp.maximum(1.0, size / CLIP)
        if which == 0:
            left = lax.rsqrt(row3[:, 0:1] / mean) * scale
            right = lax.rsqrt(cols)
            new = [
                wide3[at] - parts[at] * left * right[at : at + 1, :] for at in range(2 * UNITS)
            ]
            put_flat(new3, natural(new, sub))
            col3[...] = natural([cols[at : at + 1, :] for at in range(2 * UNITS)], sub)
        else:
            left = lax.rsqrt(row4[:, 0:1] / mean) * scale
            put_flat(new4, wide4[...] - g4[...] * left * lax.rsqrt(cols))
            col4[...] = cols


def update(place, vec, mine, got, g4, wide3, wide4, row3, row4, old3, old4, sub):
    inputs = [place, vec, mine, got, g4, wide3, wide4, row3, row4, old3, old4]
    return call(
        functools.partial(update_kernel, sub),
        "update",
        inputs,
        [SMEM] + [VMEM] * 10,
        [
            struct((wide3.size // LANES, LANES), F32),
            struct((wide4.size // LANES, LANES), F32),
            struct((1, DC), F32),
            struct((1, D), F32),
            struct((8, LANES), F32),
        ],
        mib=12,
    )


def expand(row, col, start, length):
    columns = col.shape[0]
    covered = length // columns + 2
    padded = jnp.concatenate([row, jnp.ones((covered,), F32)])
    here = lax.dynamic_slice(padded, (start // columns,), (covered,))
    whole = (here[:, None] * col[None, :]).reshape(-1)
    return lax.dynamic_slice(whole, (start % columns,), (length,))


class Links:
    def __init__(self, size, token):
        self.size = size
        self.chips = size // 2
        bits = self.chips.bit_length() - 1
        high = [1 << b for b in range(2, bits)]
        self.groups = [high[at : at + 2] for at in range(0, len(high), 2)]
        self.orders = (high + [1, 2], high + [2, 1])
        self.index = lax.axis_index("fsdp")
        self.core = self.index & 1
        self.chip = self.index >> 1
        self.token = token

    def tie(self, x):
        x, self.token = lax.optimization_barrier((x, self.token))
        return x

    land = tie

    def run(self, function, *inputs):
        return self.tie(function(*self.tie(inputs)))

    def swap(self, x, mask):
        return lax.ppermute(self.tie(x), "fsdp", [(i, i ^ mask) for i in range(self.size)])

    def cross(self, x, last):
        masks = (2, 1) if last else (1, 2)
        pairs = [(i, i ^ (masks[i & 1] << 1)) for i in range(self.size)]
        return lax.ppermute(self.tie(x), "fsdp", pairs)

    def masks(self, group):
        return [
            sum(bit for at, bit in enumerate(group) if (j >> at) & 1)
            for j in range(1, 1 << len(group))
        ]

    def owners(self, core):
        place = jnp.arange(self.chips, dtype=jnp.int32)
        owner = jnp.full((self.chips,), self.chip, jnp.int32)
        for level in range(len(self.orders[0])):
            bit = (place >> level) & 1
            mask = jnp.where(core == 0, self.orders[0][level], self.orders[1][level])
            owner = owner ^ (bit * mask)
        return owner

    def places(self, core):
        relative = jnp.arange(self.chips, dtype=jnp.int32) ^ self.chip
        place = jnp.zeros_like(relative)
        for level in range(len(self.orders[0])):
            mask = jnp.where(core == 0, self.orders[0][level], self.orders[1][level])
            place = place | (((relative & mask) != 0).astype(jnp.int32) << level)
        return place

    def table(self, core):
        if self.chips == BLOCKS:
            return jnp.concatenate([self.owners(core), self.places(core)])
        order = jnp.arange(BLOCKS, dtype=jnp.int32)
        return jnp.concatenate([order, order])

    def gather_high(self, x):
        return [x] + [self.swap(x, mask << 1) for mask in self.masks(self.groups[0])]

    def join(self, parts):
        x = self.run(lambda *p: join(p), *self.land(parts))
        for group in self.groups[1:]:
            parts = [x] + [self.swap(x, mask << 1) for mask in self.masks(group)]
            x = self.run(lambda *p: join(p), *self.land(parts))
        return x

    def scatter_high(self, x, received):
        for group in reversed(self.groups[1:]):
            own, *sends = self.run(lambda *p, g=group: fold(p, 1 << len(g)), x, *received)
            x, received = own, [
                self.swap(s, mask << 1) for s, mask in zip(sends, self.masks(group))
            ]
        group = self.groups[0]
        own, *sends = self.run(lambda *p: fold(p, 1 << len(group)), x, *received)
        return own, [self.swap(s, mask << 1) for s, mask in zip(sends, self.masks(group))]

    def scatter_end(self, own, received):
        return self.run(lambda *p: fold(p, 1), own, *received)[0][0]

    def as_blocks(self, halves, core):
        if self.chips == BLOCKS:
            return halves
        x = jnp.take(jnp.concatenate(halves, axis=0), self.places(core), axis=0)
        x = x.reshape(BLOCKS, TILE, D)
        return x[: BLOCKS // 2], x[BLOCKS // 2 :]

    def ordered(self, halves, core):
        if self.chips == BLOCKS:
            return halves
        send, keep = halves
        x = jnp.concatenate([keep, send], axis=0).reshape(self.chips, -1, D)
        x = jnp.take(x, self.owners(core), axis=0)
        return x[self.chips // 2 :], x[: self.chips // 2]

    def flat_join(self, x, got, mask):
        upper = (self.index & mask) != 0
        return jnp.where(
            upper, jnp.concatenate([got, x], axis=1), jnp.concatenate([x, got], axis=1)
        )

    def flat_halves(self, x, mask):
        half = x.shape[1] // 2
        upper = (self.index & mask) != 0
        keep = jnp.where(upper, x[:, half:], x[:, :half])
        send = jnp.where(upper, x[:, :half], x[:, half:])
        return keep, send.astype(BF)


def shards(
    images,
    cotangent,
    counts,
    w_token_in,
    w_token_out,
    w_chan_in,
    w_chan_out,
    gains,
    row_states,
    col_states,
    gain_states,
):
    links = Links(D * DC // w_chan_in.shape[0], counts)
    size, chips, core = links.size, links.chips, links.core
    run, land, swap, cross = links.run, links.land, links.swap, links.cross
    count = images.shape[0]
    rows = count * PATCHES
    table = links.table(core)
    steps = [1 << at for at in range(size.bit_length() - 1)]
    x = images.transpose(1, 0, 2).reshape(rows, D)
    cot = cotangent.transpose(1, 0, 2).reshape(rows, D)
    masters = (w_token_in, w_token_out, w_chan_in, w_chan_out)

    rows3 = D // size
    rows4 = DC // size
    sub = rows4 // UNITS
    w12 = jnp.stack([w_token_in, w_token_out])
    place = jnp.stack([core, links.index])
    token = w12.astype(BF)
    token_got = swap(token, 1)
    mine, theirs, local4, wide3, wide4, weight_squares = run(
        prepare, place, w12, w_chan_in, w_chan_out
    )
    got = swap(theirs, 1)

    edges_r = (0, PATCHES, PATCHES + HIDDEN, PATCHES + HIDDEN + D, PATCHES + HIDDEN + D + DC)
    edges_c = (0, HIDDEN, HIDDEN + PATCHES, HIDDEN + PATCHES + DC, HIDDEN + PATCHES + DC + D)

    def old_statistics(rows, cols):
        rows = [rows[edges_r[k] : edges_r[k + 1]] for k in range(4)]
        cols = [cols[edges_c[k] : edges_c[k + 1]] for k in range(4)]
        rows[2:] = rows[2].reshape(1, D), rows[3].reshape(4, D)
        wide = cols[2].reshape(chips, 2, UNITS, sub).transpose(1, 2, 0, 3).reshape(2 * UNITS, F)
        cols[2:] = wide, cols[3].reshape(1, D)
        return rows, cols

    def blocks(lo, hi):
        return links.as_blocks((lo, hi), core)

    token_got, got = land((token_got, got))
    token = links.flat_join(token, token_got, 1)
    token_got = swap(token, steps[1])
    local3 = jnp.where(
        core == 0, jnp.concatenate([mine, got], axis=1), jnp.concatenate([got, mine], axis=1)
    )[:, None]
    a0 = links.gather_high(local3[0])
    y1, dout = run(first_norm, counts, x, cot, gains)
    token = links.flat_join(token, land(token_got), steps[1])
    token_got = swap(token, steps[2])
    other_dout = swap(dout, 1)
    token = links.flat_join(token, land(token_got), steps[2])
    for mask in steps[3:]:
        token_got = swap(token, mask)
        if mask == steps[-1]:
            a0 = links.join(a0)
            a0_got = cross(a0, False)
            a1 = links.gather_high(local3[1])
        token = links.flat_join(token, land(token_got), mask)
    w1 = token[0].reshape(PATCHES, HIDDEN)
    w2 = token[1].reshape(HIDDEN, PATCHES)
    a0 = run(lambda *p: join(p), a0, land(a0_got))
    a0_hi = cross(a0, True)
    old_rows, old_cols = run(old_statistics, row_states, col_states)
    h, slope, x1, y2 = run(token_forward, x, y1, w1, w2, gains)
    other_y2 = swap(y2, 1)
    a1 = links.join(a1)
    a1_got = cross(a1, False)
    b = links.gather_high(local4[:, None].transpose(1, 0, 2, 3))

    act_a0, slope_a0, w3_0 = run(channel_forward, table, *blocks(a0, land(a0_hi)), y2)
    other_y2, other_dout = land((other_y2, other_dout))
    a1 = run(lambda *p: join(p), a1, land(a1_got))
    a1_hi = cross(a1, True)
    act_b0, slope_b0, *c0 = run(
        channel_forward_grad, table, w3_0, other_y2, act_a0, dout, other_dout
    )
    b = links.join(b)
    b_got = cross(b, False)
    act_a1, slope_a1, w3_1 = run(channel_forward, table, *blocks(a1, land(a1_hi)), y2)
    act_b1, slope_b1, *c1 = run(
        channel_forward_grad, table, w3_1, other_y2, act_a1, dout, other_dout
    )
    b = run(lambda *p: join(p), b, land(b_got))
    b_hi = cross(b, True)
    c0, c1 = links.ordered(c0, core), links.ordered(c1, core)
    c_send, c_keep = (jnp.stack(pair, axis=1) for pair in zip(c0, c1))
    c_got = cross(c_send, True)

    b_hi = land(b_hi)
    dc_a0, dc_b0, *d0, w4_0 = run(
        channel_backward,
        table,
        *blocks(b[:, 0], b_hi[:, 0]),
        dout,
        other_dout,
        y2,
        other_y2,
        slope_a0,
        slope_b0,
    )
    d0_send, d0_keep = links.ordered(d0, core)
    d0_got = cross(d0_send, True)
    c_keep, c_send = run(lambda *p: fold(p, 2), c_keep, land(c_got))
    c_got = cross(c_send, False)
    dc_a1, dc_b1, *d1, w4_1 = run(
        channel_backward,
        table,
        *blocks(b[:, 1], b_hi[:, 1]),
        dout,
        other_dout,
        y2,
        other_y2,
        slope_a1,
        slope_b1,
    )
    d1_send, d1_keep = links.ordered(d1, core)
    d1_got = cross(d1_send, True)
    dy2_other = run(
        functools.partial(partial_product, "partial_back", NT), (dc_b0, dc_b1), (w3_0, w3_1)
    )
    dy2_got = swap(dy2_other, 1)
    d0_keep, d0_send = run(lambda *p: fold(p, 2), d0_keep, land(d0_got))
    d0_got = cross(d0_send, False)
    c_keep, c_got = links.scatter_high(c_keep, [land(c_got)])
    out_other = run(
        functools.partial(partial_product, "partial_out", NN), (act_b0, act_b1), (w4_0, w4_1)
    )
    out_got = swap(out_other, 1)

    dx1, dg2 = run(
        second_back, (dc_a0, dc_a1), (w3_0, w3_1), land(dy2_got), dout, x1, gains
    )
    d1_keep, d1_send = run(lambda *p: fold(p, 2), d1_keep, land(d1_got))
    d1_got = cross(d1_send, False)
    d0_keep, d0_got = links.scatter_high(d0_keep, [land(d0_got)])
    da, g1, g2 = run(token_back, dx1, h, slope, y1, w2)
    keep, send = links.flat_halves(jnp.stack([g1.reshape(-1), g2.reshape(-1)]), steps[-1])
    got = swap(send, steps[-1])
    grad4 = links.scatter_end(c_keep, land(c_got)).reshape(rows4, D)
    d1_keep, d1_got = links.scatter_high(d1_keep, [land(d1_got)])
    grad_input, dg1 = run(input_gradient, x, da, dx1, w1, gains)
    token_grads = keep + land(got).astype(F32)
    for mask in reversed(steps[:-1]):
        keep, send = links.flat_halves(token_grads, mask)
        got = swap(send, mask)
        if mask == steps[0]:
            block_out = run(
                block_output, counts, (act_a0, act_a1), (w4_0, w4_1), land(out_got), x1
            )
        token_grads = keep + land(got).astype(F32)
    mine, theirs = run(
        lambda p, *units: end_sums(p, units), place, [d0_keep, *land(d0_got)], [d1_keep, *land(d1_got)]
    )
    got = land(swap(theirs, 1))
    grad_input = grad_input.reshape(PATCHES, count, D).transpose(1, 0, 2)
    block_out = block_out.reshape(PATCHES, count, D).transpose(1, 0, 2)

    vec, flat3, flat4, row3, row4 = run(
        lambda *p: statistics(*p, sub),
        place, mine, got, grad4, old_rows[2], old_rows[3], dg1, dg2, weight_squares,
    )
    summed, token_all = vec, token_grads.astype(BF)
    for mask in steps:
        vec_got, token_got = land((swap(summed, mask), swap(token_all, mask)))
        summed = summed + vec_got
        token_all = links.flat_join(token_all, token_got, mask)
    token_all = token_all.astype(F32)
    full = (token_all[0].reshape(PATCHES, HIDDEN), token_all[1].reshape(HIDDEN, PATCHES))
    new3, new4, col3, col4, sizes = update(
        place, summed, mine, got, grad4, wide3, wide4, row3, row4, old_cols[2], old_cols[3], sub
    )

    shapes = ((PATCHES, HIDDEN), (HIDDEN, PATCHES))
    rows_out, cols_out, update_sizes, new_weights = [], [], [], []
    for which in range(2):
        row_count, col_count = shapes[which]
        squares = full[which] * full[which]
        row = DECAY * old_rows[which] + (1.0 - DECAY) * jnp.mean(squares + 1e-30, axis=1)
        col = DECAY * old_cols[which] + (1.0 - DECAY) * jnp.mean(squares + 1e-30, axis=0)
        mean_row = jnp.mean(row)
        scaled = squares / (row[:, None] * col[None, :])
        size_of = jnp.sqrt(jnp.mean(scaled) * mean_row)
        rows_out.append(row)
        cols_out.append(col)
        update_sizes.append(size_of)
        length = masters[which].shape[0]
        factor = lax.rsqrt(expand(row, col, links.index * length, length) / mean_row)
        scale = jnp.sqrt(summed[SQUARES + which, 0] / (row_count * col_count) + 1e-06)
        scale = STEP * scale / jnp.maximum(1.0, size_of / CLIP)
        new_weights.append(masters[which] - token_grads[which] * factor * scale)
    rows_out += [summed[ROW3], summed[ROW4 : ROW4 + 4].reshape(-1)]
    cols_out += [col3.reshape(-1), col4.reshape(-1)]
    update_sizes += [sizes[0, 0], sizes[1, 0]]
    new_weights += [new3.reshape(-1), new4.reshape(-1)]
    dg1, dg2 = summed[GAINS], summed[GAINS + 1]

    gain_grads = jnp.stack([dg1, dg2])
    gain_stats = DECAY * gain_states + (1.0 - DECAY) * (gain_grads * gain_grads + 1e-30)
    gain_update = gain_grads * lax.rsqrt(gain_stats)
    gain_sizes = jnp.sqrt(jnp.mean(gain_update * gain_update, axis=1))
    gain_update = gain_update / jnp.maximum(1.0, gain_sizes / CLIP)[:, None]
    gain_scale = jnp.sqrt(jnp.mean(gains * gains, axis=1) + 1e-06)
    new_gains = gains - STEP * gain_scale[:, None] * gain_update
    update_rms = jnp.concatenate([jnp.stack(update_sizes), gain_sizes])
    return (
        block_out,
        grad_input,
        token_grads[0],
        token_grads[1],
        flat3.reshape(-1),
        flat4.reshape(-1),
        new_weights[0],
        new_weights[1],
        new_weights[2],
        new_weights[3],
        gain_grads,
        gain_stats,
        new_gains,
        jnp.concatenate(rows_out),
        jnp.concatenate(cols_out),
        update_rms,
    )


def solution(mesh):
    split = P("fsdp")
    images = P("fsdp", None, None)
    in_specs = (images, images) + (split,) * 5 + (P(),) * 4
    out_specs = (images, images) + (split,) * 8 + (P(),) * 6
    return jax.shard_map(
        shards, mesh=mesh, in_specs=in_specs, out_specs=out_specs, check_vma=False
    )
```

```python
import functools

import jax
import jax.numpy as jnp
from jax import lax
from jax.experimental import pallas as pl
from jax.experimental.pallas import tpu as pltpu
from jax.sharding import PartitionSpec as P

D = 768
PATCHES = 196
HIDDEN = 384
DC = 3072
UNITS = 2
F = DC // (2 * UNITS)
BLOCKS = 16
TILE = D // BLOCKS

PACE = 1.0

DECAY = 0.5
CLIP = 0.5
STEP = 1.0

NN = ((1,), (0,))
NT = ((1,), (1,))
TN = ((0,), (0,))

GELU_A = 0.7978845608028654
GELU_B = 0.7978845608028654 * 0.044715

BF = jnp.bfloat16
F32 = jnp.float32


def dot(a, b, dims):
    return lax.dot_general(a, b, (dims, ((), ())), preferred_element_type=F32)


def gelu_pair(v):
    square = v * v
    t = jnp.tanh(v * (GELU_A + GELU_B * square))
    half = 0.5 + 0.5 * t
    slope = half + (0.5 * v) * (1.0 - t * t) * (GELU_A + (3.0 * GELU_B) * square)
    return v * half, slope


def normalize(values):
    centred = values - jnp.mean(values, axis=-1, keepdims=True)
    spread = jnp.mean(centred * centred, axis=-1, keepdims=True)
    inverse = lax.rsqrt(spread + 1e-06)
    return centred * inverse, inverse


def norm_back(grad, normed, inverse):
    first = jnp.mean(grad, axis=-1, keepdims=True)
    second = jnp.mean(grad * normed, axis=-1, keepdims=True)
    return inverse * (grad - first - normed * second)


ANY = pl.BlockSpec(memory_space=pl.ANY)
SMEM = pl.BlockSpec(memory_space=pltpu.SMEM)
VMEM = pl.BlockSpec(memory_space=pltpu.VMEM)


def struct(shape, dtype):
    return jax.ShapeDtypeStruct(shape, dtype)


def held(shape, dtype):
    return pltpu.VMEM(shape, dtype)


def hbm(shape, dtype):
    return pltpu.HBM(shape, dtype)


def call(kernel, name, inputs, in_specs, outs, scratch=(), mib=16, grid=(), out_specs=None, micros=1.0):
    return pl.pallas_call(
        kernel,
        grid=grid,
        in_specs=in_specs,
        out_specs=out_specs or [VMEM] * len(outs),
        out_shape=outs,
        scratch_shapes=scratch,
        compiler_params=pltpu.CompilerParams(vmem_limit_bytes=mib * 2**20),
        cost_estimate=pl.CostEstimate(
            flops=int(micros * 1.15e9 * PACE), bytes_accessed=1024, transcendentals=0
        ),
        name=name,
    )(*inputs)


def tiled(rows, size, body, carry=0):
    def step(at, carry):
        return body(pl.ds(pl.multiple_of(at * size, 16), size), at * size, carry)

    return lax.fori_loop(0, rows // size, step, carry)


LANES = 128
GROUP = D // LANES


def split(rows, dtype=F32):
    return held((GROUP, rows, LANES), dtype)


def put_rows(ref, here, value):
    for at in range(GROUP):
        ref[at, here, :] = value[:, at * LANES : (at + 1) * LANES]


def get_rows(ref, here):
    return jnp.concatenate([ref[at, here, :] for at in range(GROUP)], axis=1)


def of_image(at, count):
    return pl.ds(at, PATCHES, stride=count)


def lane_block(rows):
    return pl.BlockSpec((rows, D), lambda i: (0, i))


def row_block(rows, columns=D):
    return pl.BlockSpec((rows, columns), lambda i: (i, 0))


def used(counts, first, size, count):
    row = lax.broadcasted_iota(jnp.int32, (size, 1), 0) + first
    return lax.rem(row, count) < counts[0]


def column_sums(value):
    return jnp.sum(value.reshape(-1, 8, D), axis=0)


def from_hbm(x):
    return pltpu.with_memory_space_constraint(x, pltpu.HBM)


def prepare_kernel(place, w12, w3, w4, mine, theirs, local4, wide3, wide4, squares):
    rows3, rows4 = wide3.shape[1], wide4.shape[0]
    sub = rows4 // UNITS
    first = place[0] == 0
    per3, per4 = DC // LANES, D // LANES
    full = jnp.concatenate([w3[pl.ds(j, rows3, stride=per3), :] for j in range(per3)], axis=1)
    parts = []
    for at in range(2 * UNITS):
        step = 2 * UNITS * sub
        part = jnp.concatenate(
            [full[:, m * step + at * sub : m * step + (at + 1) * sub] for m in range(DC // step)],
            axis=1,
        )
        wide3[at] = part
        parts.append(part.astype(BF))
    for u in range(UNITS):
        mine[u] = jnp.where(first, parts[u], parts[UNITS + u])
        theirs[u] = jnp.where(first, parts[UNITS + u], parts[u])
    four = jnp.concatenate([w4[pl.ds(j, rows4, stride=per4), :] for j in range(per4)], axis=1)
    wide4[...] = four
    for u in range(UNITS):
        local4[u] = four[u * sub : (u + 1) * sub, :].astype(BF)
    squares[...] = jnp.zeros_like(squares)
    for at, value in enumerate((w12[0:1, :], w12[1:2, :], full, four)):
        total = jnp.sum(jnp.sum(value * value, axis=1, keepdims=True), axis=0, keepdims=True)
        squares[at : at + 1, :] = jnp.broadcast_to(total, (1, LANES))


def prepare(place, w12, w3, w4):
    rows3, rows4 = w3.size // DC, w4.size // D
    return call(
        prepare_kernel,
        "prepare",
        [place, w12, w3.reshape(-1, LANES), w4.reshape(-1, LANES)],
        [SMEM, VMEM, VMEM, VMEM],
        [
            struct((UNITS, rows3, F), BF),
            struct((UNITS, rows3, F), BF),
            struct((UNITS, rows4 // UNITS, D), BF),
            struct((2 * UNITS, rows3, F), F32),
            struct((rows4, D), F32),
            struct((8, LANES), F32),
        ],
        micros=8,
        mib=8,
    )


def keep_kernel(count, counts, cot, dout):
    size = cot.shape[0]
    keep = used(counts, pl.program_id(0) * size, size, count)
    dout[...] = jnp.where(keep, cot[...].astype(F32), 0.0).astype(BF)


def kept_cotangent(counts, cot):
    rows = cot.shape[0]
    size = rows // 2
    return call(
        functools.partial(keep_kernel, rows // PATCHES),
        "kept_cotangent",
        [counts, from_hbm(cot)],
        [SMEM, row_block(size)],
        [held((rows, D), BF)],
        micros=3,
        grid=(2,),
        out_specs=[row_block(size)],
    )[0]


def first_kernel(count, x, gains, y1, scratch):
    rows = x.shape[0]

    def body(here, first, carry):
        normed, _ = normalize(x[here, :].astype(F32))
        put_rows(scratch, here, normed * gains[0:1, :])
        return carry

    tiled(rows, rows // 7, body)
    for at in range(count):
        y1[:, at * D : (at + 1) * D] = get_rows(scratch, of_image(at, count)).astype(BF)


def first_norm(x, gains):
    rows = x.shape[0]
    count = rows // PATCHES
    return call(
        functools.partial(first_kernel, count),
        "first_norm",
        [x, gains],
        [VMEM, VMEM],
        [held((PATCHES, count * D), BF)],
        [split(rows)],
        micros=4,
        mib=16,
    )[0]


def token_kernel(count, x, y1, w1, w2, gains, x1, y2, scratch):
    rows = x.shape[0]

    def image(at, carry):
        lanes = pl.ds(pl.multiple_of(at * D, LANES), D)
        pre = dot(w1[...], y1[:, lanes], TN)
        act = pre * (0.5 + 0.5 * jnp.tanh(pre * (GELU_A + GELU_B * (pre * pre))))
        put_rows(scratch, of_image(at, count), dot(w2[...], act.astype(BF), TN))
        return carry

    lax.fori_loop(0, count, image, 0, unroll=4)

    def body(here, first, carry):
        mixed = x[here, :].astype(F32) + get_rows(scratch, here)
        x1[here, :] = mixed
        normed, _ = normalize(mixed)
        y2[here, :] = (normed * gains[1:2, :]).astype(BF)
        return carry

    tiled(rows, rows // 7, body)


def token_forward(x, y1, w1, w2, gains):
    rows = x.shape[0]
    count = rows // PATCHES
    return call(
        functools.partial(token_kernel, count),
        "token_forward",
        [x, y1, w1, w2, gains],
        [VMEM] * 5,
        [held((rows, D), F32), held((rows, D), BF)],
        [split(rows)],
        micros=8,
        mib=20,
    )


def load_unit(table, lo, hi, dest, sems):
    copies = []
    for at in range(BLOCKS):
        source = (lo, hi)[at * 2 // BLOCKS].at[at % (BLOCKS // 2)]
        row = pl.multiple_of(table[at] * TILE, 16)
        copies.append(pltpu.make_async_copy(source, dest.at[pl.ds(row, TILE), :], sems.at[at]))
    for copy in copies:
        copy.start()
    return copies


def store_blocks(table, send, keep, total):
    half = BLOCKS // 2
    unit = send.shape[1] - 1
    for at in range(BLOCKS):
        block = total[at * TILE : (at + 1) * TILE, :]
        place = table[BLOCKS + at]

        @pl.when(place < half)
        def _():
            keep[place, unit] = block

        @pl.when(place >= half)
        def _():
            send[place - half, unit] = block


def rows_forward(y2, weight, act, slope):
    def body(here, first, carry):
        value, der = gelu_pair(dot(y2[here, :], weight[...], NN))
        act[here, :] = value.astype(BF)
        slope[here, :] = der.astype(BF)
        return carry

    tiled(y2.shape[0], y2.shape[0] // 4, body)


def forward_kernel(table, lo, hi, y2, act, slope, weight, sems):
    for copy in load_unit(table, lo, hi, weight, sems):
        copy.wait()
    rows_forward(y2, weight, act, slope)


def channel_forward(table, lo, hi, y2):
    acts = held((y2.shape[0], F), BF)
    return call(
        forward_kernel,
        "channel_forward",
        [table, lo, hi, y2],
        [SMEM, ANY, ANY, VMEM],
        [acts, acts, held((D, F), BF)],
        [pltpu.SemaphoreType.DMA((BLOCKS,))],
        micros=7,
        mib=10,
    )


def join_before(before, send, keep):
    if before:
        send[:, 0] = before[0][:, 0]
        keep[:, 0] = before[1][:, 0]


def forward_grad_kernel(table, weight, y2, act0, dout0, dout1, *refs):
    *before, act, slope, send, keep = refs
    rows_forward(y2, weight, act, slope)
    join_before(before, send, keep)
    total = dot(act0[...], dout0[...], TN) + dot(act[...], dout1[...], TN)
    store_blocks(table, send, keep, total.astype(BF))


def channel_forward_grad(table, weight, y2, act0, dout0, dout1, *before):
    acts = held((y2.shape[0], F), BF)
    half = held((BLOCKS // 2, 1 + len(before) // 2, TILE, D), BF)
    return call(
        forward_grad_kernel,
        "channel_forward_grad",
        [table, weight, y2, act0, dout0, dout1, *before],
        [SMEM] + [VMEM] * (5 + len(before)),
        [acts, acts, half, half],
        micros=11,
        mib=15,
    )


def backward_kernel(table, lo, hi, dout0, dout1, slope0, slope1, dc0, dc1, weight, sems):
    for copy in load_unit(table, lo, hi, weight, sems):
        copy.wait()
    for dout, slope, dc in ((dout0, slope0, dc0), (dout1, slope1, dc1)):

        def body(here, first, carry, dout=dout, slope=slope, dc=dc):
            value = slope[here, :].astype(F32) * dot(dout[here, :], weight[...], NT)
            dc[here, :] = value.astype(BF)
            return carry

        tiled(dout.shape[0], dout.shape[0] // 4, body)


def channel_backward(table, lo, hi, dout0, dout1, slope0, slope1):
    acts = held((dout0.shape[0], F), BF)
    return call(
        backward_kernel,
        "channel_backward",
        [table, lo, hi, dout0, dout1, slope0, slope1],
        [SMEM, ANY, ANY] + [VMEM] * 4,
        [acts, acts, held((F, D), BF)],
        [pltpu.SemaphoreType.DMA((BLOCKS,))],
        micros=8,
        mib=12,
    )


def backward_grad_kernel(table, y0, y1, dc0, dc1, *refs):
    *before, send, keep = refs
    total = dot(y0[...], dc0[...], TN) + dot(y1[...], dc1[...], TN)
    join_before(before, send, keep)
    store_blocks(table, send, keep, total.astype(BF))


def channel_backward_grad(table, y0, y1, dc0, dc1, *before):
    half = held((BLOCKS // 2, 1 + len(before) // 2, TILE, D), BF)
    return call(
        backward_grad_kernel,
        "channel_backward_grad",
        [table, y0, y1, dc0, dc1, *before],
        [SMEM] + [VMEM] * (4 + len(before)),
        [half, half],
        micros=6,
        mib=15,
    )


def partial_kernel(dims, a0, a1, w0, w1, out):
    def body(here, first, carry):
        total = dot(a0[here, :], w0[...], dims) + dot(a1[here, :], w1[...], dims)
        out[here, :] = total.astype(BF)
        return carry

    tiled(a0.shape[0], a0.shape[0] // 4, body)


def partial_product(name, dims, acts, weights):
    return call(
        functools.partial(partial_kernel, dims),
        name,
        [*acts, *weights],
        [VMEM] * 4,
        [held((acts[0].shape[0], D), BF)],
        micros=5,
        mib=8,
    )[0]


def second_kernel(d0, d1, w0, w1, got, dout, x1, gains, dx1, dg2):
    def body(here, first, carry):
        grad = dot(d0[here, :], w0[...], NT) + dot(d1[here, :], w1[...], NT)
        grad += got[here, :].astype(F32)
        normed, inverse = normalize(x1[here, :])
        total = dout[here, :].astype(F32) + norm_back(grad * gains[1:2, :], normed, inverse)
        put_rows(dx1, here, total)
        return carry + column_sums(grad * normed)

    rows = x1.shape[0]
    sums = tiled(rows, rows // 4, body, jnp.zeros((8, D), F32))
    dg2[...] = jnp.sum(sums, axis=0, keepdims=True)


def second_back(dcs, weights, got, dout, x1, gains):
    rows = x1.shape[0]
    return call(
        second_kernel,
        "second_back",
        [*dcs, *weights, got, dout, x1, gains],
        [VMEM] * 8,
        [split(rows), held((1, D), F32)],
        micros=9,
        mib=14,
    )


def token_back_kernel(size, touched, length, place, dx1, y1, w1, w2, da, keep, send, g1, g2, every):
    count = dx1.shape[1] // PATCHES
    g1[...] = jnp.zeros_like(g1)
    g2[...] = jnp.zeros_like(g2)

    def body(at, carry):
        lanes = pl.ds(pl.multiple_of(at * D, LANES), D)
        act, slope = gelu_pair(dot(w1[...], y1[:, lanes], TN))
        low = get_rows(dx1, of_image(at, count)).astype(BF)
        back = (slope * dot(w2[...], low, NN)).astype(BF)
        da[:, lanes] = back
        g1[0:PATCHES, :] += dot(y1[:, lanes], back, NT)
        g2[0:HIDDEN, :] += dot(act.astype(BF), low, NT)
        return carry

    lax.fori_loop(0, count, body, 0, unroll=2)
    for at in range(size):
        first = at * length // HIDDEN
        every[at, 0 : touched[0], :] = g1[first : first + touched[0], :]
        first = at * length // PATCHES
        every[at, touched[0] :, 0:PATCHES] = g2[first : first + touched[1], :]
        every[at, touched[0] :, PATCHES:] = jnp.zeros((touched[1], HIDDEN - PATCHES), F32)
    half = size // 2
    upper = place[1] // half
    keep[...] = every[pl.ds(upper * half, half)]
    send[...] = every[pl.ds((1 - upper) * half, half)].astype(BF)


def token_back(size, touched, length, place, dx1, y1, w1, w2):
    count = dx1.shape[1] // PATCHES
    rows = sum(touched)
    return call(
        functools.partial(token_back_kernel, size, touched, length),
        "token_back",
        [place, dx1, y1, w1, w2],
        [SMEM] + [VMEM] * 4,
        [
            held((HIDDEN, count * D), BF),
            held((size // 2, rows, HIDDEN), F32),
            held((size // 2, rows, HIDDEN), BF),
        ],
        [
            pltpu.VMEM((PATCHES + touched[0], HIDDEN), F32),
            pltpu.VMEM((HIDDEN + touched[1], PATCHES), F32),
            pltpu.VMEM((size, rows, HIDDEN), F32),
        ],
        micros=10,
        mib=16,
    )


def input_kernel(count, x, da, dx1, w1, gains, out, dg1, scratch):
    step = pl.program_id(0)
    size = out.shape[0]

    @pl.when(step == 0)
    def _():
        for at in range(count):
            lanes = slice(at * D, (at + 1) * D)
            put_rows(scratch, of_image(at, count), dot(w1[...], da[:, lanes], NN))
        dg1[...] = jnp.zeros_like(dg1)

    here = pl.ds(pl.multiple_of(step * size, 8), size)
    grad = get_rows(scratch, here)
    normed, inverse = normalize(x[...].astype(F32))
    dg1[...] += jnp.sum(column_sums(grad * normed), axis=0, keepdims=True)
    out[...] = get_rows(dx1, here) + norm_back(grad * gains[0:1, :], normed, inverse)


def input_gradient(x, da, dx1, w1, gains):
    rows = x.shape[0]
    count = rows // PATCHES
    size = rows // 4
    return call(
        functools.partial(input_kernel, count),
        "input_gradient",
        [from_hbm(x), da, dx1, w1, gains],
        [row_block(size), VMEM, VMEM, VMEM, VMEM],
        [hbm((rows, D), F32), held((1, D), F32)],
        [split(rows)],
        micros=10,
        mib=16,
        grid=(4,),
        out_specs=[row_block(size), VMEM],
    )


def out_kernel(count, counts, a0, a1, w0, w1, got, x1, out):
    size = out.shape[0]
    first = pl.program_id(0) * size
    here = pl.ds(pl.multiple_of(first, 16), size)
    total = dot(a0[here, :], w0[...], NN) + dot(a1[here, :], w1[...], NN)
    total += got[here, :].astype(F32) + x1[here, :]
    out[...] = jnp.where(used(counts, first, size, count), total, 0.0)


def block_output(counts, acts, weights, got, x1):
    rows = x1.shape[0]
    size = rows // 4
    return call(
        functools.partial(out_kernel, rows // PATCHES),
        "block_output",
        [counts, *acts, *weights, got, x1],
        [SMEM] + [VMEM] * 6,
        [hbm((rows, D), F32)],
        micros=9,
        mib=12,
        grid=(4,),
        out_specs=[row_block(size)],
    )[0]


def join_two(a, b):
    return join([a, b])


def fold_two(a, b):
    return fold([a, b], 2)


def join_kernel(*refs):
    rows = refs[0].shape[0]
    for at, ref in enumerate(refs[:-1]):
        refs[-1][at * rows : (at + 1) * rows, :] = ref[...]


def join(parts):
    shape = parts[0].shape
    flat = [x.reshape(-1, D) for x in parts]
    out = held((len(parts) * flat[0].shape[0], D), BF)
    x = call(join_kernel, "join", flat, [VMEM] * len(parts), [out], mib=8)[0]
    return x.reshape((len(parts) * shape[0],) + shape[1:])


def fold_kernel(parts, splits, *refs):
    rows = refs[0].shape[0] // splits
    for at in range(splits):
        here = slice(at * rows, (at + 1) * rows)
        total = refs[0][here, :].astype(F32)
        for part in refs[1:parts]:
            total = total + part[here, :].astype(F32)
        refs[parts + at][...] = total.astype(refs[parts + at].dtype)


def fold(parts, splits):
    shape = parts[0].shape
    lead = shape[0] // splits
    flat = [x.reshape(-1, D) for x in parts]
    rows = flat[0].shape[0] // splits
    dtypes = [F32 if lead == 1 else BF] + [BF] * (splits - 1)
    outs = call(
        functools.partial(fold_kernel, len(parts), splits),
        "fold",
        flat,
        [VMEM] * len(parts),
        [held((rows, D), dtype) for dtype in dtypes],
        mib=10,
    )
    return [x.reshape((lead,) + shape[1:]) for x in outs]


def end_kernel(place, *refs):
    *parts, mine, theirs = refs
    rows = mine.shape[1]
    first = place[0] == 0
    for unit in range(UNITS):
        total = parts[0][unit].astype(F32)
        for part in parts[1:]:
            total = total + part[unit].astype(F32)
        mine[unit] = jnp.where(first, total[:rows], total[rows:])
        theirs[unit] = jnp.where(first, total[rows:], total[:rows])


def end_sums(place, parts):
    parts = [x[0] for x in parts]
    out = held((UNITS, parts[0].shape[1] // 2, F), F32)
    return call(
        end_kernel,
        "end_sums",
        [place, *parts],
        [SMEM] + [VMEM] * len(parts),
        [out, out],
        mib=8,
    )


def in_order(place, mine, got):
    first = place[0] == 0
    own = [mine[u] for u in range(UNITS)]
    other = [got[u] for u in range(UNITS)]
    return [jnp.where(first, x, y) for x, y in zip(own + other, other + own)]


def natural(parts, sub):
    return jnp.concatenate(
        [part[:, m * sub : (m + 1) * sub] for m in range(F // sub) for part in parts], axis=1
    )


def put_flat(ref, value):
    per = value.shape[1] // LANES
    for j in range(per):
        ref[pl.ds(j, value.shape[0], stride=per), :] = value[:, j * LANES : (j + 1) * LANES]


STATS = 24
COL3, WEIGHTED3, COL4, WEIGHTED4, ROW3, ROW4, GAINS, SQUARES = 0, 4, 8, 9, 10, 11, 15, 17


def row_statistics(index, grad, squares, old, vec, start):
    rows = grad.shape[0]
    spots = old.shape[0]
    column = lax.broadcasted_iota(jnp.int32, (rows, D), 1)
    target = lax.broadcasted_iota(jnp.int32, (rows, D), 0) + index * rows
    here = [column + spot * D == target for spot in range(spots)]
    before = sum(
        jnp.sum(jnp.where(mask, old[spot : spot + 1, :], 0.0), axis=1, keepdims=True)
        for spot, mask in enumerate(here)
    )
    mean = squares / (grad.shape[1]) + 1e-30
    row = DECAY * before + (1.0 - DECAY) * mean
    for spot, mask in enumerate(here):
        vec[start + spot : start + spot + 1, :] = jnp.sum(
            jnp.where(mask, row, 0.0), axis=0, keepdims=True
        )
    return row


ROW1, ROW2, COL1, WEIGHTED1, COL2, WEIGHTED2 = 18, 19, 20, 21, 22, 23


def covered(columns, length, size):
    return max((at * length + length - 1) // columns - at * length // columns + 1 for at in range(size))


def in_piece(index, length, rows, columns):
    first = index * length // columns
    row = lax.broadcasted_iota(jnp.int32, (rows, columns), 0) + first
    at = row * columns + lax.broadcasted_iota(jnp.int32, (rows, columns), 1)
    return first, (at >= index * length) & (at < (index + 1) * length)


def spots(first, rows):
    column = lax.broadcasted_iota(jnp.int32, (rows, D), 1)
    return column == lax.broadcasted_iota(jnp.int32, (rows, D), 0) + first


def token_statistics(index, length, grad, old, vec, row_at, col_at):
    rows, columns = grad.shape
    first, inside = in_piece(index, length, rows, columns)
    squares = grad * grad
    here = spots(first, rows)
    before = jnp.sum(jnp.where(here, old, 0.0), axis=1, keepdims=True)
    mean = jnp.sum(squares, axis=1, keepdims=True) / columns + 1e-30
    row = DECAY * before + (1.0 - DECAY) * mean
    mine = jnp.where(inside, squares, 0.0)
    vec[col_at : col_at + 1, 0:columns] = jnp.sum(mine, axis=0, keepdims=True)
    weighted = jnp.where(inside, squares / row, 0.0)
    vec[col_at + 1 : col_at + 2, 0:columns] = jnp.sum(weighted, axis=0, keepdims=True)
    starts = jnp.where(inside[:, 0:1] & here, row, 0.0)
    vec[row_at : row_at + 1, :] = jnp.sum(starts, axis=0, keepdims=True)


def stats_kernel(sub, length, place, mine, got, g4, old3, old4, dg1, dg2, sums, g1, g2, old1, old2, *refs):
    vec, flat3, flat4, row3, row4 = refs
    parts = in_order(place, mine, got)
    index = place[1]
    rows3 = parts[0].shape[0]
    squared = [x * x for x in parts]
    vec[...] = jnp.zeros_like(vec)
    total = sum(jnp.sum(x, axis=1, keepdims=True) for x in squared)
    wide = jnp.concatenate(squared, axis=1)
    row = row_statistics(index, wide, total, old3, vec, ROW3)
    row3[...] = jnp.broadcast_to(row, (rows3, LANES))
    scale = 1.0 / row
    for at, x in enumerate(squared):
        vec[COL3 + at : COL3 + at + 1, :] = jnp.sum(x, axis=0, keepdims=True)
        vec[WEIGHTED3 + at : WEIGHTED3 + at + 1, :] = jnp.sum(x * scale, axis=0, keepdims=True)
    four = g4[...]
    square4 = four * four
    row = row_statistics(
        index, square4, jnp.sum(square4, axis=1, keepdims=True), old4, vec, ROW4
    )
    row4[...] = jnp.broadcast_to(row, (four.shape[0], LANES))
    vec[COL4 : COL4 + 1, :] = jnp.sum(square4, axis=0, keepdims=True)
    vec[WEIGHTED4 : WEIGHTED4 + 1, :] = jnp.sum(square4 * (1.0 / row), axis=0, keepdims=True)
    vec[GAINS : GAINS + 1, :] = dg1[...]
    vec[GAINS + 1 : GAINS + 2, :] = dg2[...]
    for at in range(4):
        vec[SQUARES : SQUARES + 1, at * LANES : (at + 1) * LANES] = sums[at : at + 1, :]
    token_statistics(index, length, g1[...], old1[...], vec, ROW1, COL1)
    token_statistics(index, length, g2[...], old2[...], vec, ROW2, COL2)
    put_flat(flat3, natural(parts, sub))
    put_flat(flat4, four)


def statistics(sub, length, *inputs):
    rows3, rows4 = inputs[1].shape[1], inputs[3].shape[0]
    return call(
        functools.partial(stats_kernel, sub, length),
        "statistics",
        list(inputs),
        [SMEM] + [VMEM] * (len(inputs) - 1),
        [
            struct((STATS, D), F32),
            struct((rows3 * DC // LANES, LANES), F32),
            struct((rows4 * D // LANES, LANES), F32),
            held((rows3, LANES), F32),
            held((rows4, LANES), F32),
        ],
        micros=2,
        mib=12,
    )


def lane_total(x):
    return jnp.sum(jnp.sum(x, axis=1, keepdims=True), axis=0, keepdims=True)


def token_update(index, length, which, grad, old, vec, row_at, col_at, new, col_out, sizes):
    rows, columns = grad.shape
    count = float(PATCHES * HIDDEN)
    every = PATCHES * HIDDEN // columns
    first, _ = in_piece(index, length, rows, columns)
    row = vec[row_at : row_at + 1, :]
    mean = lane_total(row) / every
    col = DECAY * old[...] + (1.0 - DECAY) * (vec[col_at : col_at + 1, 0:columns] / every + 1e-30)
    weighted = vec[col_at + 1 : col_at + 2, 0:columns]
    size = jnp.sqrt(lane_total(weighted / col) * mean / count)
    sizes[which : which + 1, :] = jnp.broadcast_to(size, (1, LANES))
    square = vec[SQUARES : SQUARES + 1, which * LANES : which * LANES + 1]
    scale = STEP * jnp.sqrt(square / count + 1e-06) / jnp.maximum(1.0, size / CLIP)
    here = spots(first, rows)
    left = jnp.sum(jnp.where(here, row, 0.0), axis=1, keepdims=True)
    known = lax.broadcasted_iota(jnp.int32, (rows, 1), 0) + first < every
    left = jnp.where(known, lax.rsqrt(jnp.where(known, left, 1.0) / mean), 0.0)
    new[...] = grad[...] * left * lax.rsqrt(col) * scale
    col_out[...] = col


def update_kernel(sub, length, place, vec, mine, got, g4, wide3, wide4, row3, row4, old3, old4, *refs):
    g1, g2, old1, old2, new3, new4, col3, col4, sizes, new1, new2, col1, col2 = refs
    parts = in_order(place, mine, got)
    count = float(D * DC)
    sizes[...] = jnp.zeros_like(sizes)
    token_update(place[1], length, 0, g1, old1, vec, ROW1, COL1, new1, col1, sizes)
    token_update(place[1], length, 1, g2, old2, vec, ROW2, COL2, new2, col2, sizes)
    for which in range(2):
        rows = vec[ROW3 : ROW3 + 1, :] if which == 0 else vec[ROW4 : ROW4 + 4, :]
        mean = lane_total(rows) / (D if which == 0 else DC)
        if which == 0:
            cols = DECAY * old3[...] + (1.0 - DECAY) * (vec[COL3 : COL3 + 4, :] / D + 1e-30)
            weighted = vec[WEIGHTED3 : WEIGHTED3 + 4, :]
        else:
            cols = DECAY * old4[...] + (1.0 - DECAY) * (vec[COL4 : COL4 + 1, :] / DC + 1e-30)
            weighted = vec[WEIGHTED4 : WEIGHTED4 + 1, :]
        size = jnp.sqrt(lane_total(weighted / cols) * mean / count)
        sizes[which + 2 : which + 3, :] = jnp.broadcast_to(size, (1, LANES))
        square = vec[SQUARES : SQUARES + 1, (which + 2) * LANES : (which + 2) * LANES + 1]
        scale = STEP * jnp.sqrt(square / count + 1e-06) / jnp.maximum(1.0, size / CLIP)
        if which == 0:
            left = lax.rsqrt(row3[:, 0:1] / mean) * scale
            right = lax.rsqrt(cols)
            new = [
                wide3[at] - parts[at] * left * right[at : at + 1, :] for at in range(2 * UNITS)
            ]
            put_flat(new3, natural(new, sub))
            col3[...] = natural([cols[at : at + 1, :] for at in range(2 * UNITS)], sub)
        else:
            left = lax.rsqrt(row4[:, 0:1] / mean) * scale
            put_flat(new4, wide4[...] - g4[...] * left * lax.rsqrt(cols))
            col4[...] = cols


def update(sub, length, *inputs):
    wide3, wide4 = inputs[5:7]
    g1, g2 = inputs[-4:-2]
    return call(
        functools.partial(update_kernel, sub, length),
        "update",
        list(inputs),
        [SMEM] + [VMEM] * (len(inputs) - 1),
        [
            struct((wide3.size // LANES, LANES), F32),
            struct((wide4.size // LANES, LANES), F32),
            struct((1, DC), F32),
            struct((1, D), F32),
            struct((8, LANES), F32),
            struct(g1.shape, F32),
            struct(g2.shape, F32),
            struct((1, HIDDEN), F32),
            struct((1, PATCHES), F32),
        ],
        micros=2,
        mib=12,
    )


class Links:
    def __init__(self, size, token):
        self.size = size
        self.chips = size // 2
        bits = self.chips.bit_length() - 1
        high = [1 << b for b in range(2, bits)]
        self.groups = [high[at : at + 2] for at in range(0, len(high), 2)]
        self.orders = (high + [1, 2], high + [2, 1])
        self.index = lax.axis_index("fsdp")
        self.core = self.index & 1
        self.chip = self.index >> 1
        self.token = token

    def tie(self, x):
        x, self.token = lax.optimization_barrier((x, self.token))
        return x

    land = tie

    def run(self, function, *inputs, landing=None):
        out = function(*self.tie(inputs))
        if landing is None:
            return self.tie(out)
        return self.tie((out, landing))

    def swap(self, x, mask):
        return lax.ppermute(self.tie(x), "fsdp", [(i, i ^ mask) for i in range(self.size)])

    def cross(self, x, last):
        masks = (2, 1) if last else (1, 2)
        pairs = [(i, i ^ (masks[i & 1] << 1)) for i in range(self.size)]
        return lax.ppermute(self.tie(x), "fsdp", pairs)

    def masks(self, group):
        return [
            sum(bit for at, bit in enumerate(group) if (j >> at) & 1)
            for j in range(1, 1 << len(group))
        ]

    def owners(self, core):
        place = jnp.arange(self.chips, dtype=jnp.int32)
        owner = jnp.full((self.chips,), self.chip, jnp.int32)
        for level in range(len(self.orders[0])):
            bit = (place >> level) & 1
            mask = jnp.where(core == 0, self.orders[0][level], self.orders[1][level])
            owner = owner ^ (bit * mask)
        return owner

    def places(self, core):
        relative = jnp.arange(self.chips, dtype=jnp.int32) ^ self.chip
        place = jnp.zeros_like(relative)
        for level in range(len(self.orders[0])):
            mask = jnp.where(core == 0, self.orders[0][level], self.orders[1][level])
            place = place | (((relative & mask) != 0).astype(jnp.int32) << level)
        return place

    def table(self, core):
        if self.chips == BLOCKS:
            return jnp.concatenate([self.owners(core), self.places(core)])
        order = jnp.arange(BLOCKS, dtype=jnp.int32)
        return jnp.concatenate([order, order])

    def gather_high(self, x):
        return [x] + [self.swap(x, mask << 1) for mask in self.masks(self.groups[0])]

    def join(self, parts):
        x = self.run(lambda *p: join(p), *self.land(parts))
        for group in self.groups[1:]:
            parts = [x] + [self.swap(x, mask << 1) for mask in self.masks(group)]
            x = self.run(lambda *p: join(p), *self.land(parts))
        return x

    def scatter_high(self, x, received):
        for group in reversed(self.groups[1:]):
            own, *sends = self.run(lambda *p, g=group: fold(p, 1 << len(g)), x, *received)
            x, received = own, [
                self.swap(s, mask << 1) for s, mask in zip(sends, self.masks(group))
            ]
        group = self.groups[0]
        own, *sends = self.run(lambda *p: fold(p, 1 << len(group)), x, *received)
        return own, [self.swap(s, mask << 1) for s, mask in zip(sends, self.masks(group))]

    def scatter_end(self, own, received):
        return self.run(lambda *p: fold(p, 1), own, *received)[0][0]

    def as_blocks(self, halves, core):
        if self.chips == BLOCKS:
            return halves
        x = jnp.take(jnp.concatenate(halves, axis=0), self.places(core), axis=0)
        x = x.reshape(BLOCKS, TILE, D)
        return x[: BLOCKS // 2], x[BLOCKS // 2 :]

    def ordered(self, halves, core):
        if self.chips == BLOCKS:
            return halves
        send, keep = halves
        x = jnp.concatenate([keep, send], axis=0).transpose(1, 0, 2, 3)
        x = x.reshape(x.shape[0], self.chips, -1, D).transpose(1, 0, 2, 3)
        x = jnp.take(x, self.owners(core), axis=0)
        return x[self.chips // 2 :], x[: self.chips // 2]

    def flat_join(self, x, got, mask, axis=1):
        upper = (self.index & mask) != 0
        return jnp.where(
            upper, jnp.concatenate([got, x], axis=axis), jnp.concatenate([x, got], axis=axis)
        )

    def halves(self, x, mask, dtype):
        half = x.shape[0] // 2
        upper = (self.index & mask) != 0
        keep = jnp.where(upper, x[half:], x[:half])
        send = jnp.where(upper, x[:half], x[half:])
        return keep, send.astype(dtype)


def shards(
    images,
    cotangent,
    counts,
    w_token_in,
    w_token_out,
    w_chan_in,
    w_chan_out,
    gains,
    row_states,
    col_states,
    gain_states,
):
    links = Links(D * DC // w_chan_in.shape[0], counts)
    size, chips, core = links.size, links.chips, links.core
    run, land, swap, cross = links.run, links.land, links.swap, links.cross
    count = images.shape[0]
    rows = count * PATCHES
    table = links.table(core)
    steps = [1 << at for at in range(size.bit_length() - 1)]
    x = images.transpose(1, 0, 2).reshape(rows, D)
    cot = cotangent.transpose(1, 0, 2).reshape(rows, D)
    masters = (w_token_in, w_token_out, w_chan_in, w_chan_out)

    rows3 = D // size
    rows4 = DC // size
    sub = rows4 // UNITS
    length = w_token_in.shape[0]
    w12 = jnp.stack([w_token_in, w_token_out])
    place = jnp.stack([core, links.index])
    edges_r = (0, PATCHES, PATCHES + HIDDEN, PATCHES + HIDDEN + D, PATCHES + HIDDEN + D + DC)
    edges_c = (0, HIDDEN, HIDDEN + PATCHES, HIDDEN + PATCHES + DC, HIDDEN + PATCHES + DC + D)

    def old_statistics(rows, cols):
        rows = [rows[edges_r[k] : edges_r[k + 1]] for k in range(4)]
        cols = [cols[edges_c[k] : edges_c[k + 1]] for k in range(4)]
        rows[2:] = rows[2].reshape(1, D), rows[3].reshape(4, D)
        wide = cols[2].reshape(chips, 2, UNITS, sub).transpose(1, 2, 0, 3).reshape(2 * UNITS, F)
        cols[2:] = wide, cols[3].reshape(1, D)
        rows[:2] = (jnp.pad(row, (0, D - row.shape[0]))[None] for row in rows[:2])
        cols[:2] = (col[None] for col in cols[:2])
        return rows, cols

    def blocks(lo, hi):
        return links.as_blocks((lo, hi), core)

    token = jnp.concatenate([w_token_in, w_token_out]).astype(BF)[None]
    high = steps[3:]
    token_got = swap(token, high[0])
    (mine, theirs, local4, wide3, wide4, weight_squares), token_got = run(
        prepare, place, w12, w_chan_in, w_chan_out, landing=token_got
    )
    token = links.flat_join(token, token_got, high[0], 0)
    got = swap(theirs, 1)
    for mask in high[1:-1]:
        token = links.flat_join(token, land(swap(token, mask)), mask, 0)
    token_got = swap(token, high[-1])
    dout, (token_got, got) = run(kept_cotangent, counts, cot, landing=(token_got, got))
    token = links.flat_join(token, token_got, high[-1], 0)
    local3 = jnp.where(
        core == 0, jnp.concatenate([mine, got], axis=1), jnp.concatenate([got, mine], axis=1)
    )[:, None]
    a0 = links.gather_high(local3[0])
    token_got = swap(token, 1)
    y1, token_got = run(first_norm, x, gains, landing=token_got)
    token = links.flat_join(token, token_got, 1, 1)
    for mask in steps[1:3]:
        token = links.flat_join(token, land(swap(token, mask)), mask, 1)
    token = token.reshape(size, 2, length)
    a0 = links.join(a0)
    a0_got = cross(a0, False)
    other_dout = swap(dout, 1)
    w1 = token[:, 0].reshape(PATCHES, HIDDEN)
    w2 = token[:, 1].reshape(HIDDEN, PATCHES)
    (old_rows, old_cols, w1, w2), a0_got = run(
        lambda r, c, *w: (*old_statistics(r, c), *w), row_states, col_states, w1, w2, landing=a0_got
    )
    a0 = run(join_two, a0, a0_got)
    a0_hi = cross(a0, True)
    a1 = links.gather_high(local3[1])
    (x1, y2), (a0_hi, a1) = run(token_forward, x, y1, w1, w2, gains, landing=(a0_hi, a1))

    other_y2 = swap(y2, 1)
    a1 = links.join(a1)
    a1_got = cross(a1, False)
    (act_a0, slope_a0, w3_0), (other_y2, other_dout, a1_got) = run(
        channel_forward, table, *blocks(a0, a0_hi), y2, landing=(other_y2, other_dout, a1_got)
    )
    a1 = run(join_two, a1, a1_got)
    a1_hi = cross(a1, True)
    b0 = links.gather_high(local4[0][None])
    (act_b0, slope_b0, *c0), (a1_hi, b0) = run(
        channel_forward_grad, table, w3_0, other_y2, act_a0, dout, other_dout, landing=(a1_hi, b0)
    )
    b0 = links.join(b0)
    b0_got = cross(b0, False)
    (act_a1, slope_a1, w3_1), b0_got = run(
        channel_forward, table, *blocks(a1, a1_hi), y2, landing=b0_got
    )
    b0 = run(join_two, b0, b0_got)
    b0_hi = cross(b0, True)
    b1 = links.gather_high(local4[1][None])
    (act_b1, slope_b1, *c), (b0_hi, b1) = run(
        channel_forward_grad,
        table,
        w3_1,
        other_y2,
        act_a1,
        dout,
        other_dout,
        *c0,
        landing=(b0_hi, b1),
    )

    b1 = links.join(b1)
    b1_got = cross(b1, False)
    (dc_a0, dc_b0, w4_0), b1_got = run(
        channel_backward,
        table,
        *blocks(b0, b0_hi),
        dout,
        other_dout,
        slope_a0,
        slope_b0,
        landing=b1_got,
    )
    b1 = run(join_two, b1, b1_got)
    b1_hi = cross(b1, True)
    d0, b1_hi = run(channel_backward_grad, table, y2, other_y2, dc_a0, dc_b0, landing=b1_hi)
    c_send, c_keep = links.ordered(c, core)
    c_got = cross(c_send, True)
    dc_a1, dc_b1, w4_1 = run(
        channel_backward, table, *blocks(b1, b1_hi), dout, other_dout, slope_a1, slope_b1
    )
    d, c_got = run(
        channel_backward_grad, table, y2, other_y2, dc_a1, dc_b1, *d0, landing=c_got
    )
    d_send, d_keep = links.ordered(d, core)
    d_got = cross(d_send, True)
    c_keep, c_send = run(fold_two, c_keep, c_got)
    c_got = cross(c_send, False)
    dy2_other = run(
        functools.partial(partial_product, "partial_back", NT), (dc_b0, dc_b1), (w3_0, w3_1)
    )
    dy2_got = swap(dy2_other, 1)
    out_other, (dy2_got, c_got) = run(
        functools.partial(partial_product, "partial_out", NN),
        (act_b0, act_b1),
        (w4_0, w4_1),
        landing=(dy2_got, c_got),
    )
    c_keep, c_got = links.scatter_high(c_keep, [c_got])

    (dx1, dg2), (d_got, c_got) = run(
        second_back,
        (dc_a0, dc_a1),
        (w3_0, w3_1),
        dy2_got,
        dout,
        x1,
        gains,
        landing=(d_got, c_got),
    )
    d_keep, d_send = run(fold_two, d_keep, d_got)
    d_got = cross(d_send, False)
    out_got = swap(out_other, 1)
    shapes = ((PATCHES, HIDDEN), (HIDDEN, PATCHES))
    touched = [covered(columns, length, size) for _, columns in shapes]
    (da, keep, send), (d_got, out_got) = run(
        functools.partial(token_back, size, touched, length),
        place,
        dx1,
        y1,
        w1,
        w2,
        landing=(d_got, out_got),
    )
    d_keep, d_got = links.scatter_high(d_keep, [d_got])
    got = swap(send, steps[-1])
    (grad_input, dg1), (got, d_got) = run(
        input_gradient, x, da, dx1, w1, gains, landing=(got, d_got)
    )
    token_grads = keep + got.astype(F32)
    keep, send = links.halves(token_grads, steps[-2], BF)
    got = swap(send, steps[-2])
    mine, theirs = run(lambda p, *parts: end_sums(p, parts), place, d_keep, *d_got)
    theirs_got = swap(theirs, 1)
    block_out, (got, theirs_got) = run(
        block_output,
        counts,
        (act_a0, act_a1),
        (w4_0, w4_1),
        out_got,
        x1,
        landing=(got, theirs_got),
    )
    token_grads = keep + got.astype(F32)
    grad4 = links.scatter_end(c_keep, c_got).reshape(rows4, D)
    for mask in reversed(steps[:-2]):
        keep, send = links.halves(token_grads, mask, F32)
        token_grads = keep + land(swap(send, mask))
    token_grads = (token_grads[0, : touched[0]], token_grads[0, touched[0] :, :PATCHES])
    got = theirs_got
    grad_input = grad_input.reshape(PATCHES, count, D).transpose(1, 0, 2)
    block_out = block_out.reshape(PATCHES, count, D).transpose(1, 0, 2)

    summed, flat3, flat4, row3, row4 = run(
        functools.partial(statistics, sub, length),
        place,
        mine,
        got,
        grad4,
        old_rows[2],
        old_rows[3],
        dg1,
        dg2,
        weight_squares,
        *token_grads,
        *old_rows[:2],
    )

    def own_piece(x):
        columns = x.shape[1]
        start = links.index * length - links.index * length // columns * columns
        return lax.dynamic_slice_in_dim(x.reshape(-1), start, length)

    flat12 = None
    for mask in steps:
        got_sums = swap(summed, mask)
        if flat12 is None:
            flat12, got_sums = run(
                lambda *g: [own_piece(x) for x in g], *token_grads, landing=got_sums
            )
        else:
            got_sums = land(got_sums)
        summed = summed + got_sums
    new3, new4, col3, col4, sizes, new1, new2, col1, col2 = update(
        sub,
        length,
        place,
        summed,
        mine,
        got,
        grad4,
        wide3,
        wide4,
        row3,
        row4,
        old_cols[2],
        old_cols[3],
        *token_grads,
        *old_cols[:2],
    )
    rows_out = [summed[ROW1, :PATCHES], summed[ROW2, :HIDDEN], summed[ROW3]]
    rows_out.append(summed[ROW4 : ROW4 + 4].reshape(-1))
    cols_out = [x.reshape(-1) for x in (col1, col2, col3, col4)]
    update_sizes = [sizes[:4, 0]]
    new_weights = [
        w_token_in - own_piece(new1),
        w_token_out - own_piece(new2),
        new3.reshape(-1),
        new4.reshape(-1),
    ]
    token_grads = flat12
    dg1, dg2 = summed[GAINS], summed[GAINS + 1]

    gain_grads = jnp.stack([dg1, dg2])
    gain_stats = DECAY * gain_states + (1.0 - DECAY) * (gain_grads * gain_grads + 1e-30)
    gain_update = gain_grads * lax.rsqrt(gain_stats)
    gain_sizes = jnp.sqrt(jnp.mean(gain_update * gain_update, axis=1))
    gain_update = gain_update / jnp.maximum(1.0, gain_sizes / CLIP)[:, None]
    gain_scale = jnp.sqrt(jnp.mean(gains * gains, axis=1) + 1e-06)
    new_gains = gains - STEP * gain_scale[:, None] * gain_update
    update_rms = jnp.concatenate(update_sizes + [gain_sizes])
    return (
        block_out,
        grad_input,
        token_grads[0],
        token_grads[1],
        flat3.reshape(-1),
        flat4.reshape(-1),
        new_weights[0],
        new_weights[1],
        new_weights[2],
        new_weights[3],
        gain_grads,
        gain_stats,
        new_gains,
        jnp.concatenate(rows_out),
        jnp.concatenate(cols_out),
        update_rms,
    )


def solution(mesh):
    split = P("fsdp")
    images = P("fsdp", None, None)
    in_specs = (images, images) + (split,) * 5 + (P(),) * 4
    out_specs = (images, images) + (split,) * 8 + (P(),) * 6
    return jax.shard_map(
        shards, mesh=mesh, in_specs=in_specs, out_specs=out_specs, check_vma=False
    )
```

```python
import functools

import jax
import jax.numpy as jnp
from jax import lax
from jax.experimental import pallas as pl
from jax.experimental.pallas import tpu as pltpu
from jax.sharding import PartitionSpec as P

D = 768
PATCHES = 196
HIDDEN = 384
DC = 3072
UNITS = 2
F = DC // (2 * UNITS)
BLOCKS = 16
TILE = D // BLOCKS

PACE = 1.0

DECAY = 0.5
CLIP = 0.5
STEP = 1.0

NN = ((1,), (0,))
NT = ((1,), (1,))
TN = ((0,), (0,))

GELU_A = 0.7978845608028654
GELU_B = 0.7978845608028654 * 0.044715

BF = jnp.bfloat16
F32 = jnp.float32


def dot(a, b, dims):
    return lax.dot_general(a, b, (dims, ((), ())), preferred_element_type=F32)


def gelu_pair(v):
    square = v * v
    half = 0.5 + 0.5 * jnp.tanh(v * (GELU_A + GELU_B * square))
    value = v * half
    return value, half + (value - value * half) * (2.0 * GELU_A + (6.0 * GELU_B) * square)


def normalize(values):
    centred = values - jnp.mean(values, axis=-1, keepdims=True)
    spread = jnp.mean(centred * centred, axis=-1, keepdims=True)
    inverse = lax.rsqrt(spread + 1e-06)
    return centred * inverse, inverse


def norm_back(grad, normed, inverse):
    first = jnp.mean(grad, axis=-1, keepdims=True)
    second = jnp.mean(grad * normed, axis=-1, keepdims=True)
    return inverse * (grad - first - normed * second)


ANY = pl.BlockSpec(memory_space=pl.ANY)
SMEM = pl.BlockSpec(memory_space=pltpu.SMEM)
VMEM = pl.BlockSpec(memory_space=pltpu.VMEM)


def struct(shape, dtype):
    return jax.ShapeDtypeStruct(shape, dtype)


def held(shape, dtype):
    return pltpu.VMEM(shape, dtype)


def hbm(shape, dtype):
    return pltpu.HBM(shape, dtype)


def call(kernel, name, inputs, in_specs, outs, scratch=(), mib=16, grid=(), out_specs=None, micros=1.0):
    return pl.pallas_call(
        kernel,
        grid=grid,
        in_specs=in_specs,
        out_specs=out_specs or [VMEM] * len(outs),
        out_shape=outs,
        scratch_shapes=scratch,
        compiler_params=pltpu.CompilerParams(vmem_limit_bytes=mib * 2**20),
        cost_estimate=pl.CostEstimate(
            flops=int(micros * 1.15e9 * PACE), bytes_accessed=1024, transcendentals=0
        ),
        name=name,
    )(*inputs)


def tiled(rows, size, body, carry=0, unroll=1):
    def step(at, carry):
        return body(pl.ds(pl.multiple_of(at * size, 16), size), at * size, carry)

    return lax.fori_loop(0, rows // size, step, carry, unroll=unroll)


LANES = 128
GROUP = D // LANES


def split(rows, dtype=F32):
    return held((GROUP, rows, LANES), dtype)


def put_rows(ref, here, value):
    for at in range(GROUP):
        ref[at, here, :] = value[:, at * LANES : (at + 1) * LANES]


def get_rows(ref, here):
    return jnp.concatenate([ref[at, here, :] for at in range(GROUP)], axis=1)


def of_image(at, count):
    return pl.ds(at, PATCHES, stride=count)


def lane_block(rows):
    return pl.BlockSpec((rows, D), lambda i: (0, i))


def row_block(rows, columns=D):
    return pl.BlockSpec((rows, columns), lambda i: (i, 0))


def used(counts, first, size, count):
    row = lax.broadcasted_iota(jnp.int32, (size, 1), 0) + first
    return lax.rem(row, count) < counts[0]


def column_sums(value):
    return jnp.sum(value.reshape(-1, 8, D), axis=0)


def from_hbm(x):
    return pltpu.with_memory_space_constraint(x, pltpu.HBM)


def prepare_kernel(place, w12, w3, w4, mine, theirs, local4, wide3, wide4, squares):
    rows3, rows4 = wide3.shape[1], wide4.shape[0]
    sub = rows4 // UNITS
    first = place[0] == 0
    per3, per4 = DC // LANES, D // LANES
    full = jnp.concatenate([w3[pl.ds(j, rows3, stride=per3), :] for j in range(per3)], axis=1)
    parts = []
    for at in range(2 * UNITS):
        step = 2 * UNITS * sub
        part = jnp.concatenate(
            [full[:, m * step + at * sub : m * step + (at + 1) * sub] for m in range(DC // step)],
            axis=1,
        )
        wide3[at] = part
        parts.append(part.astype(BF))
    for u in range(UNITS):
        mine[u] = jnp.where(first, parts[u], parts[UNITS + u])
        theirs[u] = jnp.where(first, parts[UNITS + u], parts[u])
    four = jnp.concatenate([w4[pl.ds(j, rows4, stride=per4), :] for j in range(per4)], axis=1)
    wide4[...] = four
    for u in range(UNITS):
        local4[u] = four[u * sub : (u + 1) * sub, :].astype(BF)
    squares[...] = jnp.zeros_like(squares)
    for at, value in enumerate((w12[0:1, :], w12[1:2, :], full, four)):
        total = jnp.sum(jnp.sum(value * value, axis=1, keepdims=True), axis=0, keepdims=True)
        squares[at : at + 1, :] = jnp.broadcast_to(total, (1, LANES))


def prepare(place, w12, w3, w4):
    rows3, rows4 = w3.size // DC, w4.size // D
    return call(
        prepare_kernel,
        "prepare",
        [place, w12, w3.reshape(-1, LANES), w4.reshape(-1, LANES)],
        [SMEM, VMEM, VMEM, VMEM],
        [
            struct((UNITS, rows3, F), BF),
            struct((UNITS, rows3, F), BF),
            struct((UNITS, rows4 // UNITS, D), BF),
            hbm((2 * UNITS, rows3, F), F32),
            hbm((rows4, D), F32),
            hbm((8, LANES), F32),
        ],
        micros=8,
        mib=6,
    )


def keep_kernel(count, counts, cot, dout):
    size = cot.shape[0]
    keep = used(counts, pl.program_id(0) * size, size, count)
    dout[...] = jnp.where(keep, cot[...].astype(F32), 0.0).astype(BF)


def kept_cotangent(counts, cot):
    rows = cot.shape[0]
    size = rows // 2
    return call(
        functools.partial(keep_kernel, rows // PATCHES),
        "kept_cotangent",
        [counts, from_hbm(cot)],
        [SMEM, row_block(size)],
        [held((rows, D), BF)],
        micros=3,
        grid=(2,),
        out_specs=[row_block(size)],
    )[0]


def first_kernel(count, x, gains, y1, scratch):
    rows = x.shape[0]

    def body(here, first, carry):
        normed, _ = normalize(x[here, :].astype(F32))
        put_rows(scratch, here, normed * gains[0:1, :])
        return carry

    tiled(rows, rows // 7, body)
    for at in range(count):
        y1[:, at * D : (at + 1) * D] = get_rows(scratch, of_image(at, count)).astype(BF)


def first_norm(x, gains):
    rows = x.shape[0]
    count = rows // PATCHES
    return call(
        functools.partial(first_kernel, count),
        "first_norm",
        [x, gains],
        [VMEM, VMEM],
        [held((PATCHES, count * D), BF)],
        [split(rows)],
        micros=4,
        mib=10,
    )[0]


def token_kernel(count, x, y1, w1, w2, gains, away, y2, scratch, x1, sems):
    rows = x.shape[0]

    def image(at, carry):
        lanes = pl.ds(pl.multiple_of(at * D, LANES), D)
        pre = dot(w1[...], y1[:, lanes], TN)
        act = pre * (0.5 + 0.5 * jnp.tanh(pre * (GELU_A + GELU_B * (pre * pre))))
        put_rows(scratch, of_image(at, count), dot(w2[...], act.astype(BF), TN))
        return carry

    lax.fori_loop(0, count, image, 0, unroll=4)
    size = rows // 7

    def leave(at):
        here = pl.ds(pl.multiple_of(at * size, 16), size)
        return pltpu.make_async_copy(x1.at[here, :], away.at[here, :], sems.at[at])

    def body(here, first, carry):
        mixed = x[here, :].astype(F32) + get_rows(scratch, here)
        x1[here, :] = mixed
        leave(first // size).start()
        normed, _ = normalize(mixed)
        y2[here, :] = (normed * gains[1:2, :]).astype(BF)
        return carry

    tiled(rows, size, body)
    for at in range(7):
        leave(at).wait()


def token_forward(x, y1, w1, w2, gains):
    rows = x.shape[0]
    count = rows // PATCHES
    return call(
        functools.partial(token_kernel, count),
        "token_forward",
        [x, y1, w1, w2, gains],
        [VMEM] * 5,
        [hbm((rows, D), F32), held((rows, D), BF)],
        [split(rows), pltpu.VMEM((rows, D), F32), pltpu.SemaphoreType.DMA((7,))],
        micros=8,
        mib=16,
        out_specs=[ANY, VMEM],
    )


def load_unit(table, lo, hi, dest, sems):
    copies = []
    for at in range(BLOCKS):
        source = (lo, hi)[at * 2 // BLOCKS].at[at % (BLOCKS // 2)]
        row = pl.multiple_of(table[at] * TILE, 16)
        copies.append(pltpu.make_async_copy(source, dest.at[pl.ds(row, TILE), :], sems.at[at]))
    for copy in copies:
        copy.start()
    return copies


def store_blocks(table, send, keep, total):
    half = BLOCKS // 2
    unit = send.shape[1] - 1
    for at in range(BLOCKS):
        block = total[at * TILE : (at + 1) * TILE, :]
        place = table[BLOCKS + at]

        @pl.when(place < half)
        def _():
            keep[place, unit] = block

        @pl.when(place >= half)
        def _():
            send[place - half, unit] = block


def rows_forward(y2, weight, act, slope):
    def body(here, first, carry):
        value, der = gelu_pair(dot(y2[here, :], weight[...], NN))
        act[here, :] = value.astype(BF)
        slope[here, :] = der.astype(BF)
        return carry

    tiled(y2.shape[0], y2.shape[0] // 7, body, unroll=7)


def forward_kernel(table, lo, hi, y2, act, slope, weight, sems):
    for copy in load_unit(table, lo, hi, weight, sems):
        copy.wait()
    rows_forward(y2, weight, act, slope)


def channel_forward(table, lo, hi, y2):
    acts = held((y2.shape[0], F), BF)
    return call(
        forward_kernel,
        "channel_forward",
        [table, lo, hi, y2],
        [SMEM, ANY, ANY, VMEM],
        [acts, acts, held((D, F), BF)],
        [pltpu.SemaphoreType.DMA((BLOCKS,))],
        micros=7,
        mib=9,
    )


def join_before(before, send, keep):
    if before:
        send[:, 0] = before[0][:, 0]
        keep[:, 0] = before[1][:, 0]


def forward_grad_kernel(table, weight, y2, act0, dout0, dout1, *refs):
    *before, slope, send, keep, away0, away, act, leaving = refs
    copies = [pltpu.make_async_copy(act0, away0, leaving.at[0])]
    copies[0].start()
    rows_forward(y2, weight, act, slope)
    copies.append(pltpu.make_async_copy(act, away, leaving.at[1]))
    copies[1].start()
    join_before(before, send, keep)
    total = dot(act0[...], dout0[...], TN) + dot(act[...], dout1[...], TN)
    store_blocks(table, send, keep, total.astype(BF))
    for copy in copies:
        copy.wait()


def channel_forward_grad(table, weight, y2, act0, dout0, dout1, *before):
    acts = held((y2.shape[0], F), BF)
    half = held((BLOCKS // 2, 1 + len(before) // 2, TILE, D), BF)
    return call(
        forward_grad_kernel,
        "channel_forward_grad",
        [table, weight, y2, act0, dout0, dout1, *before],
        [SMEM] + [VMEM] * (5 + len(before)),
        [acts, half, half, hbm(acts.shape, BF), hbm(acts.shape, BF)],
        [pltpu.VMEM(acts.shape, BF), pltpu.SemaphoreType.DMA((2,))],
        out_specs=[VMEM] * 3 + [ANY] * 2,
        micros=11,
        mib=17,
    )


def backward_kernel(table, lo, hi, dout0, dout1, slope0, slope1, dc0, dc1, weight, sems):
    for copy in load_unit(table, lo, hi, weight, sems):
        copy.wait()
    for dout, slope, dc in ((dout0, slope0, dc0), (dout1, slope1, dc1)):

        def body(here, first, carry, dout=dout, slope=slope, dc=dc):
            value = slope[here, :].astype(F32) * dot(dout[here, :], weight[...], NT)
            dc[here, :] = value.astype(BF)
            return carry

        tiled(dout.shape[0], dout.shape[0] // 2, body)


def channel_backward(table, lo, hi, dout0, dout1, slope0, slope1):
    acts = held((dout0.shape[0], F), BF)
    return call(
        backward_kernel,
        "channel_backward",
        [table, lo, hi, dout0, dout1, slope0, slope1],
        [SMEM, ANY, ANY] + [VMEM] * 4,
        [acts, acts, held((F, D), BF)],
        [pltpu.SemaphoreType.DMA((BLOCKS,))],
        micros=8,
        mib=10,
    )


def backward_grad_kernel(table, y0, y1, dc0, dc1, *refs):
    *before, send, keep = refs
    total = dot(y0[...], dc0[...], TN) + dot(y1[...], dc1[...], TN)
    join_before(before, send, keep)
    store_blocks(table, send, keep, total.astype(BF))


def channel_backward_grad(table, y0, y1, dc0, dc1, *before):
    half = held((BLOCKS // 2, 1 + len(before) // 2, TILE, D), BF)
    return call(
        backward_grad_kernel,
        "channel_backward_grad",
        [table, y0, y1, dc0, dc1, *before],
        [SMEM] + [VMEM] * (4 + len(before)),
        [half, half],
        micros=6,
        mib=13,
    )


def partial_kernel(d0, d1, w0, w1, out):
    def body(here, first, carry):
        total = dot(d0[here, :], w0[...], NT) + dot(d1[here, :], w1[...], NT)
        out[here, :] = total.astype(BF)
        return carry

    tiled(d0.shape[0], d0.shape[0] // 2, body)


def partial_back(dcs, weights):
    out = held((dcs[0].shape[0], D), BF)
    return call(
        partial_kernel, "partial_back", [*dcs, *weights], [VMEM] * 4, [out], mib=10, micros=5
    )[0]


def partial_out_kernel(a0, a1, w0, w1, y1, wt, out, h, slope):
    total = dot(a0[...], w0[...], NN) + dot(a1[...], w1[...], NN)
    out[...] = total.astype(BF)
    step = pl.program_id(0)
    count = y1.shape[1] // D // 2
    for at in range(count):
        lanes = pl.ds(pl.multiple_of((step * count + at) * D, LANES), D)
        act, der = gelu_pair(dot(wt[...], y1[:, lanes], TN))
        h[:, lanes] = act.astype(BF)
        slope[:, lanes] = der.astype(BF)


def partial_out(acts, weights, y1, wt):
    rows = acts[0].shape[0]
    size = rows // 2
    out = held((HIDDEN, y1.shape[1]), BF)
    return call(
        partial_out_kernel,
        "partial_out",
        [*map(from_hbm, acts), *weights, y1, wt],
        [row_block(size, F)] * 2 + [VMEM] * 4,
        [held((rows, D), BF), out, out],
        micros=10,
        mib=13,
        grid=(2,),
        out_specs=[row_block(size), VMEM, VMEM],
    )


def second_kernel(d0, d1, w0, w1, got, dout, x1, gains, dx1, dg2):
    def body(here, first, carry):
        grad = dot(d0[here, :], w0[...], NT) + dot(d1[here, :], w1[...], NT)
        grad += got[here, :].astype(F32)
        normed, inverse = normalize(x1[here, :])
        total = dout[here, :].astype(F32) + norm_back(grad * gains[1:2, :], normed, inverse)
        put_rows(dx1, here, total)
        return carry + column_sums(grad * normed)

    rows = x1.shape[0]
    sums = tiled(rows, rows // 7, body, jnp.zeros((8, D), F32))
    dg2[...] = jnp.sum(sums, axis=0, keepdims=True)


def second_back(dcs, weights, got, dout, x1, gains):
    rows = x1.shape[0]
    return call(
        second_kernel,
        "second_back",
        [*dcs, *weights, got, dout, x1, gains],
        [VMEM] * 8,
        [split(rows), held((1, D), F32)],
        micros=9,
        mib=10,
    )


def mirrored(value, size):
    out = 0
    for bit in range(size.bit_length() - 1):
        out = out * 2 + (value >> bit) % 2
    return out


def token_back_kernel(size, touched, length, place, dx1, h, slope, y1, w2, da, keep, send, g1, g2, every):
    count = dx1.shape[1] // PATCHES
    g1[...] = jnp.zeros_like(g1)
    g2[...] = jnp.zeros_like(g2)

    def body(at, carry):
        lanes = pl.ds(pl.multiple_of(at * D, LANES), D)
        low = get_rows(dx1, of_image(at, count)).astype(BF)
        back = (slope[:, lanes].astype(F32) * dot(w2[...], low, NN)).astype(BF)
        da[:, lanes] = back
        g1[0:PATCHES, :] += dot(y1[:, lanes], back, NT)
        g2[0:HIDDEN, :] += dot(h[:, lanes], low, NT)
        return carry

    lax.fori_loop(0, count, body, 0, unroll=4)
    for at in range(size):
        spot = mirrored(at, size)
        first = at * length // HIDDEN
        every[spot, 0 : touched[0], :] = g1[first : first + touched[0], :]
        first = at * length // PATCHES
        every[spot, touched[0] :, 0:PATCHES] = g2[first : first + touched[1], :]
        every[spot, touched[0] :, PATCHES:] = jnp.zeros((touched[1], HIDDEN - PATCHES), F32)
    half = size // 2
    keep[...] = every[pl.ds(place[0] * half, half)]
    send[...] = every[pl.ds((1 - place[0]) * half, half)]


def token_back(size, touched, length, place, dx1, h, slope, y1, w2):
    count = dx1.shape[1] // PATCHES
    rows = sum(touched)
    return call(
        functools.partial(token_back_kernel, size, touched, length),
        "token_back",
        [place, dx1, h, slope, y1, w2],
        [SMEM] + [VMEM] * 5,
        [
            held((HIDDEN, count * D), BF),
            held((size // 2, rows, HIDDEN), F32),
            held((size // 2, rows, HIDDEN), F32),
        ],
        [
            pltpu.VMEM((PATCHES + touched[0], HIDDEN), F32),
            pltpu.VMEM((HIDDEN + touched[1], PATCHES), F32),
            pltpu.VMEM((size, rows, HIDDEN), F32),
        ],
        micros=10,
        mib=12,
    )


def input_product_kernel(da, w1, out):
    count = da.shape[1] // D

    def body(at, carry):
        lanes = pl.ds(pl.multiple_of(at * D, LANES), D)
        put_rows(out, of_image(at, count), dot(w1[...], da[:, lanes], NN))
        return carry

    lax.fori_loop(0, count, body, 0, unroll=4)


def input_product(da, w1):
    rows = da.shape[1] // D * PATCHES
    return call(
        input_product_kernel, "input_product", [da, w1], [VMEM] * 2, [split(rows)], mib=6, micros=4
    )[0]


def input_kernel(x, dy1, dx1, gains, out, dg1):
    step = pl.program_id(0)
    size = out.shape[0]

    @pl.when(step == 0)
    def _():
        dg1[...] = jnp.zeros_like(dg1)

    here = pl.ds(pl.multiple_of(step * size, 8), size)
    grad = get_rows(dy1, here)
    normed, inverse = normalize(x[...].astype(F32))
    dg1[...] += jnp.sum(column_sums(grad * normed), axis=0, keepdims=True)
    out[...] = get_rows(dx1, here) + norm_back(grad * gains[0:1, :], normed, inverse)


def input_gradient(x, dy1, dx1, gains):
    rows = x.shape[0]
    size = rows // 7
    return call(
        input_kernel,
        "input_gradient",
        [from_hbm(x), dy1, dx1, gains],
        [row_block(size), VMEM, VMEM, VMEM],
        [hbm((rows, D), F32), held((1, D), F32)],
        micros=6,
        mib=12,
        grid=(7,),
        out_specs=[row_block(size), VMEM],
    )


def out_kernel(count, counts, a0, a1, w0, w1, got, x1, out):
    size = out.shape[0]
    first = pl.program_id(0) * size
    here = pl.ds(pl.multiple_of(first, 16), size)
    total = dot(a0[...], w0[...], NN) + dot(a1[...], w1[...], NN)
    total += got[here, :].astype(F32) + x1[here, :]
    out[...] = jnp.where(used(counts, first, size, count), total, 0.0)


def block_output(counts, acts, weights, got, x1):
    rows = x1.shape[0]
    size = rows // 2
    return call(
        functools.partial(out_kernel, rows // PATCHES),
        "block_output",
        [counts, *map(from_hbm, acts), *weights, got, x1],
        [SMEM] + [row_block(size, F)] * 2 + [VMEM] * 4,
        [hbm((rows, D), F32)],
        micros=9,
        mib=22,
        grid=(2,),
        out_specs=[row_block(size)],
    )[0]


def join_two(a, b):
    return join([a, b])


def fold_two(a, b):
    return fold([a, b], 2)


def join_kernel(*refs):
    rows = refs[0].shape[0]
    for at, ref in enumerate(refs[:-1]):
        refs[-1][at * rows : (at + 1) * rows, :] = ref[...]


def join(parts):
    shape = parts[0].shape
    flat = [x.reshape(-1, D) for x in parts]
    out = held((len(parts) * flat[0].shape[0], D), BF)
    x = call(join_kernel, "join", flat, [VMEM] * len(parts), [out], mib=8)[0]
    return x.reshape((len(parts) * shape[0],) + shape[1:])


def fold_kernel(parts, splits, *refs):
    rows = refs[0].shape[0] // splits
    for at in range(splits):
        here = slice(at * rows, (at + 1) * rows)
        total = refs[0][here, :].astype(F32)
        for part in refs[1:parts]:
            total = total + part[here, :].astype(F32)
        refs[parts + at][...] = total.astype(refs[parts + at].dtype)


def fold(parts, splits):
    shape = parts[0].shape
    lead = shape[0] // splits
    flat = [x.reshape(-1, D) for x in parts]
    rows = flat[0].shape[0] // splits
    dtypes = [F32 if lead == 1 else BF] + [BF] * (splits - 1)
    outs = call(
        functools.partial(fold_kernel, len(parts), splits),
        "fold",
        flat,
        [VMEM] * len(parts),
        [held((rows, D), dtype) for dtype in dtypes],
        mib=8,
    )
    return [x.reshape((lead,) + shape[1:]) for x in outs]


def end_kernel(place, *refs):
    *parts, mine, theirs = refs
    rows = mine.shape[1]
    first = place[0] == 0
    for unit in range(UNITS):
        total = parts[0][unit].astype(F32)
        for part in parts[1:]:
            total = total + part[unit].astype(F32)
        mine[unit] = jnp.where(first, total[:rows], total[rows:])
        theirs[unit] = jnp.where(first, total[rows:], total[:rows])


def end_sums(place, parts):
    parts = [x[0] for x in parts]
    out = held((UNITS, parts[0].shape[1] // 2, F), F32)
    return call(
        end_kernel,
        "end_sums",
        [place, *parts],
        [SMEM] + [VMEM] * len(parts),
        [out, out],
        mib=6,
    )


def in_order(place, mine, got):
    first = place[0] == 0
    own = [mine[u] for u in range(UNITS)]
    other = [got[u] for u in range(UNITS)]
    return [jnp.where(first, x, y) for x, y in zip(own + other, other + own)]


def natural(parts, sub):
    return jnp.concatenate(
        [part[:, m * sub : (m + 1) * sub] for m in range(F // sub) for part in parts], axis=1
    )


def put_flat(ref, value):
    per = value.shape[1] // LANES
    for j in range(per):
        ref[pl.ds(j, value.shape[0], stride=per), :] = value[:, j * LANES : (j + 1) * LANES]


STATS = 24
COL3, WEIGHTED3, COL4, WEIGHTED4, ROW3, ROW4, GAINS, SQUARES = 0, 4, 8, 9, 10, 11, 15, 17


def row_statistics(index, grad, squares, old, vec, start):
    rows = grad.shape[0]
    spots = old.shape[0]
    column = lax.broadcasted_iota(jnp.int32, (rows, D), 1)
    target = lax.broadcasted_iota(jnp.int32, (rows, D), 0) + index * rows
    here = [column + spot * D == target for spot in range(spots)]
    before = sum(
        jnp.sum(jnp.where(mask, old[spot : spot + 1, :], 0.0), axis=1, keepdims=True)
        for spot, mask in enumerate(here)
    )
    mean = squares / (grad.shape[1]) + 1e-30
    row = DECAY * before + (1.0 - DECAY) * mean
    for spot, mask in enumerate(here):
        vec[start + spot : start + spot + 1, :] = jnp.sum(
            jnp.where(mask, row, 0.0), axis=0, keepdims=True
        )
    return row


ROW1, ROW2, COL1, WEIGHTED1, COL2, WEIGHTED2 = 18, 19, 20, 21, 22, 23


def covered(columns, length, size):
    return max((at * length + length - 1) // columns - at * length // columns + 1 for at in range(size))


def in_piece(index, length, rows, columns):
    first = index * length // columns
    row = lax.broadcasted_iota(jnp.int32, (rows, columns), 0) + first
    at = row * columns + lax.broadcasted_iota(jnp.int32, (rows, columns), 1)
    return first, (at >= index * length) & (at < (index + 1) * length)


def spots(first, rows):
    column = lax.broadcasted_iota(jnp.int32, (rows, D), 1)
    return column == lax.broadcasted_iota(jnp.int32, (rows, D), 0) + first


def token_statistics(index, length, grad, old, vec, row_at, col_at):
    rows, columns = grad.shape
    first, inside = in_piece(index, length, rows, columns)
    squares = grad * grad
    here = spots(first, rows)
    before = jnp.sum(jnp.where(here, old, 0.0), axis=1, keepdims=True)
    mean = jnp.sum(squares, axis=1, keepdims=True) / columns + 1e-30
    row = DECAY * before + (1.0 - DECAY) * mean
    mine = jnp.where(inside, squares, 0.0)
    vec[col_at : col_at + 1, 0:columns] = jnp.sum(mine, axis=0, keepdims=True)
    weighted = jnp.where(inside, squares / row, 0.0)
    vec[col_at + 1 : col_at + 2, 0:columns] = jnp.sum(weighted, axis=0, keepdims=True)
    starts = jnp.where(inside[:, 0:1] & here, row, 0.0)
    vec[row_at : row_at + 1, :] = jnp.sum(starts, axis=0, keepdims=True)


def stats_kernel(sub, length, place, mine, got, g4, old3, old4, dg1, dg2, sums, g1, g2, old1, old2, *refs):
    vec, flat3, flat4, row3, row4 = refs
    parts = in_order(place, mine, got)
    index = place[1]
    rows3 = parts[0].shape[0]
    squared = [x * x for x in parts]
    vec[...] = jnp.zeros_like(vec)
    total = sum(jnp.sum(x, axis=1, keepdims=True) for x in squared)
    wide = jnp.concatenate(squared, axis=1)
    row = row_statistics(index, wide, total, old3, vec, ROW3)
    row3[...] = jnp.broadcast_to(row, (rows3, LANES))
    scale = 1.0 / row
    for at, x in enumerate(squared):
        vec[COL3 + at : COL3 + at + 1, :] = jnp.sum(x, axis=0, keepdims=True)
        vec[WEIGHTED3 + at : WEIGHTED3 + at + 1, :] = jnp.sum(x * scale, axis=0, keepdims=True)
    four = g4[...]
    square4 = four * four
    row = row_statistics(
        index, square4, jnp.sum(square4, axis=1, keepdims=True), old4, vec, ROW4
    )
    row4[...] = jnp.broadcast_to(row, (four.shape[0], LANES))
    vec[COL4 : COL4 + 1, :] = jnp.sum(square4, axis=0, keepdims=True)
    vec[WEIGHTED4 : WEIGHTED4 + 1, :] = jnp.sum(square4 * (1.0 / row), axis=0, keepdims=True)
    vec[GAINS : GAINS + 1, :] = dg1[...]
    vec[GAINS + 1 : GAINS + 2, :] = dg2[...]
    for at in range(4):
        vec[SQUARES : SQUARES + 1, at * LANES : (at + 1) * LANES] = sums[at : at + 1, :]
    token_statistics(index, length, g1[...], old1[...], vec, ROW1, COL1)
    token_statistics(index, length, g2[...], old2[...], vec, ROW2, COL2)
    put_flat(flat3, natural(parts, sub))
    put_flat(flat4, four)


def statistics(sub, length, *inputs):
    rows3, rows4 = inputs[1].shape[1], inputs[3].shape[0]
    return call(
        functools.partial(stats_kernel, sub, length),
        "statistics",
        list(inputs),
        [SMEM] + [VMEM] * (len(inputs) - 1),
        [
            struct((STATS, D), F32),
            struct((rows3 * DC // LANES, LANES), F32),
            struct((rows4 * D // LANES, LANES), F32),
            held((rows3, LANES), F32),
            held((rows4, LANES), F32),
        ],
        micros=2,
        mib=8,
    )


def lane_total(x):
    return jnp.sum(jnp.sum(x, axis=1, keepdims=True), axis=0, keepdims=True)


def token_update(index, length, which, grad, old, vec, row_at, col_at, new, col_out, sizes):
    rows, columns = grad.shape
    count = float(PATCHES * HIDDEN)
    every = PATCHES * HIDDEN // columns
    first, _ = in_piece(index, length, rows, columns)
    row = vec[row_at : row_at + 1, :]
    mean = lane_total(row) / every
    col = DECAY * old[...] + (1.0 - DECAY) * (vec[col_at : col_at + 1, 0:columns] / every + 1e-30)
    weighted = vec[col_at + 1 : col_at + 2, 0:columns]
    size = jnp.sqrt(lane_total(weighted / col) * mean / count)
    sizes[which : which + 1, :] = jnp.broadcast_to(size, (1, LANES))
    square = vec[SQUARES : SQUARES + 1, which * LANES : which * LANES + 1]
    scale = STEP * jnp.sqrt(square / count + 1e-06) / jnp.maximum(1.0, size / CLIP)
    here = spots(first, rows)
    left = jnp.sum(jnp.where(here, row, 0.0), axis=1, keepdims=True)
    known = lax.broadcasted_iota(jnp.int32, (rows, 1), 0) + first < every
    left = jnp.where(known, lax.rsqrt(jnp.where(known, left, 1.0) / mean), 0.0)
    new[...] = grad[...] * left * lax.rsqrt(col) * scale
    col_out[...] = col


def update_kernel(sub, length, place, vec, mine, got, g4, wide3, wide4, row3, row4, old3, old4, *refs):
    g1, g2, old1, old2, new3, new4, col3, col4, sizes, new1, new2, col1, col2 = refs
    parts = in_order(place, mine, got)
    count = float(D * DC)
    sizes[...] = jnp.zeros_like(sizes)
    token_update(place[1], length, 0, g1, old1, vec, ROW1, COL1, new1, col1, sizes)
    token_update(place[1], length, 1, g2, old2, vec, ROW2, COL2, new2, col2, sizes)
    for which in range(2):
        rows = vec[ROW3 : ROW3 + 1, :] if which == 0 else vec[ROW4 : ROW4 + 4, :]
        mean = lane_total(rows) / (D if which == 0 else DC)
        if which == 0:
            cols = DECAY * old3[...] + (1.0 - DECAY) * (vec[COL3 : COL3 + 4, :] / D + 1e-30)
            weighted = vec[WEIGHTED3 : WEIGHTED3 + 4, :]
        else:
            cols = DECAY * old4[...] + (1.0 - DECAY) * (vec[COL4 : COL4 + 1, :] / DC + 1e-30)
            weighted = vec[WEIGHTED4 : WEIGHTED4 + 1, :]
        size = jnp.sqrt(lane_total(weighted / cols) * mean / count)
        sizes[which + 2 : which + 3, :] = jnp.broadcast_to(size, (1, LANES))
        square = vec[SQUARES : SQUARES + 1, (which + 2) * LANES : (which + 2) * LANES + 1]
        scale = STEP * jnp.sqrt(square / count + 1e-06) / jnp.maximum(1.0, size / CLIP)
        if which == 0:
            left = lax.rsqrt(row3[:, 0:1] / mean) * scale
            right = lax.rsqrt(cols)
            new = [
                wide3[at] - parts[at] * left * right[at : at + 1, :] for at in range(2 * UNITS)
            ]
            put_flat(new3, natural(new, sub))
            col3[...] = natural([cols[at : at + 1, :] for at in range(2 * UNITS)], sub)
        else:
            left = lax.rsqrt(row4[:, 0:1] / mean) * scale
            put_flat(new4, wide4[...] - g4[...] * left * lax.rsqrt(cols))
            col4[...] = cols


def update(sub, length, *inputs):
    wide3, wide4 = inputs[5:7]
    g1, g2 = inputs[-4:-2]
    return call(
        functools.partial(update_kernel, sub, length),
        "update",
        list(inputs),
        [SMEM] + [VMEM] * (len(inputs) - 1),
        [
            struct((wide3.size // LANES, LANES), F32),
            struct((wide4.size // LANES, LANES), F32),
            struct((1, DC), F32),
            struct((1, D), F32),
            struct((8, LANES), F32),
            struct(g1.shape, F32),
            struct(g2.shape, F32),
            struct((1, HIDDEN), F32),
            struct((1, PATCHES), F32),
        ],
        micros=2,
        mib=8,
    )


class Links:
    def __init__(self, size, token):
        self.size = size
        self.chips = size // 2
        bits = self.chips.bit_length() - 1
        self.high = [1 << b for b in reversed(range(2, bits))]
        self.orders = (self.high + [1, 2], self.high + [2, 1])
        self.index = lax.axis_index("fsdp")
        self.core = self.index & 1
        self.chip = self.index >> 1
        self.token = token

    def tie(self, x):
        x, self.token = lax.optimization_barrier((x, self.token))
        return x

    land = tie

    def run(self, function, *inputs, landing=None):
        out = function(*self.tie(inputs))
        if landing is None:
            return self.tie(out)
        return self.tie((out, landing))

    def swap(self, x, mask):
        return lax.ppermute(self.tie(x), "fsdp", [(i, i ^ mask) for i in range(self.size)])

    def cross(self, x, last):
        masks = (2, 1) if last else (1, 2)
        pairs = [(i, i ^ (masks[i & 1] << 1)) for i in range(self.size)]
        return lax.ppermute(self.tie(x), "fsdp", pairs)

    def line(self, x, level):
        return self.swap(x, self.high[level] << 1)

    def line_gather(self, x):
        for mask in self.high[:-2]:
            x = self.run(join_two, x, self.land(self.swap(x, mask << 1)))
        return x

    def line_scatter(self, keep, send):
        for mask in reversed(self.high[1:-1]):
            keep, send = self.run(fold_two, keep, self.land(self.swap(send, mask << 1)))
        return keep, self.swap(send, self.high[0] << 1)

    def owners(self, core):
        place = jnp.arange(self.chips, dtype=jnp.int32)
        owner = jnp.full((self.chips,), self.chip, jnp.int32)
        for level in range(len(self.orders[0])):
            bit = (place >> level) & 1
            mask = jnp.where(core == 0, self.orders[0][level], self.orders[1][level])
            owner = owner ^ (bit * mask)
        return owner

    def places(self, core):
        relative = jnp.arange(self.chips, dtype=jnp.int32) ^ self.chip
        place = jnp.zeros_like(relative)
        for level in range(len(self.orders[0])):
            mask = jnp.where(core == 0, self.orders[0][level], self.orders[1][level])
            place = place | (((relative & mask) != 0).astype(jnp.int32) << level)
        return place

    def table(self, core):
        if self.chips == BLOCKS:
            return jnp.concatenate([self.owners(core), self.places(core)])
        order = jnp.arange(BLOCKS, dtype=jnp.int32)
        return jnp.concatenate([order, order])

    def scatter_end(self, own, received):
        return self.run(lambda *p: fold(p, 1), own, received)[0][0]

    def as_blocks(self, halves, core):
        if self.chips == BLOCKS:
            return halves
        x = jnp.take(jnp.concatenate(halves, axis=0), self.places(core), axis=0)
        x = x.reshape(BLOCKS, TILE, D)
        return x[: BLOCKS // 2], x[BLOCKS // 2 :]

    def ordered(self, halves, core):
        if self.chips == BLOCKS:
            return halves
        send, keep = halves
        x = jnp.concatenate([keep, send], axis=0).transpose(1, 0, 2, 3)
        x = x.reshape(x.shape[0], self.chips, -1, D).transpose(1, 0, 2, 3)
        x = jnp.take(x, self.owners(core), axis=0)
        return x[self.chips // 2 :], x[: self.chips // 2]

    def flat_join(self, x, got, mask, axis=1):
        upper = (self.index & mask) != 0
        return jnp.where(
            upper, jnp.concatenate([got, x], axis=axis), jnp.concatenate([x, got], axis=axis)
        )

    def halves(self, x, mask, dtype):
        half = x.shape[0] // 2
        upper = (self.index & mask) != 0
        keep = jnp.where(upper, x[half:], x[:half])
        send = jnp.where(upper, x[:half], x[half:])
        return keep, send.astype(dtype)


def shards(
    images,
    cotangent,
    counts,
    w_token_in,
    w_token_out,
    w_chan_in,
    w_chan_out,
    gains,
    row_states,
    col_states,
    gain_states,
):
    links = Links(D * DC // w_chan_in.shape[0], counts)
    size, chips, core = links.size, links.chips, links.core
    run, land, swap, cross = links.run, links.land, links.swap, links.cross
    count = images.shape[0]
    rows = count * PATCHES
    table = links.table(core)
    steps = [1 << at for at in range(size.bit_length() - 1)]
    x = images.transpose(1, 0, 2).reshape(rows, D)
    cot = cotangent.transpose(1, 0, 2).reshape(rows, D)
    masters = (w_token_in, w_token_out, w_chan_in, w_chan_out)

    rows3 = D // size
    rows4 = DC // size
    sub = rows4 // UNITS
    length = w_token_in.shape[0]
    w12 = jnp.stack([w_token_in, w_token_out])
    place = jnp.stack([core, links.index])
    edges_r = (0, PATCHES, PATCHES + HIDDEN, PATCHES + HIDDEN + D, PATCHES + HIDDEN + D + DC)
    edges_c = (0, HIDDEN, HIDDEN + PATCHES, HIDDEN + PATCHES + DC, HIDDEN + PATCHES + DC + D)

    def old_row_statistics(rows):
        rows = [rows[edges_r[k] : edges_r[k + 1]] for k in range(4)]
        rows[2:] = rows[2].reshape(1, D), rows[3].reshape(4, D)
        rows[:2] = (jnp.pad(row, (0, D - row.shape[0]))[None] for row in rows[:2])
        return rows

    def old_column_statistics(cols):
        cols = [cols[edges_c[k] : edges_c[k + 1]] for k in range(4)]
        wide = cols[2].reshape(chips, 2, UNITS, sub).transpose(1, 2, 0, 3).reshape(2 * UNITS, F)
        cols[2:] = wide, cols[3].reshape(1, D)
        cols[:2] = (col[None] for col in cols[:2])
        return cols

    def blocks(lo, hi):
        return links.as_blocks((lo, hi), core)

    token = jnp.concatenate([w_token_in, w_token_out]).astype(BF)[None]
    high = steps[3:]
    token_got = swap(token, high[0])
    (mine, theirs, local4, wide3, wide4, weight_squares), token_got = run(
        prepare, place, w12, w_chan_in, w_chan_out, landing=token_got
    )
    token = links.flat_join(token, token_got, high[0], 0)
    got = swap(theirs, 1)
    for mask in high[1:-1]:
        token = links.flat_join(token, land(swap(token, mask)), mask, 0)
    token_got = swap(token, high[-1])
    dout, (token_got, got) = run(kept_cotangent, counts, cot, landing=(token_got, got))
    token = links.flat_join(token, token_got, high[-1], 0)
    token_got = swap(token, 1)
    local3 = run(
        lambda m, g: jnp.where(
            core == 0, jnp.concatenate([m, g], axis=1), jnp.concatenate([g, m], axis=1)
        )[:, None],
        mine,
        got,
    )
    token = links.flat_join(token, land(token_got), 1, 1)
    a0 = links.line_gather(local3[0])
    a0_got = links.line(a0, -2)
    token_got = swap(token, 2)
    (y1, old_rows), (token_got, a0_got) = run(
        lambda x, g, r: (first_norm(x, g), old_row_statistics(r)),
        x,
        gains,
        row_states,
        landing=(token_got, a0_got),
    )
    token = links.flat_join(token, token_got, 2, 1)
    a0 = run(join_two, a0, a0_got)
    a0_got = links.line(a0, -1)
    token_got = swap(token, 4)
    other_dout = swap(dout, 1)
    old_cols, (token_got, a0_got) = run(
        old_column_statistics, col_states, landing=(token_got, a0_got)
    )
    a0 = run(join_two, a0, a0_got)
    a0_got = cross(a0, False)
    a1 = links.line_gather(local3[1])
    a1_got = links.line(a1, -2)

    def matrices(x, got):
        x = links.flat_join(x, got, 4, 1).reshape(size, 2, length)
        return x[:, 0].reshape(PATCHES, HIDDEN), x[:, 1].reshape(HIDDEN, PATCHES)

    (w1, w2), (a0_got, a1_got) = run(matrices, token, token_got, landing=(a0_got, a1_got))
    a0 = run(join_two, a0, a0_got)
    a0_hi = cross(a0, True)
    a1 = run(join_two, a1, a1_got)
    a1_got = links.line(a1, -1)
    (x1, y2), (a0_hi, a1_got) = run(
        token_forward, x, y1, w1, w2, gains, landing=(a0_hi, a1_got)
    )

    other_y2 = swap(y2, 1)
    a1 = run(join_two, a1, a1_got)
    a1_got = cross(a1, False)
    b0 = links.line_gather(local4[0][None])
    b0_got = links.line(b0, -2)
    (held_a0, slope_a0, w3_0), (other_y2, other_dout, a1_got, b0_got) = run(
        channel_forward,
        table,
        *blocks(a0, a0_hi),
        y2,
        landing=(other_y2, other_dout, a1_got, b0_got),
    )
    a1 = run(join_two, a1, a1_got)
    a1_hi = cross(a1, True)
    b0 = run(join_two, b0, b0_got)
    b0_got = links.line(b0, -1)
    b1 = links.line_gather(local4[1][None])
    b1_got = links.line(b1, -2)
    (slope_b0, *c0, act_a0, act_b0), (a1_hi, b0_got, b1_got) = run(
        channel_forward_grad,
        table,
        w3_0,
        other_y2,
        held_a0,
        dout,
        other_dout,
        landing=(a1_hi, b0_got, b1_got),
    )
    b0 = run(join_two, b0, b0_got)
    b0_got = cross(b0, False)
    b1 = run(join_two, b1, b1_got)
    b1_got = links.line(b1, -1)
    (held_a1, slope_a1, w3_1), (b0_got, b1_got) = run(
        channel_forward, table, *blocks(a1, a1_hi), y2, landing=(b0_got, b1_got)
    )
    b0 = run(join_two, b0, b0_got)
    b0_hi = cross(b0, True)
    (slope_b1, *c, act_a1, act_b1), b0_hi = run(
        channel_forward_grad,
        table,
        w3_1,
        other_y2,
        held_a1,
        dout,
        other_dout,
        *c0,
        landing=b0_hi,
    )

    b1 = run(join_two, b1, b1_got)
    b1_got = cross(b1, False)
    (dc_a0, dc_b0, w4_0), b1_got = run(
        channel_backward,
        table,
        *blocks(b0, b0_hi),
        dout,
        other_dout,
        slope_a0,
        slope_b0,
        landing=b1_got,
    )
    b1 = run(join_two, b1, b1_got)
    b1_hi = cross(b1, True)
    d0, b1_hi = run(channel_backward_grad, table, y2, other_y2, dc_a0, dc_b0, landing=b1_hi)
    c_send, c_keep = links.ordered(c, core)
    c_got = cross(c_send, True)
    (dc_a1, dc_b1, w4_1), c_got = run(
        channel_backward,
        table,
        *blocks(b1, b1_hi),
        dout,
        other_dout,
        slope_a1,
        slope_b1,
        landing=c_got,
    )
    d0_send, d0_keep = links.ordered(d0, core)
    d0_got = cross(d0_send, True)
    d1, d0_got = run(channel_backward_grad, table, y2, other_y2, dc_a1, dc_b1, landing=d0_got)
    d1_send, d1_keep = links.ordered(d1, core)
    d1_got = cross(d1_send, True)
    c_keep, c_send = run(fold_two, c_keep, c_got)
    c_got = cross(c_send, False)
    d0_keep, d0_send = run(fold_two, d0_keep, d0_got)
    dy2_other = run(partial_back, (dc_b0, dc_b1), (w3_0, w3_1))
    dy2_got = swap(dy2_other, 1)
    (out_other, h, slope), (dy2_got, d1_got, c_got) = run(
        partial_out,
        (act_b0, act_b1),
        (w4_0, w4_1),
        y1,
        w1,
        landing=(dy2_got, d1_got, c_got),
    )
    d1_keep, d1_send = run(fold_two, d1_keep, d1_got)
    d_keep, d_send = (jnp.concatenate(x, axis=1) for x in ((d0_keep, d1_keep), (d0_send, d1_send)))
    d_got = cross(d_send, False)
    c_keep, c_send = run(fold_two, c_keep, c_got)
    c_got = links.line(c_send, -1)
    out_got = swap(out_other, 1)

    (dx1, dg2), (d_got, c_got, out_got) = run(
        second_back,
        (dc_a0, dc_a1),
        (w3_0, w3_1),
        dy2_got,
        dout,
        x1,
        gains,
        landing=(d_got, c_got, out_got),
    )
    d_keep, d_send = run(fold_two, d_keep, d_got)
    d_got = links.line(d_send, -1)
    c_keep, c_send = run(fold_two, c_keep, c_got)
    c_keep, c_got = links.line_scatter(c_keep, c_send)
    block_out = run(
        block_output, counts, (act_a0, act_a1), (w4_0, w4_1), out_got, x1
    ).reshape(PATCHES, count, D).transpose(1, 0, 2)
    shapes = ((PATCHES, HIDDEN), (HIDDEN, PATCHES))
    touched = [covered(columns, length, size) for _, columns in shapes]
    (da, keep, send), (d_got, c_got) = run(
        functools.partial(token_back, size, touched, length),
        place,
        dx1,
        h,
        slope,
        y1,
        w2,
        landing=(d_got, c_got),
    )
    d_keep, d_send = run(fold_two, d_keep, d_got)
    got = swap(send, steps[0])
    dy1, got = run(input_product, da, w1, landing=got)
    token_grads = keep + got
    keep, send = links.halves(token_grads, steps[1], BF)
    got = swap(send, steps[1])
    d_keep, d_got = links.line_scatter(d_keep, d_send)
    (grad_input, dg1), (got, d_got) = run(
        input_gradient, x, dy1, dx1, gains, landing=(got, d_got)
    )
    token_grads = keep + got.astype(F32)
    mine, theirs = run(lambda p, *parts: end_sums(p, parts), place, d_keep, d_got)
    theirs_got = swap(theirs, 1)
    grad4 = links.scatter_end(c_keep, c_got).reshape(rows4, D)
    for mask in steps[2:]:
        keep, send = links.halves(token_grads, mask, BF if mask == 4 else F32)
        got = swap(send, mask)
        if mask == steps[2]:
            got, theirs_got = land((got, theirs_got))
        else:
            got = land(got)
        token_grads = keep + got.astype(F32)
    token_grads = (token_grads[0, : touched[0]], token_grads[0, touched[0] :, :PATCHES])
    got = theirs_got
    grad_input = grad_input.reshape(PATCHES, count, D).transpose(1, 0, 2)

    summed, flat3, flat4, row3, row4 = run(
        functools.partial(statistics, sub, length),
        place,
        mine,
        got,
        grad4,
        old_rows[2],
        old_rows[3],
        dg1,
        dg2,
        weight_squares,
        *token_grads,
        *old_rows[:2],
    )

    def own_piece(x):
        columns = x.shape[1]
        start = links.index * length - links.index * length // columns * columns
        return lax.dynamic_slice_in_dim(x.reshape(-1), start, length)

    flat12 = None
    for mask in steps:
        got_sums = swap(summed, mask)
        if flat12 is None:
            flat12, got_sums = run(
                lambda *g: [own_piece(x) for x in g], *token_grads, landing=got_sums
            )
        else:
            got_sums = land(got_sums)
        summed = summed + got_sums
    new3, new4, col3, col4, sizes, new1, new2, col1, col2 = update(
        sub,
        length,
        place,
        summed,
        mine,
        got,
        grad4,
        wide3,
        wide4,
        row3,
        row4,
        old_cols[2],
        old_cols[3],
        *token_grads,
        *old_cols[:2],
    )
    rows_out = [summed[ROW1, :PATCHES], summed[ROW2, :HIDDEN], summed[ROW3]]
    rows_out.append(summed[ROW4 : ROW4 + 4].reshape(-1))
    cols_out = [x.reshape(-1) for x in (col1, col2, col3, col4)]
    update_sizes = [sizes[:4, 0]]
    new_weights = [
        w_token_in - own_piece(new1),
        w_token_out - own_piece(new2),
        new3.reshape(-1),
        new4.reshape(-1),
    ]
    token_grads = flat12
    dg1, dg2 = summed[GAINS], summed[GAINS + 1]

    gain_grads = jnp.stack([dg1, dg2])
    gain_stats = DECAY * gain_states + (1.0 - DECAY) * (gain_grads * gain_grads + 1e-30)
    gain_update = gain_grads * lax.rsqrt(gain_stats)
    gain_sizes = jnp.sqrt(jnp.mean(gain_update * gain_update, axis=1))
    gain_update = gain_update / jnp.maximum(1.0, gain_sizes / CLIP)[:, None]
    gain_scale = jnp.sqrt(jnp.mean(gains * gains, axis=1) + 1e-06)
    new_gains = gains - STEP * gain_scale[:, None] * gain_update
    update_rms = jnp.concatenate(update_sizes + [gain_sizes])
    return (
        block_out,
        grad_input,
        token_grads[0],
        token_grads[1],
        flat3.reshape(-1),
        flat4.reshape(-1),
        new_weights[0],
        new_weights[1],
        new_weights[2],
        new_weights[3],
        gain_grads,
        gain_stats,
        new_gains,
        jnp.concatenate(rows_out),
        jnp.concatenate(cols_out),
        update_rms,
    )


def solution(mesh):
    split = P("fsdp")
    images = P("fsdp", None, None)
    in_specs = (images, images) + (split,) * 5 + (P(),) * 4
    out_specs = (images, images) + (split,) * 8 + (P(),) * 6
    return jax.shard_map(
        shards, mesh=mesh, in_specs=in_specs, out_specs=out_specs, check_vma=False
    )
```

```python
import functools

import jax
import jax.numpy as jnp
from jax import lax
from jax.experimental import pallas as pl
from jax.experimental.pallas import tpu as pltpu
from jax.sharding import PartitionSpec as P

D = 768
PATCHES = 196
HIDDEN = 384
DC = 3072
UNITS = 2
F = DC // (2 * UNITS)
BLOCKS = 16
TILE = D // BLOCKS

PACE = 1.0

DECAY = 0.5
CLIP = 0.5
STEP = 1.0

NN = ((1,), (0,))
NT = ((1,), (1,))
TN = ((0,), (0,))

GELU_A = 0.7978845608028654
GELU_B = 0.7978845608028654 * 0.044715

BF = jnp.bfloat16
F32 = jnp.float32


def dot(a, b, dims):
    return lax.dot_general(a, b, (dims, ((), ())), preferred_element_type=F32)


def gelu_pair(v):
    square = v * v
    half = 0.5 + 0.5 * jnp.tanh(v * (GELU_A + GELU_B * square))
    value = v * half
    return value, half + (value - value * half) * (2.0 * GELU_A + (6.0 * GELU_B) * square)


def normalize(values):
    centred = values - jnp.mean(values, axis=-1, keepdims=True)
    spread = jnp.mean(centred * centred, axis=-1, keepdims=True)
    inverse = lax.rsqrt(spread + 1e-06)
    return centred * inverse, inverse


def norm_back(grad, normed, inverse):
    first = jnp.mean(grad, axis=-1, keepdims=True)
    second = jnp.mean(grad * normed, axis=-1, keepdims=True)
    return inverse * (grad - first - normed * second)


ANY = pl.BlockSpec(memory_space=pl.ANY)
SMEM = pl.BlockSpec(memory_space=pltpu.SMEM)
VMEM = pl.BlockSpec(memory_space=pltpu.VMEM)


def struct(shape, dtype):
    return jax.ShapeDtypeStruct(shape, dtype)


def held(shape, dtype):
    return pltpu.VMEM(shape, dtype)


def hbm(shape, dtype):
    return pltpu.HBM(shape, dtype)


def call(kernel, name, inputs, in_specs, outs, scratch=(), mib=16, grid=(), out_specs=None, micros=1.0):
    return pl.pallas_call(
        kernel,
        grid=grid,
        in_specs=in_specs,
        out_specs=out_specs or [VMEM] * len(outs),
        out_shape=outs,
        scratch_shapes=scratch,
        compiler_params=pltpu.CompilerParams(vmem_limit_bytes=mib * 2**20),
        cost_estimate=pl.CostEstimate(
            flops=int(micros * 1.15e9 * PACE), bytes_accessed=1024, transcendentals=0
        ),
        name=name,
    )(*inputs)


def tiled(rows, size, body, carry=0, unroll=1):
    def step(at, carry):
        return body(pl.ds(pl.multiple_of(at * size, 16), size), at * size, carry)

    return lax.fori_loop(0, rows // size, step, carry, unroll=unroll)


LANES = 128
GROUP = D // LANES


def split(rows, dtype=F32):
    return held((GROUP, rows, LANES), dtype)


def put_rows(ref, here, value):
    for at in range(GROUP):
        ref[at, here, :] = value[:, at * LANES : (at + 1) * LANES]


def get_rows(ref, here):
    return jnp.concatenate([ref[at, here, :] for at in range(GROUP)], axis=1)


def of_image(at, count):
    return pl.ds(at, PATCHES, stride=count)


def lane_block(rows):
    return pl.BlockSpec((rows, D), lambda i: (0, i))


def row_block(rows, columns=D):
    return pl.BlockSpec((rows, columns), lambda i: (i, 0))


def used(counts, first, size, count):
    row = lax.broadcasted_iota(jnp.int32, (size, 1), 0) + first
    return lax.rem(row, count) < counts[0]


def column_sums(value):
    return jnp.sum(value.reshape(-1, 8, D), axis=0)


def from_hbm(x):
    return pltpu.with_memory_space_constraint(x, pltpu.HBM)


def prepare_kernel(place, from3, from4, mine, theirs, local4, wide3, wide4, squares, w3, w4, sems):
    copies = [
        pltpu.make_async_copy(from3, w3, sems.at[0]),
        pltpu.make_async_copy(from4, w4, sems.at[1]),
    ]
    for copy in copies:
        copy.start()
    for copy in copies:
        copy.wait()
    rows3, rows4 = wide3.shape[1], wide4.shape[0]
    sub = rows4 // UNITS
    first = place[0] == 0
    per3, per4 = DC // LANES, D // LANES
    full = jnp.concatenate([w3[pl.ds(j, rows3, stride=per3), :] for j in range(per3)], axis=1)
    parts = []
    for at in range(2 * UNITS):
        step = 2 * UNITS * sub
        part = jnp.concatenate(
            [full[:, m * step + at * sub : m * step + (at + 1) * sub] for m in range(DC // step)],
            axis=1,
        )
        wide3[at] = part
        parts.append(part.astype(BF))
    for u in range(UNITS):
        mine[u] = jnp.where(first, parts[u], parts[UNITS + u])
        theirs[u] = jnp.where(first, parts[UNITS + u], parts[u])
    four = jnp.concatenate([w4[pl.ds(j, rows4, stride=per4), :] for j in range(per4)], axis=1)
    wide4[...] = four
    for u in range(UNITS):
        local4[u] = four[u * sub : (u + 1) * sub, :].astype(BF)
    squares[...] = jnp.zeros_like(squares)
    for at, value in enumerate((full, four)):
        total = jnp.sum(jnp.sum(value * value, axis=1, keepdims=True), axis=0, keepdims=True)
        squares[at : at + 1, :] = jnp.broadcast_to(total, (1, LANES))


def prepare(place, w3, w4):
    rows3, rows4 = w3.size // DC, w4.size // D
    w3, w4 = w3.reshape(-1, LANES), w4.reshape(-1, LANES)
    return call(
        prepare_kernel,
        "prepare",
        [place, from_hbm(w3), from_hbm(w4)],
        [SMEM, ANY, ANY],
        [
            struct((UNITS, rows3, F), BF),
            struct((UNITS, rows3, F), BF),
            struct((UNITS, rows4 // UNITS, D), BF),
            hbm((2 * UNITS, rows3, F), F32),
            hbm((rows4, D), F32),
            hbm((8, LANES), F32),
        ],
        [pltpu.VMEM(w3.shape, F32), pltpu.VMEM(w4.shape, F32), pltpu.SemaphoreType.DMA((2,))],
        micros=8,
        mib=6,
    )


def keep_kernel(count, counts, cot, dout):
    size = cot.shape[0]
    keep = used(counts, pl.program_id(0) * size, size, count)
    dout[...] = jnp.where(keep, cot[...].astype(F32), 0.0).astype(BF)


def kept_cotangent(counts, cot):
    rows = cot.shape[0]
    size = rows // 2
    return call(
        functools.partial(keep_kernel, rows // PATCHES),
        "kept_cotangent",
        [counts, from_hbm(cot)],
        [SMEM, row_block(size)],
        [held((rows, D), BF)],
        micros=3,
        grid=(2,),
        out_specs=[row_block(size)],
    )[0]


def first_kernel(count, x, gains, y1, scratch):
    rows = x.shape[0]

    def body(here, first, carry):
        normed, _ = normalize(x[here, :].astype(F32))
        put_rows(scratch, here, normed * gains[0:1, :])
        return carry

    tiled(rows, rows // 7, body)
    for at in range(count):
        y1[:, at * D : (at + 1) * D] = get_rows(scratch, of_image(at, count)).astype(BF)


def first_norm(x, gains):
    rows = x.shape[0]
    count = rows // PATCHES
    return call(
        functools.partial(first_kernel, count),
        "first_norm",
        [x, gains],
        [VMEM, VMEM],
        [held((PATCHES, count * D), BF)],
        [split(rows)],
        micros=4,
        mib=10,
    )[0]


def token_kernel(count, x, y1, w1, w2, gains, away, y2, scratch, x1, sems):
    rows = x.shape[0]

    def image(at, carry):
        lanes = pl.ds(pl.multiple_of(at * D, LANES), D)
        pre = dot(w1[...], y1[:, lanes], TN)
        act = pre * (0.5 + 0.5 * jnp.tanh(pre * (GELU_A + GELU_B * (pre * pre))))
        put_rows(scratch, of_image(at, count), dot(w2[...], act.astype(BF), TN))
        return carry

    lax.fori_loop(0, count, image, 0, unroll=4)
    size = rows // 7

    def leave(at):
        here = pl.ds(pl.multiple_of(at * size, 16), size)
        return pltpu.make_async_copy(x1.at[here, :], away.at[here, :], sems.at[at])

    def body(here, first, carry):
        mixed = x[here, :].astype(F32) + get_rows(scratch, here)
        x1[here, :] = mixed
        leave(first // size).start()
        normed, _ = normalize(mixed)
        y2[here, :] = (normed * gains[1:2, :]).astype(BF)
        return carry

    tiled(rows, size, body)
    for at in range(7):
        leave(at).wait()


def token_forward(x, y1, w1, w2, gains):
    rows = x.shape[0]
    count = rows // PATCHES
    return call(
        functools.partial(token_kernel, count),
        "token_forward",
        [x, y1, w1, w2, gains],
        [VMEM] * 5,
        [hbm((rows, D), F32), held((rows, D), BF)],
        [split(rows), pltpu.VMEM((rows, D), F32), pltpu.SemaphoreType.DMA((7,))],
        micros=8,
        mib=16,
        out_specs=[ANY, VMEM],
    )


def load_unit(table, lo, hi, dest, sems):
    copies = []
    for at in range(BLOCKS):
        source = (lo, hi)[at * 2 // BLOCKS].at[at % (BLOCKS // 2)]
        row = pl.multiple_of(table[at] * TILE, 16)
        copies.append(pltpu.make_async_copy(source, dest.at[pl.ds(row, TILE), :], sems.at[at]))
    for copy in copies:
        copy.start()
    return copies


def store_blocks(table, send, keep, total):
    half = BLOCKS // 2
    unit = send.shape[1] - 1
    for at in range(BLOCKS):
        block = total[at * TILE : (at + 1) * TILE, :]
        place = table[BLOCKS + at]

        @pl.when(place < half)
        def _():
            keep[place, unit] = block

        @pl.when(place >= half)
        def _():
            send[place - half, unit] = block


def rows_forward(y2, weight, act, slope):
    def body(here, first, carry):
        value, der = gelu_pair(dot(y2[here, :], weight[...], NN))
        act[here, :] = value.astype(BF)
        slope[here, :] = der.astype(BF)
        return carry

    tiled(y2.shape[0], y2.shape[0] // 7, body, unroll=7)


def forward_kernel(table, lo, hi, y2, act, slope, weight, sems):
    for copy in load_unit(table, lo, hi, weight, sems):
        copy.wait()
    rows_forward(y2, weight, act, slope)


def channel_forward(table, lo, hi, y2):
    acts = held((y2.shape[0], F), BF)
    return call(
        forward_kernel,
        "channel_forward",
        [table, lo, hi, y2],
        [SMEM, ANY, ANY, VMEM],
        [acts, acts, held((D, F), BF)],
        [pltpu.SemaphoreType.DMA((BLOCKS,))],
        micros=7,
        mib=9,
    )


def both(a, b):
    return jnp.concatenate([a[...], b[...]], axis=0)


def join_before(before, send, keep):
    if before:
        send[:, 0] = before[0][:, 0]
        keep[:, 0] = before[1][:, 0]


def forward_grad_kernel(table, weight, y2, act0, dout0, dout1, *refs):
    *before, slope, send, keep, away0, away, act, leaving = refs
    copies = [pltpu.make_async_copy(act0, away0, leaving.at[0])]
    copies[0].start()
    rows_forward(y2, weight, act, slope)
    copies.append(pltpu.make_async_copy(act, away, leaving.at[1]))
    copies[1].start()
    join_before(before, send, keep)
    total = dot(both(act0, act), both(dout0, dout1), TN)
    store_blocks(table, send, keep, total.astype(BF))
    for copy in copies:
        copy.wait()


def channel_forward_grad(table, weight, y2, act0, dout0, dout1, *before):
    acts = held((y2.shape[0], F), BF)
    half = held((BLOCKS // 2, 1 + len(before) // 2, TILE, D), BF)
    return call(
        forward_grad_kernel,
        "channel_forward_grad",
        [table, weight, y2, act0, dout0, dout1, *before],
        [SMEM] + [VMEM] * (5 + len(before)),
        [acts, half, half, hbm(acts.shape, BF), hbm(acts.shape, BF)],
        [pltpu.VMEM(acts.shape, BF), pltpu.SemaphoreType.DMA((2,))],
        out_specs=[VMEM] * 3 + [ANY] * 2,
        micros=11,
        mib=17,
    )


def backward_kernel(table, lo, hi, dout0, dout1, slope0, slope1, dc0, dc1, weight, sems):
    for copy in load_unit(table, lo, hi, weight, sems):
        copy.wait()
    for dout, slope, dc in ((dout0, slope0, dc0), (dout1, slope1, dc1)):

        def body(here, first, carry, dout=dout, slope=slope, dc=dc):
            value = slope[here, :].astype(F32) * dot(dout[here, :], weight[...], NT)
            dc[here, :] = value.astype(BF)
            return carry

        tiled(dout.shape[0], dout.shape[0] // 2, body)


def channel_backward(table, lo, hi, dout0, dout1, slope0, slope1):
    acts = held((dout0.shape[0], F), BF)
    return call(
        backward_kernel,
        "channel_backward",
        [table, lo, hi, dout0, dout1, slope0, slope1],
        [SMEM, ANY, ANY] + [VMEM] * 4,
        [acts, acts, held((F, D), BF)],
        [pltpu.SemaphoreType.DMA((BLOCKS,))],
        micros=8,
        mib=10,
    )


def backward_grad_kernel(table, y0, y1, dc0, dc1, *refs):
    *before, send, keep = refs
    total = dot(both(y0, y1), both(dc0, dc1), TN)
    join_before(before, send, keep)
    store_blocks(table, send, keep, total.astype(BF))


def channel_backward_grad(table, y0, y1, dc0, dc1, *before):
    half = held((BLOCKS // 2, 1 + len(before) // 2, TILE, D), BF)
    return call(
        backward_grad_kernel,
        "channel_backward_grad",
        [table, y0, y1, dc0, dc1, *before],
        [SMEM] + [VMEM] * (4 + len(before)),
        [half, half],
        micros=6,
        mib=13,
    )


def partial_kernel(d0, d1, w0, w1, out):
    def body(here, first, carry):
        total = dot(d0[here, :], w0[...], NT) + dot(d1[here, :], w1[...], NT)
        out[here, :] = total.astype(BF)
        return carry

    tiled(d0.shape[0], d0.shape[0] // 2, body)


def partial_back(dcs, weights):
    out = held((dcs[0].shape[0], D), BF)
    return call(
        partial_kernel, "partial_back", [*dcs, *weights], [VMEM] * 4, [out], mib=10, micros=5
    )[0]


def partial_out_kernel(a0, a1, w0, w1, y1, wt, out, h, slope):
    total = dot(a0[...], w0[...], NN) + dot(a1[...], w1[...], NN)
    out[...] = total.astype(BF)
    step = pl.program_id(0)
    count = y1.shape[1] // D // 2
    for at in range(count):
        lanes = pl.ds(pl.multiple_of((step * count + at) * D, LANES), D)
        act, der = gelu_pair(dot(wt[...], y1[:, lanes], TN))
        h[:, lanes] = act.astype(BF)
        slope[:, lanes] = der.astype(BF)


def partial_out(acts, weights, y1, wt):
    rows = acts[0].shape[0]
    size = rows // 2
    out = held((HIDDEN, y1.shape[1]), BF)
    return call(
        partial_out_kernel,
        "partial_out",
        [*map(from_hbm, acts), *weights, y1, wt],
        [row_block(size, F)] * 2 + [VMEM] * 4,
        [held((rows, D), BF), out, out],
        micros=10,
        mib=13,
        grid=(2,),
        out_specs=[row_block(size), VMEM, VMEM],
    )


def second_kernel(d0, d1, w0, w1, got, dout, x1, gains, dx1, dg2):
    def body(here, first, carry):
        grad = dot(d0[here, :], w0[...], NT) + dot(d1[here, :], w1[...], NT)
        grad += got[here, :].astype(F32)
        normed, inverse = normalize(x1[here, :])
        total = dout[here, :].astype(F32) + norm_back(grad * gains[1:2, :], normed, inverse)
        put_rows(dx1, here, total)
        return carry + column_sums(grad * normed)

    rows = x1.shape[0]
    sums = tiled(rows, rows // 7, body, jnp.zeros((8, D), F32), unroll=7)
    dg2[...] = jnp.sum(sums, axis=0, keepdims=True)


def second_back(dcs, weights, got, dout, x1, gains):
    rows = x1.shape[0]
    return call(
        second_kernel,
        "second_back",
        [*dcs, *weights, got, dout, x1, gains],
        [VMEM] * 8,
        [split(rows), held((1, D), F32)],
        micros=9,
        mib=10,
    )


def mirrored(value, size):
    out = 0
    for bit in range(size.bit_length() - 1):
        out = out * 2 + (value >> bit) % 2
    return out


def token_back_kernel(size, touched, length, place, dx1, h, slope, y1, w2, da, keep, send, g1, g2, every):
    count = dx1.shape[1] // PATCHES
    g1[...] = jnp.zeros_like(g1)
    g2[...] = jnp.zeros_like(g2)

    def body(at, carry):
        lanes = pl.ds(pl.multiple_of(at * D, LANES), D)
        low = get_rows(dx1, of_image(at, count)).astype(BF)
        back = (slope[:, lanes].astype(F32) * dot(w2[...], low, NN)).astype(BF)
        da[:, lanes] = back
        g1[0:PATCHES, :] += dot(y1[:, lanes], back, NT)
        g2[0:HIDDEN, :] += dot(h[:, lanes], low, NT)
        return carry

    lax.fori_loop(0, count, body, 0, unroll=4)
    for at in range(size):
        spot = mirrored(at, size)
        first = at * length // HIDDEN
        every[spot, 0 : touched[0], :] = g1[first : first + touched[0], :]
        first = at * length // PATCHES
        every[spot, touched[0] :, 0:PATCHES] = g2[first : first + touched[1], :]
        every[spot, touched[0] :, PATCHES:] = jnp.zeros((touched[1], HIDDEN - PATCHES), F32)
    half = size // 2
    keep[...] = every[pl.ds(place[0] * half, half)]
    send[...] = every[pl.ds((1 - place[0]) * half, half)]


def token_back(size, touched, length, place, dx1, h, slope, y1, w2):
    count = dx1.shape[1] // PATCHES
    rows = sum(touched)
    return call(
        functools.partial(token_back_kernel, size, touched, length),
        "token_back",
        [place, dx1, h, slope, y1, w2],
        [SMEM] + [VMEM] * 5,
        [
            held((HIDDEN, count * D), BF),
            held((size // 2, rows, HIDDEN), F32),
            held((size // 2, rows, HIDDEN), F32),
        ],
        [
            pltpu.VMEM((PATCHES + touched[0], HIDDEN), F32),
            pltpu.VMEM((HIDDEN + touched[1], PATCHES), F32),
            pltpu.VMEM((size, rows, HIDDEN), F32),
        ],
        micros=10,
        mib=12,
    )


def input_product_kernel(da, w1, out):
    count = da.shape[1] // D

    def body(at, carry):
        lanes = pl.ds(pl.multiple_of(at * D, LANES), D)
        put_rows(out, of_image(at, count), dot(w1[...], da[:, lanes], NN))
        return carry

    lax.fori_loop(0, count, body, 0, unroll=4)


def input_product(da, w1):
    rows = da.shape[1] // D * PATCHES
    return call(
        input_product_kernel, "input_product", [da, w1], [VMEM] * 2, [split(rows)], mib=6, micros=4
    )[0]


def input_kernel(x, dy1, dx1, gains, out, dg1):
    step = pl.program_id(0)
    size = out.shape[0]

    @pl.when(step == 0)
    def _():
        dg1[...] = jnp.zeros_like(dg1)

    here = pl.ds(pl.multiple_of(step * size, 8), size)
    grad = get_rows(dy1, here)
    normed, inverse = normalize(x[...].astype(F32))
    dg1[...] += jnp.sum(column_sums(grad * normed), axis=0, keepdims=True)
    out[...] = get_rows(dx1, here) + norm_back(grad * gains[0:1, :], normed, inverse)


def input_gradient(x, dy1, dx1, gains):
    rows = x.shape[0]
    size = rows // 7
    return call(
        input_kernel,
        "input_gradient",
        [from_hbm(x), dy1, dx1, gains],
        [row_block(size), VMEM, VMEM, VMEM],
        [hbm((rows, D), F32), held((1, D), F32)],
        micros=6,
        mib=12,
        grid=(7,),
        out_specs=[row_block(size), VMEM],
    )


def out_kernel(count, counts, a0, a1, w0, w1, got, x1, out):
    size = out.shape[0]
    first = pl.program_id(0) * size
    here = pl.ds(pl.multiple_of(first, 16), size)
    total = dot(a0[...], w0[...], NN) + dot(a1[...], w1[...], NN)
    total += got[here, :].astype(F32) + x1[here, :]
    out[...] = jnp.where(used(counts, first, size, count), total, 0.0)


def block_output(counts, acts, weights, got, x1):
    rows = x1.shape[0]
    size = rows // 2
    return call(
        functools.partial(out_kernel, rows // PATCHES),
        "block_output",
        [counts, *map(from_hbm, acts), *weights, got, x1],
        [SMEM] + [row_block(size, F)] * 2 + [VMEM] * 4,
        [hbm((rows, D), F32)],
        micros=9,
        mib=22,
        grid=(2,),
        out_specs=[row_block(size)],
    )[0]


def join_two(a, b):
    return join([a, b])


def fold_two(a, b):
    return fold([a, b], 2)


def join_kernel(*refs):
    rows = refs[0].shape[0]
    for at, ref in enumerate(refs[:-1]):
        refs[-1][at * rows : (at + 1) * rows, :] = ref[...]


def join(parts):
    shape = parts[0].shape
    flat = [x.reshape(-1, D) for x in parts]
    out = held((len(parts) * flat[0].shape[0], D), BF)
    x = call(join_kernel, "join", flat, [VMEM] * len(parts), [out], mib=8)[0]
    return x.reshape((len(parts) * shape[0],) + shape[1:])


def fold_kernel(parts, splits, *refs):
    rows = refs[0].shape[0] // splits
    for at in range(splits):
        here = slice(at * rows, (at + 1) * rows)
        total = refs[0][here, :].astype(F32)
        for part in refs[1:parts]:
            total = total + part[here, :].astype(F32)
        refs[parts + at][...] = total.astype(refs[parts + at].dtype)


def fold(parts, splits):
    shape = parts[0].shape
    lead = shape[0] // splits
    flat = [x.reshape(-1, D) for x in parts]
    rows = flat[0].shape[0] // splits
    dtypes = [F32 if lead == 1 else BF] + [BF] * (splits - 1)
    outs = call(
        functools.partial(fold_kernel, len(parts), splits),
        "fold",
        flat,
        [VMEM] * len(parts),
        [held((rows, D), dtype) for dtype in dtypes],
        mib=8,
    )
    return [x.reshape((lead,) + shape[1:]) for x in outs]


def end_kernel(place, *refs):
    *parts, mine, theirs = refs
    rows = mine.shape[1]
    first = place[0] == 0
    for unit in range(UNITS):
        total = parts[0][unit].astype(F32)
        for part in parts[1:]:
            total = total + part[unit].astype(F32)
        mine[unit] = jnp.where(first, total[:rows], total[rows:])
        theirs[unit] = jnp.where(first, total[rows:], total[:rows])


def end_sums(place, parts):
    parts = [x[0] for x in parts]
    out = held((UNITS, parts[0].shape[1] // 2, F), F32)
    return call(
        end_kernel,
        "end_sums",
        [place, *parts],
        [SMEM] + [VMEM] * len(parts),
        [out, out],
        mib=6,
    )


def in_order(place, mine, got):
    first = place[0] == 0
    own = [mine[u] for u in range(UNITS)]
    other = [got[u] for u in range(UNITS)]
    return [jnp.where(first, x, y) for x, y in zip(own + other, other + own)]


def natural(parts, sub):
    return jnp.concatenate(
        [part[:, m * sub : (m + 1) * sub] for m in range(F // sub) for part in parts], axis=1
    )


def put_flat(ref, value):
    per = value.shape[1] // LANES
    for j in range(per):
        ref[pl.ds(j, value.shape[0], stride=per), :] = value[:, j * LANES : (j + 1) * LANES]


STATS = 24
COL3, WEIGHTED3, COL4, WEIGHTED4, ROW3, ROW4, GAINS, SQUARES = 0, 4, 8, 9, 10, 11, 15, 17


def row_statistics(index, grad, squares, old, vec, start):
    rows = grad.shape[0]
    spots = old.shape[0]
    column = lax.broadcasted_iota(jnp.int32, (rows, D), 1)
    target = lax.broadcasted_iota(jnp.int32, (rows, D), 0) + index * rows
    here = [column + spot * D == target for spot in range(spots)]
    before = sum(
        jnp.sum(jnp.where(mask, old[spot : spot + 1, :], 0.0), axis=1, keepdims=True)
        for spot, mask in enumerate(here)
    )
    mean = squares / (grad.shape[1]) + 1e-30
    row = DECAY * before + (1.0 - DECAY) * mean
    for spot, mask in enumerate(here):
        vec[start + spot : start + spot + 1, :] = jnp.sum(
            jnp.where(mask, row, 0.0), axis=0, keepdims=True
        )
    return row


ROW1, ROW2, COL1, WEIGHTED1, COL2, WEIGHTED2 = 18, 19, 20, 21, 22, 23


def covered(columns, length, size):
    return max((at * length + length - 1) // columns - at * length // columns + 1 for at in range(size))


def in_piece(index, length, rows, columns):
    first = index * length // columns
    row = lax.broadcasted_iota(jnp.int32, (rows, columns), 0) + first
    at = row * columns + lax.broadcasted_iota(jnp.int32, (rows, columns), 1)
    return first, (at >= index * length) & (at < (index + 1) * length)


def spots(first, rows):
    column = lax.broadcasted_iota(jnp.int32, (rows, D), 1)
    return column == lax.broadcasted_iota(jnp.int32, (rows, D), 0) + first


def token_statistics(index, length, grad, old, vec, row_at, col_at):
    rows, columns = grad.shape
    first, inside = in_piece(index, length, rows, columns)
    squares = grad * grad
    here = spots(first, rows)
    before = jnp.sum(jnp.where(here, old, 0.0), axis=1, keepdims=True)
    mean = jnp.sum(squares, axis=1, keepdims=True) / columns + 1e-30
    row = DECAY * before + (1.0 - DECAY) * mean
    mine = jnp.where(inside, squares, 0.0)
    vec[col_at : col_at + 1, 0:columns] = jnp.sum(mine, axis=0, keepdims=True)
    weighted = jnp.where(inside, squares / row, 0.0)
    vec[col_at + 1 : col_at + 2, 0:columns] = jnp.sum(weighted, axis=0, keepdims=True)
    starts = jnp.where(inside[:, 0:1] & here, row, 0.0)
    vec[row_at : row_at + 1, :] = jnp.sum(starts, axis=0, keepdims=True)


def stats_kernel(sub, length, place, token_sums, mine, got, g4, old3, old4, dg1, dg2, sums, g1, g2, old1, old2, *refs):
    vec, flat3, flat4, row3, row4 = refs
    parts = in_order(place, mine, got)
    index = place[1]
    rows3 = parts[0].shape[0]
    squared = [x * x for x in parts]
    vec[...] = jnp.zeros_like(vec)
    total = sum(jnp.sum(x, axis=1, keepdims=True) for x in squared)
    wide = jnp.concatenate(squared, axis=1)
    row = row_statistics(index, wide, total, old3, vec, ROW3)
    row3[...] = jnp.broadcast_to(row, (rows3, LANES))
    scale = 1.0 / row
    for at, x in enumerate(squared):
        vec[COL3 + at : COL3 + at + 1, :] = jnp.sum(x, axis=0, keepdims=True)
        vec[WEIGHTED3 + at : WEIGHTED3 + at + 1, :] = jnp.sum(x * scale, axis=0, keepdims=True)
    four = g4[...]
    square4 = four * four
    row = row_statistics(
        index, square4, jnp.sum(square4, axis=1, keepdims=True), old4, vec, ROW4
    )
    row4[...] = jnp.broadcast_to(row, (four.shape[0], LANES))
    vec[COL4 : COL4 + 1, :] = jnp.sum(square4, axis=0, keepdims=True)
    vec[WEIGHTED4 : WEIGHTED4 + 1, :] = jnp.sum(square4 * (1.0 / row), axis=0, keepdims=True)
    vec[GAINS : GAINS + 1, :] = dg1[...]
    vec[GAINS + 1 : GAINS + 2, :] = dg2[...]
    for at in range(2):
        vec[SQUARES : SQUARES + 1, at * LANES : (at + 1) * LANES] = jnp.full(
            (1, LANES), token_sums[at], F32
        )
        lanes = slice((at + 2) * LANES, (at + 3) * LANES)
        vec[SQUARES : SQUARES + 1, lanes] = sums[at : at + 1, :]
    token_statistics(index, length, g1[...], old1[...], vec, ROW1, COL1)
    token_statistics(index, length, g2[...], old2[...], vec, ROW2, COL2)
    put_flat(flat3, natural(parts, sub))
    put_flat(flat4, four)


def statistics(sub, length, *inputs):
    rows3, rows4 = inputs[2].shape[1], inputs[4].shape[0]
    return call(
        functools.partial(stats_kernel, sub, length),
        "statistics",
        list(inputs),
        [SMEM] * 2 + [VMEM] * (len(inputs) - 2),
        [
            struct((STATS, D), F32),
            struct((rows3 * DC // LANES, LANES), F32),
            struct((rows4 * D // LANES, LANES), F32),
            held((rows3, LANES), F32),
            held((rows4, LANES), F32),
        ],
        micros=2,
        mib=8,
    )


def lane_total(x):
    return jnp.sum(jnp.sum(x, axis=1, keepdims=True), axis=0, keepdims=True)


def token_update(index, length, which, grad, old, vec, row_at, col_at, new, col_out, sizes):
    rows, columns = grad.shape
    count = float(PATCHES * HIDDEN)
    every = PATCHES * HIDDEN // columns
    first, _ = in_piece(index, length, rows, columns)
    row = vec[row_at : row_at + 1, :]
    mean = lane_total(row) / every
    col = DECAY * old[...] + (1.0 - DECAY) * (vec[col_at : col_at + 1, 0:columns] / every + 1e-30)
    weighted = vec[col_at + 1 : col_at + 2, 0:columns]
    size = jnp.sqrt(lane_total(weighted / col) * mean / count)
    sizes[which : which + 1, :] = jnp.broadcast_to(size, (1, LANES))
    square = vec[SQUARES : SQUARES + 1, which * LANES : which * LANES + 1]
    scale = STEP * jnp.sqrt(square / count + 1e-06) / jnp.maximum(1.0, size / CLIP)
    here = spots(first, rows)
    left = jnp.sum(jnp.where(here, row, 0.0), axis=1, keepdims=True)
    known = lax.broadcasted_iota(jnp.int32, (rows, 1), 0) + first < every
    left = jnp.where(known, lax.rsqrt(jnp.where(known, left, 1.0) / mean), 0.0)
    new[...] = grad[...] * left * lax.rsqrt(col) * scale
    col_out[...] = col


def update_kernel(sub, length, place, vec, mine, got, g4, wide3, wide4, row3, row4, old3, old4, *refs):
    g1, g2, old1, old2, new3, new4, col3, col4, sizes, new1, new2, col1, col2 = refs
    parts = in_order(place, mine, got)
    count = float(D * DC)
    sizes[...] = jnp.zeros_like(sizes)
    token_update(place[1], length, 0, g1, old1, vec, ROW1, COL1, new1, col1, sizes)
    token_update(place[1], length, 1, g2, old2, vec, ROW2, COL2, new2, col2, sizes)
    for which in range(2):
        rows = vec[ROW3 : ROW3 + 1, :] if which == 0 else vec[ROW4 : ROW4 + 4, :]
        mean = lane_total(rows) / (D if which == 0 else DC)
        if which == 0:
            cols = DECAY * old3[...] + (1.0 - DECAY) * (vec[COL3 : COL3 + 4, :] / D + 1e-30)
            weighted = vec[WEIGHTED3 : WEIGHTED3 + 4, :]
        else:
            cols = DECAY * old4[...] + (1.0 - DECAY) * (vec[COL4 : COL4 + 1, :] / DC + 1e-30)
            weighted = vec[WEIGHTED4 : WEIGHTED4 + 1, :]
        size = jnp.sqrt(lane_total(weighted / cols) * mean / count)
        sizes[which + 2 : which + 3, :] = jnp.broadcast_to(size, (1, LANES))
        square = vec[SQUARES : SQUARES + 1, (which + 2) * LANES : (which + 2) * LANES + 1]
        scale = STEP * jnp.sqrt(square / count + 1e-06) / jnp.maximum(1.0, size / CLIP)
        if which == 0:
            left = lax.rsqrt(row3[:, 0:1] / mean) * scale
            right = lax.rsqrt(cols)
            new = [
                wide3[at] - parts[at] * left * right[at : at + 1, :] for at in range(2 * UNITS)
            ]
            put_flat(new3, natural(new, sub))
            col3[...] = natural([cols[at : at + 1, :] for at in range(2 * UNITS)], sub)
        else:
            left = lax.rsqrt(row4[:, 0:1] / mean) * scale
            put_flat(new4, wide4[...] - g4[...] * left * lax.rsqrt(cols))
            col4[...] = cols


def update(sub, length, *inputs):
    wide3, wide4 = inputs[5:7]
    g1, g2 = inputs[-4:-2]
    return call(
        functools.partial(update_kernel, sub, length),
        "update",
        list(inputs),
        [SMEM] + [VMEM] * (len(inputs) - 1),
        [
            struct((wide3.size // LANES, LANES), F32),
            struct((wide4.size // LANES, LANES), F32),
            struct((1, DC), F32),
            struct((1, D), F32),
            struct((8, LANES), F32),
            struct(g1.shape, F32),
            struct(g2.shape, F32),
            struct((1, HIDDEN), F32),
            struct((1, PATCHES), F32),
        ],
        micros=2,
        mib=8,
    )


class Links:
    def __init__(self, size, token):
        self.size = size
        self.chips = size // 2
        bits = self.chips.bit_length() - 1
        self.high = [1 << b for b in reversed(range(2, bits))]
        self.orders = (self.high + [1, 2], self.high + [2, 1])
        self.index = lax.axis_index("fsdp")
        self.core = self.index & 1
        self.chip = self.index >> 1
        self.token = token

    def tie(self, x):
        x, self.token = lax.optimization_barrier((x, self.token))
        return x

    land = tie

    def run(self, function, *inputs, landing=None):
        out = function(*self.tie(inputs))
        if landing is None:
            return self.tie(out)
        return self.tie((out, landing))

    def swap(self, x, mask):
        return lax.ppermute(self.tie(x), "fsdp", [(i, i ^ mask) for i in range(self.size)])

    def cross(self, x, last):
        masks = (2, 1) if last else (1, 2)
        pairs = [(i, i ^ (masks[i & 1] << 1)) for i in range(self.size)]
        return lax.ppermute(self.tie(x), "fsdp", pairs)

    def line(self, x, level):
        return self.swap(x, self.high[level] << 1)

    def line_gather(self, x):
        for mask in self.high[:-2]:
            x = self.run(join_two, x, self.land(self.swap(x, mask << 1)))
        return x

    def line_scatter(self, keep, send):
        for mask in reversed(self.high[1:-1]):
            keep, send = self.run(fold_two, keep, self.land(self.swap(send, mask << 1)))
        return keep, self.swap(send, self.high[0] << 1)

    def owners(self, core):
        place = jnp.arange(self.chips, dtype=jnp.int32)
        owner = jnp.full((self.chips,), self.chip, jnp.int32)
        for level in range(len(self.orders[0])):
            bit = (place >> level) & 1
            mask = jnp.where(core == 0, self.orders[0][level], self.orders[1][level])
            owner = owner ^ (bit * mask)
        return owner

    def places(self, core):
        relative = jnp.arange(self.chips, dtype=jnp.int32) ^ self.chip
        place = jnp.zeros_like(relative)
        for level in range(len(self.orders[0])):
            mask = jnp.where(core == 0, self.orders[0][level], self.orders[1][level])
            place = place | (((relative & mask) != 0).astype(jnp.int32) << level)
        return place

    def table(self, core):
        if self.chips == BLOCKS:
            return jnp.concatenate([self.owners(core), self.places(core)])
        order = jnp.arange(BLOCKS, dtype=jnp.int32)
        return jnp.concatenate([order, order])

    def scatter_end(self, own, received):
        return self.run(lambda *p: fold(p, 1), own, received)[0][0]

    def as_blocks(self, halves, core):
        if self.chips == BLOCKS:
            return halves
        x = jnp.take(jnp.concatenate(halves, axis=0), self.places(core), axis=0)
        x = x.reshape(BLOCKS, TILE, D)
        return x[: BLOCKS // 2], x[BLOCKS // 2 :]

    def ordered(self, halves, core):
        if self.chips == BLOCKS:
            return halves
        send, keep = halves
        x = jnp.concatenate([keep, send], axis=0).transpose(1, 0, 2, 3)
        x = x.reshape(x.shape[0], self.chips, -1, D).transpose(1, 0, 2, 3)
        x = jnp.take(x, self.owners(core), axis=0)
        return x[self.chips // 2 :], x[: self.chips // 2]

    def flat_join(self, x, got, mask, axis=1):
        upper = (self.index & mask) != 0
        return jnp.where(
            upper, jnp.concatenate([got, x], axis=axis), jnp.concatenate([x, got], axis=axis)
        )

    def halves(self, x, mask, dtype):
        half = x.shape[0] // 2
        upper = (self.index & mask) != 0
        keep = jnp.where(upper, x[half:], x[:half])
        send = jnp.where(upper, x[:half], x[half:])
        return keep, send.astype(dtype)


def shards(
    images,
    cotangent,
    counts,
    w_token_in,
    w_token_out,
    w_chan_in,
    w_chan_out,
    gains,
    row_states,
    col_states,
    gain_states,
):
    links = Links(D * DC // w_chan_in.shape[0], counts)
    size, chips, core = links.size, links.chips, links.core
    run, land, swap, cross = links.run, links.land, links.swap, links.cross
    count = images.shape[0]
    rows = count * PATCHES
    table = links.table(core)
    steps = [1 << at for at in range(size.bit_length() - 1)]
    x = images.transpose(1, 0, 2).reshape(rows, D)
    cot = cotangent.transpose(1, 0, 2).reshape(rows, D)

    rows3 = D // size
    rows4 = DC // size
    sub = rows4 // UNITS
    length = w_token_in.shape[0]
    place = jnp.stack([core, links.index])
    edges_r = (0, PATCHES, PATCHES + HIDDEN, PATCHES + HIDDEN + D, PATCHES + HIDDEN + D + DC)
    edges_c = (0, HIDDEN, HIDDEN + PATCHES, HIDDEN + PATCHES + DC, HIDDEN + PATCHES + DC + D)

    def old_row_statistics(rows):
        rows = [rows[edges_r[k] : edges_r[k + 1]] for k in range(4)]
        rows[2:] = rows[2].reshape(1, D), rows[3].reshape(4, D)
        rows[:2] = (jnp.pad(row, (0, D - row.shape[0]))[None] for row in rows[:2])
        return rows

    def old_column_statistics(cols):
        cols = [cols[edges_c[k] : edges_c[k + 1]] for k in range(4)]
        wide = cols[2].reshape(chips, 2, UNITS, sub).transpose(1, 2, 0, 3).reshape(2 * UNITS, F)
        cols[2:] = wide, cols[3].reshape(1, D)
        cols[:2] = (col[None] for col in cols[:2])
        return cols

    def blocks(lo, hi):
        return links.as_blocks((lo, hi), core)

    token = jnp.concatenate([w_token_in, w_token_out]).astype(BF)[None]
    high = steps[3:]
    token_got = swap(token, high[0])
    (mine, theirs, local4, wide3, wide4, weight_squares), token_got = run(
        prepare, place, w_chan_in, w_chan_out, landing=token_got
    )
    token = links.flat_join(token, token_got, high[0], 0)
    got = swap(theirs, 1)
    for mask in high[1:-1]:
        token = links.flat_join(token, land(swap(token, mask)), mask, 0)
    token_got = swap(token, high[-1])
    dout, (token_got, got) = run(kept_cotangent, counts, cot, landing=(token_got, got))
    token = links.flat_join(token, token_got, high[-1], 0)
    token_got = swap(token, 1)
    local3 = run(
        lambda m, g: jnp.where(
            core == 0, jnp.concatenate([m, g], axis=1), jnp.concatenate([g, m], axis=1)
        )[:, None],
        mine,
        got,
    )
    token = links.flat_join(token, land(token_got), 1, 1)
    a0 = links.line_gather(local3[0])
    a0_got = links.line(a0, -2)
    token_got = swap(token, 2)
    (y1, old_rows), (token_got, a0_got) = run(
        lambda x, g, r: (first_norm(x, g), old_row_statistics(r)),
        x,
        gains,
        row_states,
        landing=(token_got, a0_got),
    )
    token = links.flat_join(token, token_got, 2, 1)
    a0 = run(join_two, a0, a0_got)
    a0_got = links.line(a0, -1)
    token_got = swap(token, 4)
    other_dout = swap(dout, 1)
    (old_cols, token_sums), (token_got, a0_got) = run(
        lambda c, *w: (old_column_statistics(c), jnp.stack([jnp.sum(x * x) for x in w])),
        col_states,
        w_token_in,
        w_token_out,
        landing=(token_got, a0_got),
    )
    a0 = run(join_two, a0, a0_got)
    a0_got = cross(a0, False)
    a1 = links.line_gather(local3[1])
    a1_got = links.line(a1, -2)

    def matrices(x, got):
        x = links.flat_join(x, got, 4, 1).reshape(size, 2, length)
        return x[:, 0].reshape(PATCHES, HIDDEN), x[:, 1].reshape(HIDDEN, PATCHES)

    (w1, w2), (a0_got, a1_got) = run(matrices, token, token_got, landing=(a0_got, a1_got))
    a0 = run(join_two, a0, a0_got)
    a0_hi = cross(a0, True)
    a1 = run(join_two, a1, a1_got)
    a1_got = links.line(a1, -1)
    (x1, y2), (a0_hi, a1_got) = run(
        token_forward, x, y1, w1, w2, gains, landing=(a0_hi, a1_got)
    )

    other_y2 = swap(y2, 1)
    a1 = run(join_two, a1, a1_got)
    a1_got = cross(a1, False)
    b0 = links.line_gather(local4[0][None])
    b0_got = links.line(b0, -2)
    (held_a0, slope_a0, w3_0), (other_y2, other_dout, a1_got, b0_got) = run(
        channel_forward,
        table,
        *blocks(a0, a0_hi),
        y2,
        landing=(other_y2, other_dout, a1_got, b0_got),
    )
    a1 = run(join_two, a1, a1_got)
    a1_hi = cross(a1, True)
    b0 = run(join_two, b0, b0_got)
    b0_got = links.line(b0, -1)
    b1 = links.line_gather(local4[1][None])
    b1_got = links.line(b1, -2)
    (slope_b0, *c0, act_a0, act_b0), (a1_hi, b0_got, b1_got) = run(
        channel_forward_grad,
        table,
        w3_0,
        other_y2,
        held_a0,
        dout,
        other_dout,
        landing=(a1_hi, b0_got, b1_got),
    )
    b0 = run(join_two, b0, b0_got)
    b0_got = cross(b0, False)
    b1 = run(join_two, b1, b1_got)
    b1_got = links.line(b1, -1)
    (held_a1, slope_a1, w3_1), (b0_got, b1_got) = run(
        channel_forward, table, *blocks(a1, a1_hi), y2, landing=(b0_got, b1_got)
    )
    b0 = run(join_two, b0, b0_got)
    b0_hi = cross(b0, True)
    (slope_b1, *c, act_a1, act_b1), b0_hi = run(
        channel_forward_grad,
        table,
        w3_1,
        other_y2,
        held_a1,
        dout,
        other_dout,
        *c0,
        landing=b0_hi,
    )

    b1 = run(join_two, b1, b1_got)
    b1_got = cross(b1, False)
    (dc_a0, dc_b0, w4_0), b1_got = run(
        channel_backward,
        table,
        *blocks(b0, b0_hi),
        dout,
        other_dout,
        slope_a0,
        slope_b0,
        landing=b1_got,
    )
    b1 = run(join_two, b1, b1_got)
    b1_hi = cross(b1, True)
    d0, b1_hi = run(channel_backward_grad, table, y2, other_y2, dc_a0, dc_b0, landing=b1_hi)
    c_send, c_keep = links.ordered(c, core)
    c_got = cross(c_send, True)
    (dc_a1, dc_b1, w4_1), c_got = run(
        channel_backward,
        table,
        *blocks(b1, b1_hi),
        dout,
        other_dout,
        slope_a1,
        slope_b1,
        landing=c_got,
    )
    d0_send, d0_keep = links.ordered(d0, core)
    d0_got = cross(d0_send, True)
    d1, d0_got = run(channel_backward_grad, table, y2, other_y2, dc_a1, dc_b1, landing=d0_got)
    d1_send, d1_keep = links.ordered(d1, core)
    d1_got = cross(d1_send, True)
    c_keep, c_send = run(fold_two, c_keep, c_got)
    c_got = cross(c_send, False)
    d0_keep, d0_send = run(fold_two, d0_keep, d0_got)
    dy2_other = run(partial_back, (dc_b0, dc_b1), (w3_0, w3_1))
    dy2_got = swap(dy2_other, 1)
    (out_other, h, slope), (dy2_got, d1_got, c_got) = run(
        partial_out,
        (act_b0, act_b1),
        (w4_0, w4_1),
        y1,
        w1,
        landing=(dy2_got, d1_got, c_got),
    )
    d1_keep, d1_send = run(fold_two, d1_keep, d1_got)
    d_keep, d_send = (jnp.concatenate(x, axis=1) for x in ((d0_keep, d1_keep), (d0_send, d1_send)))
    d_got = cross(d_send, False)
    c_keep, c_send = run(fold_two, c_keep, c_got)
    c_got = links.line(c_send, -1)
    out_got = swap(out_other, 1)

    (dx1, dg2), (d_got, c_got, out_got) = run(
        second_back,
        (dc_a0, dc_a1),
        (w3_0, w3_1),
        dy2_got,
        dout,
        x1,
        gains,
        landing=(d_got, c_got, out_got),
    )
    d_keep, d_send = run(fold_two, d_keep, d_got)
    d_got = links.line(d_send, -1)
    c_keep, c_send = run(fold_two, c_keep, c_got)
    c_keep, c_got = links.line_scatter(c_keep, c_send)
    block_out = run(
        block_output, counts, (act_a0, act_a1), (w4_0, w4_1), out_got, x1
    ).reshape(PATCHES, count, D).transpose(1, 0, 2)
    shapes = ((PATCHES, HIDDEN), (HIDDEN, PATCHES))
    touched = [covered(columns, length, size) for _, columns in shapes]
    (da, keep, send), (d_got, c_got) = run(
        functools.partial(token_back, size, touched, length),
        place,
        dx1,
        h,
        slope,
        y1,
        w2,
        landing=(d_got, c_got),
    )
    d_keep, d_send = run(fold_two, d_keep, d_got)
    got = swap(send, steps[0])
    dy1, got = run(input_product, da, w1, landing=got)
    token_grads = keep + got
    keep, send = links.halves(token_grads, steps[1], BF)
    got = swap(send, steps[1])
    d_keep, d_got = links.line_scatter(d_keep, d_send)
    (grad_input, dg1), (got, d_got) = run(
        input_gradient, x, dy1, dx1, gains, landing=(got, d_got)
    )
    token_grads = keep + got.astype(F32)
    mine, theirs = run(lambda p, *parts: end_sums(p, parts), place, d_keep, d_got)
    theirs_got = swap(theirs, 1)
    grad4 = links.scatter_end(c_keep, c_got).reshape(rows4, D)
    for mask in steps[2:]:
        keep, send = links.halves(token_grads, mask, BF if mask == 4 else F32)
        got = swap(send, mask)
        if mask == steps[2]:
            got, theirs_got = land((got, theirs_got))
        else:
            got = land(got)
        token_grads = keep + got.astype(F32)
    token_grads = (token_grads[0, : touched[0]], token_grads[0, touched[0] :, :PATCHES])
    got = theirs_got
    grad_input = grad_input.reshape(PATCHES, count, D).transpose(1, 0, 2)

    summed, flat3, flat4, row3, row4 = run(
        functools.partial(statistics, sub, length),
        place,
        token_sums,
        mine,
        got,
        grad4,
        old_rows[2],
        old_rows[3],
        dg1,
        dg2,
        weight_squares,
        *token_grads,
        *old_rows[:2],
    )

    def own_piece(x):
        columns = x.shape[1]
        start = links.index * length - links.index * length // columns * columns
        return lax.dynamic_slice_in_dim(x.reshape(-1), start, length)

    flat12 = None
    for mask in steps:
        got_sums = swap(summed, mask)
        if flat12 is None:
            flat12, got_sums = run(
                lambda *g: [own_piece(x) for x in g], *token_grads, landing=got_sums
            )
        else:
            got_sums = land(got_sums)
        summed = summed + got_sums
    new3, new4, col3, col4, sizes, new1, new2, col1, col2 = update(
        sub,
        length,
        place,
        summed,
        mine,
        got,
        grad4,
        wide3,
        wide4,
        row3,
        row4,
        old_cols[2],
        old_cols[3],
        *token_grads,
        *old_cols[:2],
    )
    rows_out = [summed[ROW1, :PATCHES], summed[ROW2, :HIDDEN], summed[ROW3]]
    rows_out.append(summed[ROW4 : ROW4 + 4].reshape(-1))
    cols_out = [x.reshape(-1) for x in (col1, col2, col3, col4)]
    update_sizes = [sizes[:4, 0]]
    new_weights = [
        w_token_in - own_piece(new1),
        w_token_out - own_piece(new2),
        new3.reshape(-1),
        new4.reshape(-1),
    ]
    token_grads = flat12
    dg1, dg2 = summed[GAINS], summed[GAINS + 1]

    gain_grads = jnp.stack([dg1, dg2])
    gain_stats = DECAY * gain_states + (1.0 - DECAY) * (gain_grads * gain_grads + 1e-30)
    gain_update = gain_grads * lax.rsqrt(gain_stats)
    gain_sizes = jnp.sqrt(jnp.mean(gain_update * gain_update, axis=1))
    gain_update = gain_update / jnp.maximum(1.0, gain_sizes / CLIP)[:, None]
    gain_scale = jnp.sqrt(jnp.mean(gains * gains, axis=1) + 1e-06)
    new_gains = gains - STEP * gain_scale[:, None] * gain_update
    update_rms = jnp.concatenate(update_sizes + [gain_sizes])
    return (
        block_out,
        grad_input,
        token_grads[0],
        token_grads[1],
        flat3.reshape(-1),
        flat4.reshape(-1),
        new_weights[0],
        new_weights[1],
        new_weights[2],
        new_weights[3],
        gain_grads,
        gain_stats,
        new_gains,
        jnp.concatenate(rows_out),
        jnp.concatenate(cols_out),
        update_rms,
    )


def solution(mesh):
    split = P("fsdp")
    images = P("fsdp", None, None)
    in_specs = (images, images) + (split,) * 5 + (P(),) * 4
    out_specs = (images, images) + (split,) * 8 + (P(),) * 6
    return jax.shard_map(
        shards, mesh=mesh, in_specs=in_specs, out_specs=out_specs, check_vma=False
    )
```

```python
import functools

import jax
import jax.numpy as jnp
from jax import lax
from jax.experimental import pallas as pl
from jax.experimental.pallas import tpu as pltpu
from jax.sharding import PartitionSpec as P

D = 768
PATCHES = 196
HIDDEN = 384
DC = 3072
UNITS = 2
F = DC // (2 * UNITS)
BLOCKS = 16
TILE = D // BLOCKS

PACE = 1.0

DECAY = 0.5
CLIP = 0.5
STEP = 1.0

NN = ((1,), (0,))
NT = ((1,), (1,))
TN = ((0,), (0,))

GELU_A = 0.7978845608028654
GELU_B = 0.7978845608028654 * 0.044715

BF = jnp.bfloat16
F32 = jnp.float32


def dot(a, b, dims):
    return lax.dot_general(a, b, (dims, ((), ())), preferred_element_type=F32)


def gelu_pair(v):
    square = v * v
    half = 0.5 + 0.5 * jnp.tanh(v * (GELU_A + GELU_B * square))
    value = v * half
    return value, half + (value - value * half) * (2.0 * GELU_A + (6.0 * GELU_B) * square)


def normalize(values):
    centred = values - jnp.mean(values, axis=-1, keepdims=True)
    spread = jnp.mean(centred * centred, axis=-1, keepdims=True)
    inverse = lax.rsqrt(spread + 1e-06)
    return centred * inverse, inverse


def norm_back(grad, normed, inverse):
    first = jnp.mean(grad, axis=-1, keepdims=True)
    second = jnp.mean(grad * normed, axis=-1, keepdims=True)
    return inverse * (grad - first - normed * second)


ANY = pl.BlockSpec(memory_space=pl.ANY)
SMEM = pl.BlockSpec(memory_space=pltpu.SMEM)
VMEM = pl.BlockSpec(memory_space=pltpu.VMEM)


def struct(shape, dtype):
    return jax.ShapeDtypeStruct(shape, dtype)


def held(shape, dtype):
    return pltpu.VMEM(shape, dtype)


def hbm(shape, dtype):
    return pltpu.HBM(shape, dtype)


def call(kernel, name, inputs, in_specs, outs, scratch=(), mib=16, grid=(), out_specs=None, micros=1.0):
    return pl.pallas_call(
        kernel,
        grid=grid,
        in_specs=in_specs,
        out_specs=out_specs or [VMEM] * len(outs),
        out_shape=outs,
        scratch_shapes=scratch,
        compiler_params=pltpu.CompilerParams(vmem_limit_bytes=mib * 2**20),
        cost_estimate=pl.CostEstimate(
            flops=int(micros * 1.15e9 * PACE), bytes_accessed=1024, transcendentals=0
        ),
        name=name,
    )(*inputs)


def tiled(rows, size, body, carry=0, unroll=1):
    def step(at, carry):
        return body(pl.ds(pl.multiple_of(at * size, 16), size), at * size, carry)

    return lax.fori_loop(0, rows // size, step, carry, unroll=unroll)


LANES = 128
GROUP = D // LANES


def split(rows, dtype=F32):
    return held((GROUP, rows, LANES), dtype)


def put_rows(ref, here, value):
    for at in range(GROUP):
        ref[at, here, :] = value[:, at * LANES : (at + 1) * LANES]


def get_rows(ref, here):
    return jnp.concatenate([ref[at, here, :] for at in range(GROUP)], axis=1)


def of_image(at, count):
    return pl.ds(at, PATCHES, stride=count)


def lane_block(rows):
    return pl.BlockSpec((rows, D), lambda i: (0, i))


def row_block(rows, columns=D):
    return pl.BlockSpec((rows, columns), lambda i: (i, 0))


def used(counts, first, size, count):
    row = lax.broadcasted_iota(jnp.int32, (size, 1), 0) + first
    return lax.rem(row, count) < counts[0]


def column_sums(value):
    return jnp.sum(value.reshape(-1, 8, D), axis=0)


def from_hbm(x):
    return pltpu.with_memory_space_constraint(x, pltpu.HBM)


def prepare_kernel(place, from3, from4, mine, theirs, local4, wide3, wide4, squares, w3, w4, sems):
    copies = [
        pltpu.make_async_copy(from3, w3, sems.at[0]),
        pltpu.make_async_copy(from4, w4, sems.at[1]),
    ]
    for copy in copies:
        copy.start()
    for copy in copies:
        copy.wait()
    rows3, rows4 = wide3.shape[1], wide4.shape[0]
    sub = rows4 // UNITS
    first = place[0] == 0
    per3, per4 = DC // LANES, D // LANES
    full = jnp.concatenate([w3[pl.ds(j, rows3, stride=per3), :] for j in range(per3)], axis=1)
    parts = []
    for at in range(2 * UNITS):
        step = 2 * UNITS * sub
        part = jnp.concatenate(
            [full[:, m * step + at * sub : m * step + (at + 1) * sub] for m in range(DC // step)],
            axis=1,
        )
        wide3[at] = part
        parts.append(part.astype(BF))
    for u in range(UNITS):
        mine[u] = jnp.where(first, parts[u], parts[UNITS + u])
        theirs[u] = jnp.where(first, parts[UNITS + u], parts[u])
    four = jnp.concatenate([w4[pl.ds(j, rows4, stride=per4), :] for j in range(per4)], axis=1)
    wide4[...] = four
    for u in range(UNITS):
        local4[u] = four[u * sub : (u + 1) * sub, :].astype(BF)
    squares[...] = jnp.zeros_like(squares)
    for at, value in enumerate((full, four)):
        total = jnp.sum(jnp.sum(value * value, axis=1, keepdims=True), axis=0, keepdims=True)
        squares[at : at + 1, :] = jnp.broadcast_to(total, (1, LANES))


def prepare(place, w3, w4):
    rows3, rows4 = w3.size // DC, w4.size // D
    w3, w4 = w3.reshape(-1, LANES), w4.reshape(-1, LANES)
    return call(
        prepare_kernel,
        "prepare",
        [place, from_hbm(w3), from_hbm(w4)],
        [SMEM, ANY, ANY],
        [
            struct((UNITS, rows3, F), BF),
            struct((UNITS, rows3, F), BF),
            struct((UNITS, rows4 // UNITS, D), BF),
            hbm((2 * UNITS, rows3, F), F32),
            hbm((rows4, D), F32),
            hbm((8, LANES), F32),
        ],
        [pltpu.VMEM(w3.shape, F32), pltpu.VMEM(w4.shape, F32), pltpu.SemaphoreType.DMA((2,))],
        micros=8,
        mib=6,
    )


def keep_kernel(count, counts, cot, dout):
    size = cot.shape[0]
    keep = used(counts, pl.program_id(0) * size, size, count)
    dout[...] = jnp.where(keep, cot[...].astype(F32), 0.0).astype(BF)


def kept_cotangent(counts, cot):
    rows = cot.shape[0]
    size = rows // 2
    return call(
        functools.partial(keep_kernel, rows // PATCHES),
        "kept_cotangent",
        [counts, from_hbm(cot)],
        [SMEM, row_block(size)],
        [held((rows, D), BF)],
        micros=3,
        grid=(2,),
        out_specs=[row_block(size)],
    )[0]


def first_kernel(count, x, gains, y1, scratch):
    rows = x.shape[0]

    def body(here, first, carry):
        normed, _ = normalize(x[here, :].astype(F32))
        put_rows(scratch, here, normed * gains[0:1, :])
        return carry

    tiled(rows, rows // 7, body)
    for at in range(count):
        y1[:, at * D : (at + 1) * D] = get_rows(scratch, of_image(at, count)).astype(BF)


def first_norm(x, gains):
    rows = x.shape[0]
    count = rows // PATCHES
    return call(
        functools.partial(first_kernel, count),
        "first_norm",
        [x, gains],
        [VMEM, VMEM],
        [held((PATCHES, count * D), BF)],
        [split(rows)],
        micros=4,
        mib=10,
    )[0]


def token_kernel(count, x, y1, w1, w2, gains, away, y2, scratch, x1, sems):
    rows = x.shape[0]

    def image(at, carry):
        lanes = pl.ds(pl.multiple_of(at * D, LANES), D)
        pre = dot(w1[...], y1[:, lanes], TN)
        act = pre * (0.5 + 0.5 * jnp.tanh(pre * (GELU_A + GELU_B * (pre * pre))))
        put_rows(scratch, of_image(at, count), dot(w2[...], act.astype(BF), TN))
        return carry

    lax.fori_loop(0, count, image, 0, unroll=4)
    size = rows // 7

    def leave(at):
        here = pl.ds(pl.multiple_of(at * size, 16), size)
        return pltpu.make_async_copy(x1.at[here, :], away.at[here, :], sems.at[at])

    def body(here, first, carry):
        mixed = x[here, :].astype(F32) + get_rows(scratch, here)
        x1[here, :] = mixed
        leave(first // size).start()
        normed, _ = normalize(mixed)
        y2[here, :] = (normed * gains[1:2, :]).astype(BF)
        return carry

    tiled(rows, size, body)
    for at in range(7):
        leave(at).wait()


def token_forward(x, y1, w1, w2, gains):
    rows = x.shape[0]
    count = rows // PATCHES
    return call(
        functools.partial(token_kernel, count),
        "token_forward",
        [x, y1, w1, w2, gains],
        [VMEM] * 5,
        [hbm((rows, D), F32), held((rows, D), BF)],
        [split(rows), pltpu.VMEM((rows, D), F32), pltpu.SemaphoreType.DMA((7,))],
        micros=8,
        mib=16,
        out_specs=[ANY, VMEM],
    )


def load_unit(table, lo, hi, dest, sems):
    copies = []
    for at in range(BLOCKS):
        source = (lo, hi)[at * 2 // BLOCKS].at[at % (BLOCKS // 2)]
        row = pl.multiple_of(table[at] * TILE, 16)
        copies.append(pltpu.make_async_copy(source, dest.at[pl.ds(row, TILE), :], sems.at[at]))
    for copy in copies:
        copy.start()
    return copies


def store_blocks(table, send, keep, total):
    half = BLOCKS // 2
    unit = send.shape[1] - 1
    for at in range(BLOCKS):
        block = total[at * TILE : (at + 1) * TILE, :]
        place = table[BLOCKS + at]

        @pl.when(place < half)
        def _():
            keep[place, unit] = block

        @pl.when(place >= half)
        def _():
            send[place - half, unit] = block


def rows_forward(y2, weight, act, slope):
    def body(here, first, carry):
        value, der = gelu_pair(dot(y2[here, :], weight[...], NN))
        act[here, :] = value.astype(BF)
        slope[here, :] = der.astype(BF)
        return carry

    tiled(y2.shape[0], y2.shape[0] // 7, body, unroll=7)


def forward_kernel(table, lo, hi, y2, act, slope, weight, sems):
    for copy in load_unit(table, lo, hi, weight, sems):
        copy.wait()
    rows_forward(y2, weight, act, slope)


def channel_forward(table, lo, hi, y2):
    acts = held((y2.shape[0], F), BF)
    return call(
        forward_kernel,
        "channel_forward",
        [table, lo, hi, y2],
        [SMEM, ANY, ANY, VMEM],
        [acts, acts, held((D, F), BF)],
        [pltpu.SemaphoreType.DMA((BLOCKS,))],
        micros=7,
        mib=9,
    )


def both(a, b):
    return jnp.concatenate([a[...], b[...]], axis=0)


def join_before(before, send, keep):
    if before:
        send[:, 0] = before[0][:, 0]
        keep[:, 0] = before[1][:, 0]


def forward_grad_kernel(table, weight, y2, act0, dout0, dout1, *refs):
    *before, slope, send, keep, away0, away, act, leaving = refs
    copies = [pltpu.make_async_copy(act0, away0, leaving.at[0])]
    copies[0].start()
    rows_forward(y2, weight, act, slope)
    copies.append(pltpu.make_async_copy(act, away, leaving.at[1]))
    copies[1].start()
    join_before(before, send, keep)
    total = dot(both(act0, act), both(dout0, dout1), TN)
    store_blocks(table, send, keep, total.astype(BF))
    for copy in copies:
        copy.wait()


def channel_forward_grad(table, weight, y2, act0, dout0, dout1, *before):
    acts = held((y2.shape[0], F), BF)
    half = held((BLOCKS // 2, 1 + len(before) // 2, TILE, D), BF)
    return call(
        forward_grad_kernel,
        "channel_forward_grad",
        [table, weight, y2, act0, dout0, dout1, *before],
        [SMEM] + [VMEM] * (5 + len(before)),
        [acts, half, half, hbm(acts.shape, BF), hbm(acts.shape, BF)],
        [pltpu.VMEM(acts.shape, BF), pltpu.SemaphoreType.DMA((2,))],
        out_specs=[VMEM] * 3 + [ANY] * 2,
        micros=11,
        mib=17,
    )


def backward_kernel(table, lo, hi, dout0, dout1, slope0, slope1, dc0, dc1, weight, sems):
    for copy in load_unit(table, lo, hi, weight, sems):
        copy.wait()
    for dout, slope, dc in ((dout0, slope0, dc0), (dout1, slope1, dc1)):

        def body(here, first, carry, dout=dout, slope=slope, dc=dc):
            value = slope[here, :].astype(F32) * dot(dout[here, :], weight[...], NT)
            dc[here, :] = value.astype(BF)
            return carry

        tiled(dout.shape[0], dout.shape[0] // 2, body)


def channel_backward(table, lo, hi, dout0, dout1, slope0, slope1):
    acts = held((dout0.shape[0], F), BF)
    return call(
        backward_kernel,
        "channel_backward",
        [table, lo, hi, dout0, dout1, slope0, slope1],
        [SMEM, ANY, ANY] + [VMEM] * 4,
        [acts, acts, held((F, D), BF)],
        [pltpu.SemaphoreType.DMA((BLOCKS,))],
        micros=8,
        mib=10,
    )


def backward_grad_kernel(table, y0, y1, dc0, dc1, *refs):
    *before, send, keep = refs
    total = dot(both(y0, y1), both(dc0, dc1), TN)
    join_before(before, send, keep)
    store_blocks(table, send, keep, total.astype(BF))


def channel_backward_grad(table, y0, y1, dc0, dc1, *before):
    half = held((BLOCKS // 2, 1 + len(before) // 2, TILE, D), BF)
    return call(
        backward_grad_kernel,
        "channel_backward_grad",
        [table, y0, y1, dc0, dc1, *before],
        [SMEM] + [VMEM] * (4 + len(before)),
        [half, half],
        micros=6,
        mib=13,
    )


def partial_kernel(d0, d1, w0, w1, out):
    def body(here, first, carry):
        total = dot(d0[here, :], w0[...], NT) + dot(d1[here, :], w1[...], NT)
        out[here, :] = total.astype(BF)
        return carry

    tiled(d0.shape[0], d0.shape[0] // 2, body)


def partial_back(dcs, weights):
    out = held((dcs[0].shape[0], D), BF)
    return call(
        partial_kernel, "partial_back", [*dcs, *weights], [VMEM] * 4, [out], mib=10, micros=5
    )[0]


def partial_out_kernel(a0, a1, w0, w1, y1, wt, out, h, slope):
    total = dot(a0[...], w0[...], NN) + dot(a1[...], w1[...], NN)
    out[...] = total.astype(BF)
    step = pl.program_id(0)
    count = y1.shape[1] // D // 2
    for at in range(count):
        lanes = pl.ds(pl.multiple_of((step * count + at) * D, LANES), D)
        act, der = gelu_pair(dot(wt[...], y1[:, lanes], TN))
        h[:, lanes] = act.astype(BF)
        slope[:, lanes] = der.astype(BF)


def partial_out(acts, weights, y1, wt):
    rows = acts[0].shape[0]
    size = rows // 2
    out = held((HIDDEN, y1.shape[1]), BF)
    return call(
        partial_out_kernel,
        "partial_out",
        [*map(from_hbm, acts), *weights, y1, wt],
        [row_block(size, F)] * 2 + [VMEM] * 4,
        [held((rows, D), BF), out, out],
        micros=10,
        mib=13,
        grid=(2,),
        out_specs=[row_block(size), VMEM, VMEM],
    )


def second_kernel(d0, d1, w0, w1, got, dout, x1, gains, dx1, dg2):
    def body(here, first, carry):
        grad = dot(d0[here, :], w0[...], NT) + dot(d1[here, :], w1[...], NT)
        grad += got[here, :].astype(F32)
        normed, inverse = normalize(x1[here, :])
        total = dout[here, :].astype(F32) + norm_back(grad * gains[1:2, :], normed, inverse)
        put_rows(dx1, here, total)
        return carry + column_sums(grad * normed)

    rows = x1.shape[0]
    sums = tiled(rows, rows // 7, body, jnp.zeros((8, D), F32), unroll=7)
    dg2[...] = jnp.sum(sums, axis=0, keepdims=True)


def second_back(dcs, weights, got, dout, x1, gains):
    rows = x1.shape[0]
    return call(
        second_kernel,
        "second_back",
        [*dcs, *weights, got, dout, x1, gains],
        [VMEM] * 8,
        [split(rows), held((1, D), F32)],
        micros=9,
        mib=10,
    )


def mirrored(value, size):
    out = 0
    for bit in range(size.bit_length() - 1):
        out = out * 2 + (value >> bit) % 2
    return out


def token_back_kernel(size, touched, length, place, dx1, h, slope, y1, w2, da, keep, send, g1, g2, every):
    count = dx1.shape[1] // PATCHES
    g1[...] = jnp.zeros_like(g1)
    g2[...] = jnp.zeros_like(g2)

    def body(at, carry):
        lanes = pl.ds(pl.multiple_of(at * D, LANES), D)
        low = get_rows(dx1, of_image(at, count)).astype(BF)
        back = (slope[:, lanes].astype(F32) * dot(w2[...], low, NN)).astype(BF)
        da[:, lanes] = back
        g1[0:PATCHES, :] += dot(y1[:, lanes], back, NT)
        g2[0:HIDDEN, :] += dot(h[:, lanes], low, NT)
        return carry

    lax.fori_loop(0, count, body, 0, unroll=4)
    for at in range(size):
        spot = mirrored(at, size)
        first = at * length // HIDDEN
        every[spot, 0 : touched[0], :] = g1[first : first + touched[0], :]
        first = at * length // PATCHES
        every[spot, touched[0] :, 0:PATCHES] = g2[first : first + touched[1], :]
        every[spot, touched[0] :, PATCHES:] = jnp.zeros((touched[1], HIDDEN - PATCHES), F32)
    half = size // 2
    keep[...] = every[pl.ds(place[0] * half, half)]
    send[...] = every[pl.ds((1 - place[0]) * half, half)]


def token_back(size, touched, length, place, dx1, h, slope, y1, w2):
    count = dx1.shape[1] // PATCHES
    rows = sum(touched)
    return call(
        functools.partial(token_back_kernel, size, touched, length),
        "token_back",
        [place, dx1, h, slope, y1, w2],
        [SMEM] + [VMEM] * 5,
        [
            held((HIDDEN, count * D), BF),
            held((size // 2, rows, HIDDEN), F32),
            held((size // 2, rows, HIDDEN), F32),
        ],
        [
            pltpu.VMEM((PATCHES + touched[0], HIDDEN), F32),
            pltpu.VMEM((HIDDEN + touched[1], PATCHES), F32),
            pltpu.VMEM((size, rows, HIDDEN), F32),
        ],
        micros=10,
        mib=12,
    )


def input_product_kernel(da, w1, out):
    count = da.shape[1] // D

    def body(at, carry):
        lanes = pl.ds(pl.multiple_of(at * D, LANES), D)
        put_rows(out, of_image(at, count), dot(w1[...], da[:, lanes], NN))
        return carry

    lax.fori_loop(0, count, body, 0, unroll=4)


def input_product(da, w1):
    rows = da.shape[1] // D * PATCHES
    return call(
        input_product_kernel, "input_product", [da, w1], [VMEM] * 2, [split(rows)], mib=6, micros=4
    )[0]


def input_kernel(x, dy1, dx1, gains, out, dg1):
    step = pl.program_id(0)
    size = out.shape[0]

    @pl.when(step == 0)
    def _():
        dg1[...] = jnp.zeros_like(dg1)

    here = pl.ds(pl.multiple_of(step * size, 8), size)
    grad = get_rows(dy1, here)
    normed, inverse = normalize(x[...].astype(F32))
    dg1[...] += jnp.sum(column_sums(grad * normed), axis=0, keepdims=True)
    out[...] = get_rows(dx1, here) + norm_back(grad * gains[0:1, :], normed, inverse)


def input_gradient(x, dy1, dx1, gains):
    rows = x.shape[0]
    size = rows // 7
    return call(
        input_kernel,
        "input_gradient",
        [from_hbm(x), dy1, dx1, gains],
        [row_block(size), VMEM, VMEM, VMEM],
        [hbm((rows, D), F32), held((1, D), F32)],
        micros=6,
        mib=12,
        grid=(7,),
        out_specs=[row_block(size), VMEM],
    )


def out_kernel(count, counts, a0, a1, w0, w1, got, x1, out):
    size = out.shape[0]
    first = pl.program_id(0) * size
    here = pl.ds(pl.multiple_of(first, 16), size)
    total = dot(a0[...], w0[...], NN) + dot(a1[...], w1[...], NN)
    total += got[here, :].astype(F32) + x1[here, :]
    out[...] = jnp.where(used(counts, first, size, count), total, 0.0)


def block_output(counts, acts, weights, got, x1):
    rows = x1.shape[0]
    size = rows // 2
    return call(
        functools.partial(out_kernel, rows // PATCHES),
        "block_output",
        [counts, *map(from_hbm, acts), *weights, got, x1],
        [SMEM] + [row_block(size, F)] * 2 + [VMEM] * 4,
        [hbm((rows, D), F32)],
        micros=9,
        mib=22,
        grid=(2,),
        out_specs=[row_block(size)],
    )[0]


def join_two(a, b):
    return join([a, b])


def fold_two(a, b):
    return fold([a, b], 2)


def join_kernel(*refs):
    rows = refs[0].shape[0]
    for at, ref in enumerate(refs[:-1]):
        refs[-1][at * rows : (at + 1) * rows, :] = ref[...]


def join(parts):
    shape = parts[0].shape
    flat = [x.reshape(-1, D) for x in parts]
    out = held((len(parts) * flat[0].shape[0], D), BF)
    x = call(join_kernel, "join", flat, [VMEM] * len(parts), [out], mib=8)[0]
    return x.reshape((len(parts) * shape[0],) + shape[1:])


def fold_kernel(parts, splits, *refs):
    rows = refs[0].shape[0] // splits
    for at in range(splits):
        here = slice(at * rows, (at + 1) * rows)
        total = refs[0][here, :].astype(F32)
        for part in refs[1:parts]:
            total = total + part[here, :].astype(F32)
        refs[parts + at][...] = total.astype(refs[parts + at].dtype)


def fold(parts, splits):
    shape = parts[0].shape
    lead = shape[0] // splits
    flat = [x.reshape(-1, D) for x in parts]
    rows = flat[0].shape[0] // splits
    dtypes = [F32 if lead == 1 else BF] + [BF] * (splits - 1)
    outs = call(
        functools.partial(fold_kernel, len(parts), splits),
        "fold",
        flat,
        [VMEM] * len(parts),
        [held((rows, D), dtype) for dtype in dtypes],
        mib=8,
    )
    return [x.reshape((lead,) + shape[1:]) for x in outs]


def end_kernel(place, *refs):
    *parts, mine, theirs = refs
    rows = mine.shape[1]
    first = place[0] == 0
    for unit in range(UNITS):
        total = parts[0][unit].astype(F32)
        for part in parts[1:]:
            total = total + part[unit].astype(F32)
        mine[unit] = jnp.where(first, total[:rows], total[rows:])
        theirs[unit] = jnp.where(first, total[rows:], total[:rows])


def end_sums(place, parts):
    parts = [x[0] for x in parts]
    out = held((UNITS, parts[0].shape[1] // 2, F), F32)
    return call(
        end_kernel,
        "end_sums",
        [place, *parts],
        [SMEM] + [VMEM] * len(parts),
        [out, out],
        mib=6,
    )


def in_order(place, mine, got):
    first = place[0] == 0
    own = [mine[u] for u in range(UNITS)]
    other = [got[u] for u in range(UNITS)]
    return [jnp.where(first, x, y) for x, y in zip(own + other, other + own)]


def natural(parts, sub):
    return jnp.concatenate(
        [part[:, m * sub : (m + 1) * sub] for m in range(F // sub) for part in parts], axis=1
    )


def put_flat(ref, value):
    per = value.shape[1] // LANES
    for j in range(per):
        ref[pl.ds(j, value.shape[0], stride=per), :] = value[:, j * LANES : (j + 1) * LANES]


STATS = 24
COL3, WEIGHTED3, COL4, WEIGHTED4, ROW3, ROW4, GAINS, SQUARES = 0, 4, 8, 9, 10, 11, 15, 17


def row_statistics(index, grad, squares, old, vec, start):
    rows = grad.shape[0]
    spots = old.shape[0]
    column = lax.broadcasted_iota(jnp.int32, (rows, D), 1)
    target = lax.broadcasted_iota(jnp.int32, (rows, D), 0) + index * rows
    here = [column + spot * D == target for spot in range(spots)]
    before = sum(
        jnp.sum(jnp.where(mask, old[spot : spot + 1, :], 0.0), axis=1, keepdims=True)
        for spot, mask in enumerate(here)
    )
    mean = squares / (grad.shape[1]) + 1e-30
    row = DECAY * before + (1.0 - DECAY) * mean
    for spot, mask in enumerate(here):
        vec[start + spot : start + spot + 1, :] = jnp.sum(
            jnp.where(mask, row, 0.0), axis=0, keepdims=True
        )
    return row


ROW1, ROW2, COL1, WEIGHTED1, COL2, WEIGHTED2 = 18, 19, 20, 21, 22, 23


def covered(columns, length, size):
    return max((at * length + length - 1) // columns - at * length // columns + 1 for at in range(size))


def in_piece(index, length, rows, columns):
    first = index * length // columns
    row = lax.broadcasted_iota(jnp.int32, (rows, columns), 0) + first
    at = row * columns + lax.broadcasted_iota(jnp.int32, (rows, columns), 1)
    return first, (at >= index * length) & (at < (index + 1) * length)


def spots(first, rows):
    column = lax.broadcasted_iota(jnp.int32, (rows, D), 1)
    return column == lax.broadcasted_iota(jnp.int32, (rows, D), 0) + first


def token_statistics(index, length, grad, old, vec, row_at, col_at):
    rows, columns = grad.shape
    first, inside = in_piece(index, length, rows, columns)
    squares = grad * grad
    here = spots(first, rows)
    before = jnp.sum(jnp.where(here, old, 0.0), axis=1, keepdims=True)
    mean = jnp.sum(squares, axis=1, keepdims=True) / columns + 1e-30
    row = DECAY * before + (1.0 - DECAY) * mean
    mine = jnp.where(inside, squares, 0.0)
    vec[col_at : col_at + 1, 0:columns] = jnp.sum(mine, axis=0, keepdims=True)
    weighted = jnp.where(inside, squares / row, 0.0)
    vec[col_at + 1 : col_at + 2, 0:columns] = jnp.sum(weighted, axis=0, keepdims=True)
    starts = jnp.where(inside[:, 0:1] & here, row, 0.0)
    vec[row_at : row_at + 1, :] = jnp.sum(starts, axis=0, keepdims=True)


def stats_kernel(sub, length, place, token_sums, mine, got, g4, old3, old4, dg1, dg2, sums, g1, g2, old1, old2, *refs):
    vec, flat3, flat4, row3, row4 = refs
    parts = in_order(place, mine, got)
    index = place[1]
    rows3 = parts[0].shape[0]
    squared = [x * x for x in parts]
    vec[...] = jnp.zeros_like(vec)
    total = sum(jnp.sum(x, axis=1, keepdims=True) for x in squared)
    wide = jnp.concatenate(squared, axis=1)
    row = row_statistics(index, wide, total, old3, vec, ROW3)
    row3[...] = jnp.broadcast_to(row, (rows3, LANES))
    scale = 1.0 / row
    for at, x in enumerate(squared):
        vec[COL3 + at : COL3 + at + 1, :] = jnp.sum(x, axis=0, keepdims=True)
        vec[WEIGHTED3 + at : WEIGHTED3 + at + 1, :] = jnp.sum(x * scale, axis=0, keepdims=True)
    four = g4[...]
    square4 = four * four
    row = row_statistics(
        index, square4, jnp.sum(square4, axis=1, keepdims=True), old4, vec, ROW4
    )
    row4[...] = jnp.broadcast_to(row, (four.shape[0], LANES))
    vec[COL4 : COL4 + 1, :] = jnp.sum(square4, axis=0, keepdims=True)
    vec[WEIGHTED4 : WEIGHTED4 + 1, :] = jnp.sum(square4 * (1.0 / row), axis=0, keepdims=True)
    vec[GAINS : GAINS + 1, :] = dg1[...]
    vec[GAINS + 1 : GAINS + 2, :] = dg2[...]
    for at in range(2):
        vec[SQUARES : SQUARES + 1, at * LANES : (at + 1) * LANES] = jnp.full(
            (1, LANES), token_sums[at], F32
        )
        lanes = slice((at + 2) * LANES, (at + 3) * LANES)
        vec[SQUARES : SQUARES + 1, lanes] = sums[at : at + 1, :]
    token_statistics(index, length, g1[...], old1[...], vec, ROW1, COL1)
    token_statistics(index, length, g2[...], old2[...], vec, ROW2, COL2)
    put_flat(flat3, natural(parts, sub))
    put_flat(flat4, four)


def statistics(sub, length, *inputs):
    rows3, rows4 = inputs[2].shape[1], inputs[4].shape[0]
    return call(
        functools.partial(stats_kernel, sub, length),
        "statistics",
        list(inputs),
        [SMEM] * 2 + [VMEM] * (len(inputs) - 2),
        [
            struct((STATS, D), F32),
            struct((rows3 * DC // LANES, LANES), F32),
            struct((rows4 * D // LANES, LANES), F32),
            held((rows3, LANES), F32),
            held((rows4, LANES), F32),
        ],
        micros=2,
        mib=8,
    )


def lane_total(x):
    return jnp.sum(jnp.sum(x, axis=1, keepdims=True), axis=0, keepdims=True)


def token_update(index, length, which, grad, old, vec, row_at, col_at, new, col_out, sizes):
    rows, columns = grad.shape
    count = float(PATCHES * HIDDEN)
    every = PATCHES * HIDDEN // columns
    first, _ = in_piece(index, length, rows, columns)
    row = vec[row_at : row_at + 1, :]
    mean = lane_total(row) / every
    col = DECAY * old[...] + (1.0 - DECAY) * (vec[col_at : col_at + 1, 0:columns] / every + 1e-30)
    weighted = vec[col_at + 1 : col_at + 2, 0:columns]
    size = jnp.sqrt(lane_total(weighted / col) * mean / count)
    sizes[which : which + 1, :] = jnp.broadcast_to(size, (1, LANES))
    square = vec[SQUARES : SQUARES + 1, which * LANES : which * LANES + 1]
    scale = STEP * jnp.sqrt(square / count + 1e-06) / jnp.maximum(1.0, size / CLIP)
    here = spots(first, rows)
    left = jnp.sum(jnp.where(here, row, 0.0), axis=1, keepdims=True)
    known = lax.broadcasted_iota(jnp.int32, (rows, 1), 0) + first < every
    left = jnp.where(known, lax.rsqrt(jnp.where(known, left, 1.0) / mean), 0.0)
    new[...] = grad[...] * left * lax.rsqrt(col) * scale
    col_out[...] = col


def update_kernel(sub, length, place, vec, mine, got, g4, wide3, wide4, row3, row4, old3, old4, *refs):
    g1, g2, old1, old2, gains, gain_states = refs[:6]
    new3, new4, col3, col4, sizes, new1, new2, col1, col2, gain_stats, new_gains = refs[6:]
    parts = in_order(place, mine, got)
    count = float(D * DC)
    sizes[...] = jnp.zeros_like(sizes)
    gain = vec[GAINS : GAINS + 2, :]
    state = DECAY * gain_states[...] + (1.0 - DECAY) * (gain * gain + 1e-30)
    step = gain * lax.rsqrt(state)
    size = jnp.sqrt(jnp.sum(step * step, axis=1, keepdims=True) / D)
    scale = jnp.sqrt(jnp.sum(gains[...] * gains[...], axis=1, keepdims=True) / D + 1e-06)
    gain_stats[...] = state
    new_gains[...] = gains[...] - STEP * scale * step / jnp.maximum(1.0, size / CLIP)
    sizes[4:6, :] = jnp.broadcast_to(size, (2, LANES))
    token_update(place[1], length, 0, g1, old1, vec, ROW1, COL1, new1, col1, sizes)
    token_update(place[1], length, 1, g2, old2, vec, ROW2, COL2, new2, col2, sizes)
    for which in range(2):
        rows = vec[ROW3 : ROW3 + 1, :] if which == 0 else vec[ROW4 : ROW4 + 4, :]
        mean = lane_total(rows) / (D if which == 0 else DC)
        if which == 0:
            cols = DECAY * old3[...] + (1.0 - DECAY) * (vec[COL3 : COL3 + 4, :] / D + 1e-30)
            weighted = vec[WEIGHTED3 : WEIGHTED3 + 4, :]
        else:
            cols = DECAY * old4[...] + (1.0 - DECAY) * (vec[COL4 : COL4 + 1, :] / DC + 1e-30)
            weighted = vec[WEIGHTED4 : WEIGHTED4 + 1, :]
        size = jnp.sqrt(lane_total(weighted / cols) * mean / count)
        sizes[which + 2 : which + 3, :] = jnp.broadcast_to(size, (1, LANES))
        square = vec[SQUARES : SQUARES + 1, (which + 2) * LANES : (which + 2) * LANES + 1]
        scale = STEP * jnp.sqrt(square / count + 1e-06) / jnp.maximum(1.0, size / CLIP)
        if which == 0:
            left = lax.rsqrt(row3[:, 0:1] / mean) * scale
            right = lax.rsqrt(cols)
            new = [
                wide3[at] - parts[at] * left * right[at : at + 1, :] for at in range(2 * UNITS)
            ]
            put_flat(new3, natural(new, sub))
            col3[...] = natural([cols[at : at + 1, :] for at in range(2 * UNITS)], sub)
        else:
            left = lax.rsqrt(row4[:, 0:1] / mean) * scale
            put_flat(new4, wide4[...] - g4[...] * left * lax.rsqrt(cols))
            col4[...] = cols


def update(sub, length, *inputs):
    wide3, wide4 = inputs[5:7]
    g1, g2 = inputs[-6:-4]
    return call(
        functools.partial(update_kernel, sub, length),
        "update",
        list(inputs),
        [SMEM] + [VMEM] * (len(inputs) - 1),
        [
            struct((wide3.size // LANES, LANES), F32),
            struct((wide4.size // LANES, LANES), F32),
            struct((1, DC), F32),
            struct((1, D), F32),
            struct((8, LANES), F32),
            struct(g1.shape, F32),
            struct(g2.shape, F32),
            struct((1, HIDDEN), F32),
            struct((1, PATCHES), F32),
            struct((2, D), F32),
            struct((2, D), F32),
        ],
        micros=2,
        mib=8,
    )


class Links:
    def __init__(self, size, token):
        self.size = size
        self.chips = size // 2
        bits = self.chips.bit_length() - 1
        self.high = [1 << b for b in reversed(range(2, bits))]
        self.orders = (self.high + [1, 2], self.high + [2, 1])
        self.index = lax.axis_index("fsdp")
        self.core = self.index & 1
        self.chip = self.index >> 1
        self.token = token

    def tie(self, x):
        x, self.token = lax.optimization_barrier((x, self.token))
        return x

    land = tie

    def run(self, function, *inputs, landing=None):
        out = function(*self.tie(inputs))
        if landing is None:
            return self.tie(out)
        return self.tie((out, landing))

    def swap(self, x, mask):
        return lax.ppermute(self.tie(x), "fsdp", [(i, i ^ mask) for i in range(self.size)])

    def cross(self, x, last):
        masks = (2, 1) if last else (1, 2)
        pairs = [(i, i ^ (masks[i & 1] << 1)) for i in range(self.size)]
        return lax.ppermute(self.tie(x), "fsdp", pairs)

    def line(self, x, level):
        return self.swap(x, self.high[level] << 1)

    def line_gather(self, x):
        for mask in self.high[:-2]:
            x = self.run(join_two, x, self.land(self.swap(x, mask << 1)))
        return x

    def line_scatter(self, keep, send):
        for mask in reversed(self.high[1:-1]):
            keep, send = self.run(fold_two, keep, self.land(self.swap(send, mask << 1)))
        return keep, self.swap(send, self.high[0] << 1)

    def owners(self, core):
        place = jnp.arange(self.chips, dtype=jnp.int32)
        owner = jnp.full((self.chips,), self.chip, jnp.int32)
        for level in range(len(self.orders[0])):
            bit = (place >> level) & 1
            mask = jnp.where(core == 0, self.orders[0][level], self.orders[1][level])
            owner = owner ^ (bit * mask)
        return owner

    def places(self, core):
        relative = jnp.arange(self.chips, dtype=jnp.int32) ^ self.chip
        place = jnp.zeros_like(relative)
        for level in range(len(self.orders[0])):
            mask = jnp.where(core == 0, self.orders[0][level], self.orders[1][level])
            place = place | (((relative & mask) != 0).astype(jnp.int32) << level)
        return place

    def table(self, core):
        if self.chips == BLOCKS:
            return jnp.concatenate([self.owners(core), self.places(core)])
        order = jnp.arange(BLOCKS, dtype=jnp.int32)
        return jnp.concatenate([order, order])

    def scatter_end(self, own, received):
        return self.run(lambda *p: fold(p, 1), own, received)[0][0]

    def as_blocks(self, halves, core):
        if self.chips == BLOCKS:
            return halves
        x = jnp.take(jnp.concatenate(halves, axis=0), self.places(core), axis=0)
        x = x.reshape(BLOCKS, TILE, D)
        return x[: BLOCKS // 2], x[BLOCKS // 2 :]

    def ordered(self, halves, core):
        if self.chips == BLOCKS:
            return halves
        send, keep = halves
        x = jnp.concatenate([keep, send], axis=0).transpose(1, 0, 2, 3)
        x = x.reshape(x.shape[0], self.chips, -1, D).transpose(1, 0, 2, 3)
        x = jnp.take(x, self.owners(core), axis=0)
        return x[self.chips // 2 :], x[: self.chips // 2]

    def flat_join(self, x, got, mask, axis=1):
        upper = (self.index & mask) != 0
        return jnp.where(
            upper, jnp.concatenate([got, x], axis=axis), jnp.concatenate([x, got], axis=axis)
        )

    def halves(self, x, mask, dtype):
        half = x.shape[0] // 2
        upper = (self.index & mask) != 0
        keep = jnp.where(upper, x[half:], x[:half])
        send = jnp.where(upper, x[:half], x[half:])
        return keep, send.astype(dtype)


def shards(
    images,
    cotangent,
    counts,
    w_token_in,
    w_token_out,
    w_chan_in,
    w_chan_out,
    gains,
    row_states,
    col_states,
    gain_states,
):
    links = Links(D * DC // w_chan_in.shape[0], counts)
    size, chips, core = links.size, links.chips, links.core
    run, land, swap, cross = links.run, links.land, links.swap, links.cross
    count = images.shape[0]
    rows = count * PATCHES
    table = links.table(core)
    steps = [1 << at for at in range(size.bit_length() - 1)]
    x = images.transpose(1, 0, 2).reshape(rows, D)
    cot = cotangent.transpose(1, 0, 2).reshape(rows, D)

    rows3 = D // size
    rows4 = DC // size
    sub = rows4 // UNITS
    length = w_token_in.shape[0]
    place = jnp.stack([core, links.index])
    edges_r = (0, PATCHES, PATCHES + HIDDEN, PATCHES + HIDDEN + D, PATCHES + HIDDEN + D + DC)
    edges_c = (0, HIDDEN, HIDDEN + PATCHES, HIDDEN + PATCHES + DC, HIDDEN + PATCHES + DC + D)

    def old_row_statistics(rows):
        rows = [rows[edges_r[k] : edges_r[k + 1]] for k in range(4)]
        rows[2:] = rows[2].reshape(1, D), rows[3].reshape(4, D)
        rows[:2] = (jnp.pad(row, (0, D - row.shape[0]))[None] for row in rows[:2])
        return rows

    def old_column_statistics(cols):
        cols = [cols[edges_c[k] : edges_c[k + 1]] for k in range(4)]
        wide = cols[2].reshape(chips, 2, UNITS, sub).transpose(1, 2, 0, 3).reshape(2 * UNITS, F)
        cols[2:] = wide, cols[3].reshape(1, D)
        cols[:2] = (col[None] for col in cols[:2])
        return cols

    def blocks(lo, hi):
        return links.as_blocks((lo, hi), core)

    token = jnp.concatenate([w_token_in, w_token_out]).astype(BF)[None]
    high = steps[3:]
    token_got = swap(token, high[0])
    (mine, theirs, local4, wide3, wide4, weight_squares), token_got = run(
        prepare, place, w_chan_in, w_chan_out, landing=token_got
    )
    token = links.flat_join(token, token_got, high[0], 0)
    got = swap(theirs, 1)
    for mask in high[1:-1]:
        token = links.flat_join(token, land(swap(token, mask)), mask, 0)
    token_got = swap(token, high[-1])
    dout, (token_got, got) = run(kept_cotangent, counts, cot, landing=(token_got, got))
    token = links.flat_join(token, token_got, high[-1], 0)
    token_got = swap(token, 1)
    local3 = run(
        lambda m, g: jnp.where(
            core == 0, jnp.concatenate([m, g], axis=1), jnp.concatenate([g, m], axis=1)
        )[:, None],
        mine,
        got,
    )
    token = links.flat_join(token, land(token_got), 1, 1)
    a0 = links.line_gather(local3[0])
    a0_got = links.line(a0, -2)
    token_got = swap(token, 2)
    (y1, old_rows), (token_got, a0_got) = run(
        lambda x, g, r: (first_norm(x, g), old_row_statistics(r)),
        x,
        gains,
        row_states,
        landing=(token_got, a0_got),
    )
    token = links.flat_join(token, token_got, 2, 1)
    a0 = run(join_two, a0, a0_got)
    a0_got = links.line(a0, -1)
    token_got = swap(token, 4)
    other_dout = swap(dout, 1)
    (old_cols, token_sums), (token_got, a0_got) = run(
        lambda c, *w: (old_column_statistics(c), jnp.stack([jnp.sum(x * x) for x in w])),
        col_states,
        w_token_in,
        w_token_out,
        landing=(token_got, a0_got),
    )
    a0 = run(join_two, a0, a0_got)
    a0_got = cross(a0, False)
    a1 = links.line_gather(local3[1])
    a1_got = links.line(a1, -2)

    def matrices(x, got):
        x = links.flat_join(x, got, 4, 1).reshape(size, 2, length)
        return x[:, 0].reshape(PATCHES, HIDDEN), x[:, 1].reshape(HIDDEN, PATCHES)

    (w1, w2), (a0_got, a1_got) = run(matrices, token, token_got, landing=(a0_got, a1_got))
    a0 = run(join_two, a0, a0_got)
    a0_hi = cross(a0, True)
    a1 = run(join_two, a1, a1_got)
    a1_got = links.line(a1, -1)
    (x1, y2), (a0_hi, a1_got) = run(
        token_forward, x, y1, w1, w2, gains, landing=(a0_hi, a1_got)
    )

    other_y2 = swap(y2, 1)
    a1 = run(join_two, a1, a1_got)
    a1_got = cross(a1, False)
    b0 = links.line_gather(local4[0][None])
    b0_got = links.line(b0, -2)
    (held_a0, slope_a0, w3_0), (other_y2, other_dout, a1_got, b0_got) = run(
        channel_forward,
        table,
        *blocks(a0, a0_hi),
        y2,
        landing=(other_y2, other_dout, a1_got, b0_got),
    )
    a1 = run(join_two, a1, a1_got)
    a1_hi = cross(a1, True)
    b0 = run(join_two, b0, b0_got)
    b0_got = links.line(b0, -1)
    b1 = links.line_gather(local4[1][None])
    b1_got = links.line(b1, -2)
    (slope_b0, *c0, act_a0, act_b0), (a1_hi, b0_got, b1_got) = run(
        channel_forward_grad,
        table,
        w3_0,
        other_y2,
        held_a0,
        dout,
        other_dout,
        landing=(a1_hi, b0_got, b1_got),
    )
    b0 = run(join_two, b0, b0_got)
    b0_got = cross(b0, False)
    b1 = run(join_two, b1, b1_got)
    b1_got = links.line(b1, -1)
    (held_a1, slope_a1, w3_1), (b0_got, b1_got) = run(
        channel_forward, table, *blocks(a1, a1_hi), y2, landing=(b0_got, b1_got)
    )
    b0 = run(join_two, b0, b0_got)
    b0_hi = cross(b0, True)
    (slope_b1, *c, act_a1, act_b1), b0_hi = run(
        channel_forward_grad,
        table,
        w3_1,
        other_y2,
        held_a1,
        dout,
        other_dout,
        *c0,
        landing=b0_hi,
    )

    b1 = run(join_two, b1, b1_got)
    b1_got = cross(b1, False)
    (dc_a0, dc_b0, w4_0), b1_got = run(
        channel_backward,
        table,
        *blocks(b0, b0_hi),
        dout,
        other_dout,
        slope_a0,
        slope_b0,
        landing=b1_got,
    )
    b1 = run(join_two, b1, b1_got)
    b1_hi = cross(b1, True)
    d0, b1_hi = run(channel_backward_grad, table, y2, other_y2, dc_a0, dc_b0, landing=b1_hi)
    c_send, c_keep = links.ordered(c, core)
    c_got = cross(c_send, True)
    (dc_a1, dc_b1, w4_1), c_got = run(
        channel_backward,
        table,
        *blocks(b1, b1_hi),
        dout,
        other_dout,
        slope_a1,
        slope_b1,
        landing=c_got,
    )
    d0_send, d0_keep = links.ordered(d0, core)
    d0_got = cross(d0_send, True)
    d1, d0_got = run(channel_backward_grad, table, y2, other_y2, dc_a1, dc_b1, landing=d0_got)
    d1_send, d1_keep = links.ordered(d1, core)
    d1_got = cross(d1_send, True)
    c_keep, c_send = run(fold_two, c_keep, c_got)
    c_got = cross(c_send, False)
    d0_keep, d0_send = run(fold_two, d0_keep, d0_got)
    dy2_other = run(partial_back, (dc_b0, dc_b1), (w3_0, w3_1))
    dy2_got = swap(dy2_other, 1)
    (out_other, h, slope), (dy2_got, d1_got, c_got) = run(
        partial_out,
        (act_b0, act_b1),
        (w4_0, w4_1),
        y1,
        w1,
        landing=(dy2_got, d1_got, c_got),
    )
    d1_keep, d1_send = run(fold_two, d1_keep, d1_got)
    d_keep, d_send = (jnp.concatenate(x, axis=1) for x in ((d0_keep, d1_keep), (d0_send, d1_send)))
    d_got = cross(d_send, False)
    c_keep, c_send = run(fold_two, c_keep, c_got)
    c_got = links.line(c_send, -1)
    out_got = swap(out_other, 1)

    (dx1, dg2), (d_got, c_got, out_got) = run(
        second_back,
        (dc_a0, dc_a1),
        (w3_0, w3_1),
        dy2_got,
        dout,
        x1,
        gains,
        landing=(d_got, c_got, out_got),
    )
    d_keep, d_send = run(fold_two, d_keep, d_got)
    d_got = links.line(d_send, -1)
    c_keep, c_send = run(fold_two, c_keep, c_got)
    c_keep, c_got = links.line_scatter(c_keep, c_send)
    block_out = run(
        block_output, counts, (act_a0, act_a1), (w4_0, w4_1), out_got, x1
    ).reshape(PATCHES, count, D).transpose(1, 0, 2)
    shapes = ((PATCHES, HIDDEN), (HIDDEN, PATCHES))
    touched = [covered(columns, length, size) for _, columns in shapes]
    (da, keep, send), (d_got, c_got) = run(
        functools.partial(token_back, size, touched, length),
        place,
        dx1,
        h,
        slope,
        y1,
        w2,
        landing=(d_got, c_got),
    )
    d_keep, d_send = run(fold_two, d_keep, d_got)
    got = swap(send, steps[0])
    dy1, got = run(input_product, da, w1, landing=got)
    token_grads = keep + got
    keep, send = links.halves(token_grads, steps[1], BF)
    got = swap(send, steps[1])
    d_keep, d_got = links.line_scatter(d_keep, d_send)
    (grad_input, dg1), (got, d_got) = run(
        input_gradient, x, dy1, dx1, gains, landing=(got, d_got)
    )
    token_grads = keep + got.astype(F32)
    mine, theirs = run(lambda p, *parts: end_sums(p, parts), place, d_keep, d_got)
    theirs_got = swap(theirs, 1)
    grad4 = links.scatter_end(c_keep, c_got).reshape(rows4, D)
    for mask in steps[2:]:
        keep, send = links.halves(token_grads, mask, BF if mask == 4 else F32)
        got = swap(send, mask)
        if mask == steps[2]:
            got, theirs_got = land((got, theirs_got))
        else:
            got = land(got)
        token_grads = keep + got.astype(F32)
    token_grads = (token_grads[0, : touched[0]], token_grads[0, touched[0] :, :PATCHES])
    got = theirs_got
    grad_input = grad_input.reshape(PATCHES, count, D).transpose(1, 0, 2)

    summed, flat3, flat4, row3, row4 = run(
        functools.partial(statistics, sub, length),
        place,
        token_sums,
        mine,
        got,
        grad4,
        old_rows[2],
        old_rows[3],
        dg1,
        dg2,
        weight_squares,
        *token_grads,
        *old_rows[:2],
    )

    def own_piece(x):
        columns = x.shape[1]
        start = links.index * length - links.index * length // columns * columns
        return lax.dynamic_slice_in_dim(x.reshape(-1), start, length)

    flat12 = None
    for mask in steps:
        got_sums = swap(summed, mask)
        if flat12 is None:
            flat12, got_sums = run(
                lambda *g: [own_piece(x) for x in g], *token_grads, landing=got_sums
            )
        else:
            got_sums = land(got_sums)
        summed = summed + got_sums
    new3, new4, col3, col4, sizes, new1, new2, col1, col2, gain_stats, new_gains = update(
        sub,
        length,
        place,
        summed,
        mine,
        got,
        grad4,
        wide3,
        wide4,
        row3,
        row4,
        old_cols[2],
        old_cols[3],
        *token_grads,
        *old_cols[:2],
        gains,
        gain_states,
    )
    rows_out = [summed[ROW1, :PATCHES], summed[ROW2, :HIDDEN], summed[ROW3]]
    rows_out.append(summed[ROW4 : ROW4 + 4].reshape(-1))
    cols_out = [x.reshape(-1) for x in (col1, col2, col3, col4)]
    new_weights = [
        w_token_in - own_piece(new1),
        w_token_out - own_piece(new2),
        new3.reshape(-1),
        new4.reshape(-1),
    ]
    token_grads = flat12

    gain_grads = summed[GAINS : GAINS + 2]
    update_rms = sizes[:6, 0]
    return (
        block_out,
        grad_input,
        token_grads[0],
        token_grads[1],
        flat3.reshape(-1),
        flat4.reshape(-1),
        new_weights[0],
        new_weights[1],
        new_weights[2],
        new_weights[3],
        gain_grads,
        gain_stats,
        new_gains,
        jnp.concatenate(rows_out),
        jnp.concatenate(cols_out),
        update_rms,
    )


def solution(mesh):
    split = P("fsdp")
    images = P("fsdp", None, None)
    in_specs = (images, images) + (split,) * 5 + (P(),) * 4
    out_specs = (images, images) + (split,) * 8 + (P(),) * 6
    return jax.shard_map(
        shards, mesh=mesh, in_specs=in_specs, out_specs=out_specs, check_vma=False
    )
```
